128 devices in a mesh: dp: 16 (over x, z_lo, core), pipe: 8 (over y, z_hi).
Axes of the slice: x: 4, y: 4, z: 4 (z_hi: 2, z_lo: 2; z = z_hi * 2 + z_lo), core: 2. Of those that a mesh axis runs over, the one named last changes fastest.
Arguments:
- shallow: bfloat16 [4096, 8192], P('dp'), may hold values from -8 to 8
- teacher: bfloat16 [4096, 8192], P(('dp', 'pipe')), may hold values from -8 to 8
- positions: int32 [4096], P('dp'), may hold values from 0 to 4095
- segments: int32 [4096], P('dp'), may hold values from 0 to 255, never falling along the last dimension, each value on 1 to 64 neighbouring positions
- in_gain: float32 [8192], replicated, may hold values from 0.2 to 4.5
- w_query: bfloat16 [8192, 4096], P('dp', 'pipe'), may hold values from -0.0625 to 0.0625
- w_keyval: bfloat16 [8192, 1024], P('dp', 'pipe'), may hold values from -0.0625 to 0.0625
- w_output: bfloat16 [4096, 8192], P('pipe', 'dp'), may hold values from -0.09375 to 0.09375
Outputs:
- loss: float32 [], replicated
- step_query: float32 [8192, 4096], P('dp', 'pipe')
- step_keyval: float32 [8192, 1024], P('dp', 'pipe')
- step_output: float32 [4096, 8192], P('pipe', 'dp')
The draws below stay inside these ranges and needn't reach their ends.
Inputs may be any that keep to these rules, and one draw needn't show every extreme that they name: `segments`: ids never fall along the rows; every segment covers 1 to 64 rows.
All inputs are finite; a program needn't handle non-finite values.
Results may differ from the reference program's by a relative error of at most 0.023.
Values may be sent and summed in bfloat16 or wider, within the bound.
A program may use at most 128 MiB of HBM per device.

```python
import math
import jax
import jax.numpy as jnp
import numpy as np
from jax import lax

D = 8192
HD = 128
QH = 32
KV = 4
R = 256
ROWS = 4096
N_DP = 16
N_PIPE = 8


def shared_rows(key):
    base = jax.random.fold_in(key, 7301)
    raw = jnp.clip(jax.random.normal(base, (ROWS, D), jnp.float32), -6.0, 6.0)
    return raw


def draw_shallow(key, part):
    return jnp.clip(shared_rows(key), -8.0, 8.0).astype(jnp.bfloat16)


def draw_teacher(key, part):
    source = jnp.clip(shared_rows(key), -8.0, 8.0)
    groups = ROWS // R
    block_rows = R // N_PIPE
    rolled = jnp.roll(source.reshape(groups, N_PIPE, block_rows, D), -1, axis=1).reshape(ROWS, D)
    order = jnp.arange(ROWS).astype(jnp.float32).reshape(groups, N_PIPE, block_rows)
    target_index = jnp.roll(order, -1, axis=1).reshape(ROWS, 1)
    fraction = target_index / ROWS
    noise_key = jax.random.fold_in(key, 7302)
    weight = 0.9 * (1.0 - fraction)
    noise = jnp.clip(jax.random.normal(noise_key, (ROWS, D), jnp.float32), -6.0, 6.0)
    mixed = weight * rolled + jnp.sqrt(1.0 - weight * weight) * noise
    return jnp.clip(mixed, -8.0, 8.0).astype(jnp.bfloat16)


def draw_in_gain(key, part):
    steps = jnp.arange(D).astype(jnp.float32) / (D - 1)
    trend = jnp.exp(jnp.log(0.5) + steps * (jnp.log(2.0) - jnp.log(0.5)))
    rough = jax.random.uniform(jax.random.fold_in(key, 7311), (D,), jnp.float32, 0.8, 1.25)
    return jnp.clip(trend * rough, 0.2, 4.5)


def touch_ends(values, own_key, smallest, largest):
    place = [jax.random.randint(jax.random.fold_in(own_key, axis), (), 0, length) for axis, length in enumerate(values.shape)]
    widest = values.shape.index(max(values.shape))
    next_to = place[:widest] + [(place[widest] + 1) % values.shape[widest]] + place[widest + 1:]
    return values.at[tuple(place)].set(smallest).at[tuple(next_to)].set(largest)


def levels(own_key, dims, split, least, top_value):
    def one(axis_at, blocks):
        heights = jax.random.uniform(jax.random.fold_in(jax.random.fold_in(own_key, 6), axis_at), (blocks,), jnp.float32, least / len(split), top_value / len(split))
        return jnp.repeat(jnp.exp(heights), dims[axis_at] // blocks).reshape((-1,) + (1,) * (len(dims) - axis_at - 1))

    loudness = one(*split[0])
    for cut in split[1:]:
        loudness = loudness * one(*cut)
    return loudness


def length_profile(number_of, total, reach, lean):
    loads = [(1 << 20) // math.isqrt(rank ** lean) + 1 for rank in range(2, number_of + 1)]
    rest, holding = total - reach - (number_of - 1), [1] * (number_of - 1)
    while rest > 0:
        candidates = [i for i in range(number_of - 1) if holding[i] < reach]
        mass, budget = sum([loads[i] for i in candidates]), rest
        for i in candidates:
            addition = min(reach - holding[i], max(1, budget * loads[i] // mass), rest)
            holding[i] = holding[i] + addition
            rest = rest - addition
    return np.array([reach] + holding)


def uneven(key, number_of, total, reach, lean):
    if number_of == 2:
        one = jax.random.randint(key, (), max(1, total - reach), min(reach, total - 1) + 1)
        return jnp.stack([one, total - one])
    sizes = jnp.asarray(length_profile(number_of, total, reach, lean), jnp.int32)
    twos = (number_of - 1) // 2
    giver, sink = sizes[1:1 + 2 * twos:2], sizes[2:2 + 2 * twos:2]
    slack = jnp.minimum(giver - 1, reach - sink)
    moved = jax.random.randint(jax.random.fold_in(key, 1), (twos,), 0, 1 << 20) % (slack + 1)
    sizes = sizes.at[1:1 + 2 * twos:2].set(giver - moved).at[2:2 + 2 * twos:2].set(sink + moved)
    return sizes[jax.random.permutation(jax.random.fold_in(key, 2), number_of)]


def bell_draw(rng, extent, deviation, limit, split=(), dtype=jnp.bfloat16):
    array = jax.random.normal(rng, extent, jnp.float32) * deviation
    if len(split) > 0:
        array = levels(rng, extent, split, -0.22, 0.18) * array
    return jnp.clip(array, min=-limit, max=limit).astype(dtype)


def setup_inputs(seed: int = 0) -> dict:
    seeds = jax.random.split(jax.random.key(seed), 9)
    return {
        "shallow": draw_shallow(jax.random.fold_in(seeds[8], 71), 0),
        "teacher": draw_teacher(jax.random.fold_in(seeds[8], 71), 0),
        "positions": touch_ends(jax.random.randint(seeds[2], (ROWS,), 0, 4096), jax.random.fold_in(seeds[2], 1), 0, 4095).astype(jnp.int32),
        "segments": jnp.searchsorted(jnp.cumsum(uneven(seeds[3], ROWS // 16, ROWS, 64, 0)), jnp.arange(ROWS), side="right").astype(jnp.int32),
        "in_gain": draw_in_gain(jax.random.fold_in(seeds[8], 71), 0),
        "w_query": bell_draw(seeds[5], (D, QH * HD), D ** -0.5, 0.0625, ((0, 16), (1, 8))),
        "w_keyval": bell_draw(seeds[6], (D, 2 * KV * HD), D ** -0.5, 0.0625, ((0, 16), (1, 8))),
        "w_output": bell_draw(seeds[7], (QH * HD, D), (QH * HD) ** -0.5, 0.09375, ((0, 8), (1, 16))),
    }


theta_base = 10000.0
norm_eps = 1e-05
cosine_eps = 1e-06
mean_eps = 1e-12
mask_fill = -1e+30

def normalize_rows(rows_in, in_gain):
    widened = rows_in.astype(jnp.float32)
    spread = lax.optimization_barrier(jnp.mean(widened * widened, axis=-1, keepdims=True))
    return (widened * lax.rsqrt(spread + norm_eps) * in_gain[None, :]).astype(jnp.bfloat16)

def rotary_tables(positions, head_width):
    half_width = head_width // 2
    exponent = jnp.arange(half_width).astype(jnp.float32) * (2.0 / head_width)
    inverse = jnp.power(jnp.float32(theta_base), -exponent)
    angle_table = positions.astype(jnp.float32)[:, None] * inverse[None, :]
    return (jnp.cos(angle_table), jnp.sin(angle_table))

def rotate(values, cosine, sine_table):
    half_width = values.shape[-1] // 2
    leading = values[..., :half_width]
    trailing = values[..., half_width:]
    cosine_row = cosine[:, None, :]
    sine_row = sine_table[:, None, :]
    return jnp.concatenate([leading * cosine_row - trailing * sine_row, trailing * cosine_row + leading * sine_row], axis=-1)

def unrotate(values, cosine, sine_table):
    half_width = values.shape[-1] // 2
    leading = values[..., :half_width]
    trailing = values[..., half_width:]
    cosine_row = cosine[:, None, :]
    sine_row = sine_table[:, None, :]
    return jnp.concatenate([leading * cosine_row + trailing * sine_row, trailing * cosine_row - leading * sine_row], axis=-1)

def attend(queries, keys_head, values_head, allowed):
    score_scale = 1.0 / math.sqrt(queries.shape[-1])
    scores = jnp.einsum('rhd,khd->hrk', queries.astype(jnp.float32), keys_head.astype(jnp.float32)) * score_scale
    scores = jnp.where(allowed[None], scores, mask_fill)
    highest = lax.optimization_barrier(jnp.max(scores, axis=-1, keepdims=True))
    weights = jnp.exp(scores - highest)
    softmax_rows = weights / lax.optimization_barrier(jnp.sum(weights, axis=-1, keepdims=True))
    softmax_low = softmax_rows.astype(jnp.bfloat16)
    attended = jnp.einsum('hrk,khd->rhd', softmax_low.astype(jnp.float32), values_head.astype(jnp.float32)).astype(jnp.bfloat16)
    return (softmax_rows, softmax_low, attended)

def attend_grad(softmax_rows, softmax_low, queries, keys_head, values_head, att_grad):
    score_scale = 1.0 / math.sqrt(queries.shape[-1])
    inner_prod = jnp.einsum('rhd,khd->hrk', att_grad.astype(jnp.float32), values_head.astype(jnp.float32))
    centred = inner_prod - lax.optimization_barrier(jnp.sum(softmax_rows * inner_prod, axis=-1, keepdims=True))
    score_grad = (softmax_rows * centred * score_scale).astype(jnp.bfloat16)
    query_part = jnp.einsum('hrk,khd->rhd', score_grad.astype(jnp.float32), keys_head.astype(jnp.float32))
    key_part = jnp.einsum('hrk,rhd->khd', score_grad.astype(jnp.float32), queries.astype(jnp.float32))
    value_part = jnp.einsum('hrk,rhd->khd', softmax_low.astype(jnp.float32), att_grad.astype(jnp.float32))
    return (query_part, key_part, value_part)

def held_low(values):
    return lax.optimization_barrier(values.astype(jnp.bfloat16)).astype(jnp.float32)

def contract_rows(left, right):
    return lax.dot_general(left, right, (((0,), (0,)), ((), ())), preferred_element_type=jnp.float32)

def reference(shallow, teacher, positions, segments, in_gain, w_query, w_keyval, w_output):
    block_rows = R // N_PIPE
    head_group = QH // KV
    group_cols = QH * HD // N_PIPE
    shallow_groups = shallow.reshape(N_DP, R, D)
    teacher_groups = jnp.roll(teacher.reshape(N_DP, N_PIPE, block_rows, D), 1, axis=1).reshape(N_DP, R, D)
    position_groups = positions.reshape(N_DP, R)
    segment_groups = segments.reshape(N_DP, R)
    row_order = jnp.arange(R)

    def one_group(running, inputs):
        grad_query, grad_keyval, grad_output, loss_sum = running
        shallow_rows, target_rows, position_rows, segment_rows = inputs
        normed = normalize_rows(shallow_rows, in_gain)
        cosine, sine_table = rotary_tables(position_rows, HD)
        query_proj = jnp.dot(normed, w_query, preferred_element_type=jnp.float32).reshape(R, QH, HD)
        queries = rotate(query_proj, cosine, sine_table).astype(jnp.bfloat16)
        keyval_proj = jnp.dot(normed, w_keyval, preferred_element_type=jnp.float32).reshape(R, KV, 2, HD)
        keys = rotate(keyval_proj[:, :, 0], cosine, sine_table).astype(jnp.bfloat16)
        values = keyval_proj[:, :, 1].astype(jnp.bfloat16)
        keys_head = jnp.tile(keys, (1, head_group, 1))
        values_head = jnp.tile(values, (1, head_group, 1))
        allowed = (segment_rows[:, None] == segment_rows[None, :]) & (row_order[None, :] <= row_order[:, None])
        softmax_rows, softmax_low, attended = attend(queries, keys_head, values_head, allowed)
        att_flat = attended.reshape(R, QH * HD)
        head_sum = jnp.zeros((R, D), jnp.float32)
        for block_index in range(N_PIPE):
            low_col = block_index * group_cols
            head_sum = head_sum + held_low(jnp.dot(att_flat[:, low_col:low_col + group_cols], w_output[low_col:low_col + group_cols], preferred_element_type=jnp.float32))
        output = shallow_rows.astype(jnp.float32) + head_sum
        target = target_rows.astype(jnp.float32)
        norm_out = jnp.sqrt(lax.optimization_barrier(jnp.sum(output * output, axis=-1, keepdims=True)) + cosine_eps)
        norm_tar = jnp.sqrt(lax.optimization_barrier(jnp.sum(target * target, axis=-1, keepdims=True)) + cosine_eps)
        cosine_sim = lax.optimization_barrier(jnp.sum(output * target, axis=-1, keepdims=True)) / (norm_out * norm_tar)
        loss_part = jnp.sum(1.0 - cosine_sim)
        out_grad = (-(target / (norm_out * norm_tar) - cosine_sim * output / (norm_out * norm_out)) / ROWS).astype(jnp.bfloat16)
        att_grad = lax.dot_general(out_grad, w_output, (((1,), (1,)), ((), ())), preferred_element_type=jnp.float32).astype(jnp.bfloat16).reshape(R, QH, HD)
        query_part, key_part, value_part = attend_grad(softmax_rows, softmax_low, queries, keys_head, values_head, att_grad)
        query_grad = unrotate(query_part, cosine, sine_table).astype(jnp.bfloat16).reshape(R, QH * HD)
        key_sum = lax.optimization_barrier(jnp.sum(key_part.reshape(R, head_group, KV, HD), axis=1))
        value_sum = lax.optimization_barrier(jnp.sum(value_part.reshape(R, head_group, KV, HD), axis=1))
        keyval_grad = jnp.stack([unrotate(key_sum, cosine, sine_table), value_sum], axis=2).astype(jnp.bfloat16).reshape(R, 2 * KV * HD)
        grad_query = grad_query + held_low(contract_rows(normed, query_grad))
        grad_keyval = grad_keyval + held_low(contract_rows(normed, keyval_grad))
        grad_output = grad_output + held_low(contract_rows(att_flat, out_grad))
        return ((grad_query, grad_keyval, grad_output, loss_sum + loss_part), None)
    start_state = (jnp.zeros((D, QH * HD), jnp.float32), jnp.zeros((D, 2 * KV * HD), jnp.float32), jnp.zeros((QH * HD, D), jnp.float32), jnp.zeros((), jnp.float32))
    final_state, _ = lax.scan(one_group, start_state, (shallow_groups, teacher_groups, position_groups, segment_groups))
    grad_query, grad_keyval, grad_output, loss_sum = final_state
    square_total = jnp.sum(grad_query * grad_query) + jnp.sum(grad_keyval * grad_keyval) + jnp.sum(grad_output * grad_output)
    grad_rms = jnp.sqrt(square_total / (D * (2 * QH * HD + 2 * KV * HD)) + mean_eps)
    return (loss_sum / ROWS, grad_query / grad_rms, grad_keyval / grad_rms, grad_output / grad_rms)
```

```python
import functools
import math

import jax
import jax.numpy as jnp
from jax import lax
from jax.experimental import pallas as pl
from jax.experimental.pallas import tpu as pltpu
from jax.sharding import PartitionSpec as P

D = 8192
HD = 128
QH = 32
KV = 4
NP = 8
NX = 4
BLK = 512
ROWS = 256
HALF = 256
QUART = 128
WQ = 640

theta_base = 10000.0
norm_eps = 1e-05
cosine_eps = 1e-06
mean_eps = 1e-12
mask_fill = -1e30

MESH = pl.DeviceIdType.MESH
F32 = jnp.float32
BF16 = jnp.bfloat16
VLIM = 60 * 1024 * 1024


def remote(src, dst, send_sem, recv_sem, device):
    return pltpu.make_async_remote_copy(
        src_ref=src, dst_ref=dst, send_sem=send_sem, recv_sem=recv_sem,
        device_id=device, device_id_type=MESH,
    )


class Place:
    def __init__(self):
        dp = lax.axis_index("dp")
        self.dp = dp
        self.pipe = lax.axis_index("pipe")
        self.x = dp // 4
        self.z = (dp // 2) % 2
        self.c = dp % 2
        self.o = 1 - self.c
        self.slot = dp // 2
        self.swap_dp = self.pipe * 2 + self.c
        self.swap_pipe = self.slot
        self.swaps = self.slot != self.pipe

    def plane(self, dx, flip):
        z = 1 - self.z if flip else self.z
        return ((self.x + dx) % NX * 4 + z * 2 + self.c, self.pipe)

    def slot_of(self, dx, flip):
        z = 1 - self.z if flip else self.z
        return (self.x + dx) % NX * 2 + z

    def column(self, dj, other):
        dp = self.slot * 2 + (self.o if other else self.c)
        return (dp, (self.pipe + dj) % NP)

    def swap(self):
        return (self.swap_dp, self.swap_pipe)


def greet(devices, swap_place=None):
    barrier = pltpu.get_barrier_semaphore()
    for device in devices:
        pl.semaphore_signal(barrier, inc=1, device_id=device, device_id_type=MESH)
    if swap_place is None:
        pl.semaphore_wait(barrier, len(devices))
    else:
        @pl.when(swap_place.swaps)
        def _():
            pl.semaphore_signal(
                barrier, inc=1, device_id=swap_place.swap(), device_id_type=MESH
            )

        pl.semaphore_wait(barrier, len(devices) + swap_place.swaps.astype(jnp.int32))


GATHER = {
    "a_z": (0, 0, 0, HALF, "z"),
    "a_xp": (0, 0, 0, HALF, "p"),
    "a_xm": (0, 0, 0, HALF, "m"),
    "a_fp": (-1, 0, 0, QUART, "p"),
    "a_fm": (1, 0, QUART, QUART, "m"),
    "az_xp": (0, 1, 0, HALF, "p"),
    "az_xm": (0, 1, 0, HALF, "m"),
    "az_fp": (-1, 1, 0, QUART, "p"),
    "az_fm": (1, 1, QUART, QUART, "m"),
    "b_xp": (0, 0, HALF, HALF, "p"),
    "b_xm": (0, 0, HALF, HALF, "m"),
    "b_fp": (-1, 0, HALF, QUART, "p"),
    "b_fm": (1, 0, HALF + QUART, QUART, "m"),
    "b_z0": (0, 0, HALF, HALF, "z"),
    "b_zm": (-1, 0, HALF, HALF, "z"),
    "b_zp": (1, 0, HALF, HALF, "z"),
    "b_z2a": (2, 0, HALF, QUART, "z"),
    "b_z2b": (2, 0, HALF + QUART, QUART, "z"),
}
N_GATHER = len(GATHER)


class Gather:
    def __init__(self, place, buf, send_sems, recv_sems):
        self.place, self.buf = place, buf
        self.send_sems, self.recv_sems = send_sems, recv_sems
        self.order = {name: k for k, name in enumerate(GATHER)}

    def out(self, name):
        dx, flip, row, rows, way = GATHER[name]
        place = self.place
        k = self.order[name]
        region = self.buf.at[place.slot_of(dx, flip), pl.ds(row, rows)]
        device = {
            "p": place.plane(1, 0), "m": place.plane(-1, 0), "z": place.plane(0, 1)
        }[way]
        return remote(region, region, self.send_sems.at[k], self.recv_sems.at[k], device)

    def arrival(self, name):
        dx, flip, row, rows, way = GATHER[name]
        place = self.place
        k = self.order[name]
        dx = dx + {"p": -1, "m": 1, "z": 0}[way]
        flip = 1 - flip if way == "z" else flip
        region = self.buf.at[place.slot_of(dx, flip), pl.ds(row, rows)]
        return remote(
            region, region, self.send_sems.at[k], self.recv_sems.at[k], place.plane(0, 1)
        )

    def start(self, *names):
        for name in names:
            self.out(name).start()

    def wait(self, *names):
        for name in names:
            self.arrival(name).wait_recv()

    def begin(self):
        self.start("a_z", "a_xp", "a_xm", "b_xp", "b_xm", "b_z0")

    def middle(self):
        self.wait("a_z")
        self.start("az_xp", "az_xm")
        self.wait("a_xp")
        self.start("a_fp")
        self.wait("a_xm")
        self.start("a_fm")
        self.wait("b_xp")
        self.start("b_fp", "b_zm")
        self.wait("b_xm")
        self.start("b_fm", "b_zp")

    def late(self):
        self.wait("az_xp")
        self.start("az_fp")
        self.wait("az_xm")
        self.start("az_fm")
        self.wait("b_fp")
        self.start("b_z2a")
        self.wait("b_fm")
        self.start("b_z2b")

    def finish(self):
        self.wait("a_fp", "a_fm", "az_fp", "az_fm", "b_z0", "b_zm", "b_zp", "b_z2a", "b_z2b")

    def drain(self):
        for name in GATHER:
            self.out(name).wait_send()


def turned(v, cosine, sine):
    half = HD // 2
    rolled = jnp.concatenate([v[:, half:], v[:, :half]], axis=1)
    return v * cosine + rolled * sine


def front_kernel(
    shallow, gain, wq, wkv, wo, teacher, cosine, sine,
    q_out, kv_out, normed_out, wo_out, target_out,
    wbuf, nbuf, pbuf, acc, mine, theirs,
    w_send, w_recv, o_send, o_recv, n_send, n_recv, t_send, t_recv, k_send, k_recv,
    s_send, s_recv, local_sems,
):
    at = Place()
    column = [(dj, other) for other in (0, 1) for dj in range(NP) if (dj, other) != (0, 0)]
    greet(
        [at.plane(1, 0), at.plane(-1, 0), at.plane(0, 1)] + [at.column(*d) for d in column],
        at,
    )
    peer = at.column(0, 1)

    wbuf[at.slot, :, pl.ds(0, BLK)] = wq[...]
    wbuf[at.slot, :, pl.ds(BLK, HD)] = wkv[...]
    wg = Gather(at, wbuf, w_send, w_recv)
    og = Gather(at, wo_out, o_send, o_recv)
    wg.begin()

    swap = remote(wo, wo_out.at[at.pipe], s_send.at[0], s_recv.at[0], at.swap())
    keep = pltpu.make_async_copy(wo, wo_out.at[at.pipe], local_sems.at[0])

    @pl.when(at.swaps)
    def _():
        swap.start()

    @pl.when(jnp.logical_not(at.swaps))
    def _():
        keep.start()

    def target_copy(k):
        dj, other = column[k]
        core = at.o if other else at.c
        first = pl.multiple_of((((at.pipe + dj) % NP) * 2 + core) * BLK, BLK)
        return remote(
            teacher.at[:, pl.ds(first, BLK)],
            target_out.at[at.c, (at.pipe + 1) % NP],
            t_send.at[k], t_recv.at[k], at.column(dj, other),
        )

    def target_arrival(k):
        dj, other = column[k]
        core = at.o if other else at.c
        region = target_out.at[core, (at.pipe - dj + NP + 1) % NP]
        return remote(region, region, t_send.at[k], t_recv.at[k], peer)

    for k in range(len(column)):
        target_copy(k).start()
    first = pl.multiple_of((at.pipe * 2 + at.c) * BLK, BLK)
    own_target = pltpu.make_async_copy(
        teacher.at[:, pl.ds(first, BLK)], target_out.at[at.c, (at.pipe + 1) % NP], local_sems.at[1]
    )
    own_target.start()

    mine_rows = pl.multiple_of(at.c * ROWS, ROWS)
    their_rows = pl.multiple_of(at.o * ROWS, ROWS)

    @pl.loop(0, ROWS // 32)
    def _(step):
        rows = pl.ds(pl.multiple_of(step * 32, 32), 32)

        def squares(k, total):
            part = shallow[rows, pl.ds(pl.multiple_of(k * 1024, 1024), 1024)].astype(F32)
            return total + jnp.sum(part * part, axis=1, keepdims=True)

        total = lax.fori_loop(0, 8, squares, jnp.zeros((32, 1), F32))
        scale = lax.rsqrt(total / D + norm_eps)

        @pl.loop(0, NP)
        def _(k):
            here = pl.ds(pl.multiple_of((k * 2 + at.c) * BLK, BLK), BLK)
            there = pl.ds(pl.multiple_of((k * 2 + at.o) * BLK, BLK), BLK)
            nrows = pl.ds(pl.multiple_of(mine_rows + step * 32, 32), 32)
            nbuf[k, nrows, :] = (shallow[rows, here].astype(F32) * scale * gain[:, here]).astype(BF16)
            pbuf[k, rows, :] = (shallow[rows, there].astype(F32) * scale * gain[:, there]).astype(BF16)

    swapped_rows = nbuf.at[:, pl.ds(mine_rows, ROWS)]
    normed_copy = remote(pbuf, swapped_rows, n_send.at[0], n_recv.at[0], peer)
    normed_copy.start()

    wg.middle()
    landed = nbuf.at[:, pl.ds(their_rows, ROWS)]
    remote(pbuf, landed, n_send.at[0], n_recv.at[0], peer).wait_recv()
    save = pltpu.make_async_copy(nbuf, normed_out, local_sems.at[2])
    save.start()
    wg.late()

    @pl.when(at.swaps)
    def _():
        remote(wo, wo_out.at[at.slot], s_send.at[0], s_recv.at[0], at.swap()).wait_recv()
        swap.wait_send()

    @pl.when(jnp.logical_not(at.swaps))
    def _():
        keep.wait()

    og.begin()
    wg.finish()

    acc[...] = jnp.zeros_like(acc)

    @pl.loop(0, NP)
    def _(k):
        acc[...] += jnp.dot(nbuf[k], wbuf[k], preferred_element_type=F32)

    mine[...] = acc[pl.ds(their_rows, ROWS), :]
    sums = remote(mine, theirs, n_send.at[1], n_recv.at[1], peer)
    sums.start()
    og.middle()
    sums.wait_recv()

    cos_table, sin_table = cosine[...], sine[...]
    for head in range(BLK // HD):
        cols = pl.ds(head * HD, HD)
        v = acc[pl.ds(mine_rows, ROWS), cols] + theirs[:, cols]
        q_out[:, cols] = turned(v, cos_table, sin_table).astype(BF16)
    cols = pl.ds(BLK, HD)
    v = acc[pl.ds(mine_rows, ROWS), cols] + theirs[:, cols]
    is_key = (at.pipe % 2 == 0).astype(F32)
    kv_out[at.pipe] = (turned(v, cos_table, sin_table) * is_key + v * (1.0 - is_key)).astype(BF16)

    def kv_copy(dj):
        region = kv_out.at[at.pipe]
        return remote(region, region, k_send.at[dj], k_recv.at[dj], at.column(dj, 0))

    def kv_arrival(dj):
        region = kv_out.at[(at.pipe - dj + NP) % NP]
        return remote(region, region, k_send.at[dj], k_recv.at[dj], peer)

    for dj in range(1, NP):
        kv_copy(dj).start()
    og.late()
    og.finish()
    for dj in range(1, NP):
        kv_arrival(dj).wait_recv()
    for k in range(len(column)):
        target_arrival(k).wait_recv()

    own_target.wait()
    save.wait()
    normed_copy.wait_send()
    sums.wait_send()
    wg.drain()
    og.drain()
    for dj in range(1, NP):
        kv_copy(dj).wait_send()
    for k in range(len(column)):
        target_copy(k).wait_send()


def front(shallow, gain, wq, wkv, wo, teacher, cosine, sine):
    vmem = pl.BlockSpec(memory_space=pltpu.VMEM)
    anyspace = pl.BlockSpec(memory_space=pl.ANY)
    dma = pltpu.SemaphoreType.DMA
    return pl.pallas_call(
        front_kernel,
        out_shape=(
            jax.ShapeDtypeStruct((ROWS, BLK), BF16),
            jax.ShapeDtypeStruct((NP, ROWS, HD), BF16),
            jax.ShapeDtypeStruct((NP, 2 * ROWS, BLK), BF16),
            jax.ShapeDtypeStruct((NP, BLK, BLK), BF16),
            jax.ShapeDtypeStruct((2, NP, ROWS // NP, BLK), BF16),
        ),
        in_specs=[vmem, vmem, vmem, vmem, anyspace, anyspace, vmem, vmem],
        out_specs=(vmem, vmem, anyspace, anyspace, anyspace),
        scratch_shapes=[
            pltpu.VMEM((NP, BLK, WQ), BF16),
            pltpu.VMEM((NP, 2 * ROWS, BLK), BF16),
            pltpu.VMEM((NP, ROWS, BLK), BF16),
            pltpu.VMEM((2 * ROWS, WQ), F32),
            pltpu.VMEM((ROWS, WQ), F32),
            pltpu.VMEM((ROWS, WQ), F32),
            dma((N_GATHER,)), dma((N_GATHER,)), dma((N_GATHER,)), dma((N_GATHER,)),
            dma((2,)), dma((2,)), dma((15,)), dma((15,)), dma((NP,)), dma((NP,)),
            dma((1,)), dma((1,)), dma((3,)),
        ],
        compiler_params=pltpu.CompilerParams(
            collective_id=0, has_side_effects=True, vmem_limit_bytes=VLIM
        ),
        name="front",
    )(shallow, gain, wq, wkv, wo, teacher, cosine, sine)


COLUMN = [(dj, other) for other in (0, 1) for dj in range(NP) if (dj, other) != (0, 0)]


def nt(left, right):
    return lax.dot_general(
        left, right, (((1,), (1,)), ((), ())), preferred_element_type=F32
    )


def middle_kernel(
    attended, wo, shallow, target,
    grad_out, all_out, og_out, loss_out,
    abuf, wbuf, sbuf, acc, lanes, square, stat_send, stat_recv,
    part_mine, part_send, part_recv, sum_send, sum_recv,
    a_send, a_recv, f_send, f_recv, s_send, s_recv, p_send, p_recv, r_send, r_recv,
    h_send, h_recv, local_sems,
):
    at = Place()
    greet([at.column(*d) for d in COLUMN])
    peer = at.column(0, 1)
    mine_rows = pl.multiple_of(at.c * ROWS, ROWS)
    their_rows = pl.multiple_of(at.o * ROWS, ROWS)
    mine = pl.ds(mine_rows, ROWS)
    theirs = pl.ds(their_rows, ROWS)

    load = pltpu.make_async_copy(wo, wbuf, local_sems.at[0])
    load.start()
    abuf[at.pipe, mine, :] = attended[...]

    def share(dj):
        region = abuf.at[at.pipe, mine]
        return remote(region, region, a_send.at[dj], a_recv.at[dj], at.column(dj, 0))

    def arrival(dj):
        region = abuf.at[(at.pipe - dj + NP) % NP, mine]
        return remote(region, region, a_send.at[dj], a_recv.at[dj], peer)

    def forward(dj):
        region = abuf.at[(at.pipe - dj + NP) % NP, mine]
        return remote(region, region, f_send.at[dj], f_recv.at[dj], peer)

    def forwarded(dj):
        region = abuf.at[(at.pipe - dj + NP) % NP, theirs]
        return remote(region, region, f_send.at[dj], f_recv.at[dj], peer)

    for dj in range(1, NP):
        share(dj).start()
    forward(0).start()

    here = pl.ds(pl.multiple_of((at.pipe * 2 + at.c) * BLK, BLK), BLK)
    there = pl.ds(pl.multiple_of((at.pipe * 2 + at.o) * BLK, BLK), BLK)
    own_rows = pltpu.make_async_copy(shallow.at[:, here], sbuf.at[mine], local_sems.at[1])
    own_rows.start()
    peer_rows = remote(shallow.at[:, there], sbuf.at[mine], h_send.at[0], h_recv.at[0], peer)
    peer_rows.start()

    acc[...] = jnp.zeros_like(acc)
    load.wait()

    def multiply(dj):
        forwarded(dj).wait_recv()
        source = (at.pipe - dj + NP) % NP
        acc[...] += jnp.dot(abuf[source], wbuf[source], preferred_element_type=F32)

    for dj in range(1, NP):
        arrival(dj).wait_recv()
        forward(dj).start()
        multiply(dj - 1)
    multiply(NP - 1)
    save = pltpu.make_async_copy(abuf, all_out, local_sems.at[2])
    save.start()
    own_rows.wait()
    landed = sbuf.at[theirs]
    remote(landed, landed, h_send.at[0], h_recv.at[0], peer).wait_recv()

    lane = lax.broadcasted_iota(jnp.int32, (64, 128), 1)

    @pl.loop(0, 2 * ROWS // 64)
    def _(step):
        rows = pl.ds(pl.multiple_of(step * 64, 64), 64)
        output = acc[rows, :] + sbuf[rows, :].astype(F32)
        acc[rows, :] = output
        wanted = target[rows, :].astype(F32)
        oo = jnp.sum(output * output, axis=1, keepdims=True)
        tt = jnp.sum(wanted * wanted, axis=1, keepdims=True)
        ot = jnp.sum(output * wanted, axis=1, keepdims=True)
        lanes[rows, :] = jnp.where(lane == 0, oo, jnp.where(lane == 1, tt, jnp.where(lane == 2, ot, 0.0)))

    square[...] = lanes[...].T
    stat_send[...] = square[pl.ds(0, 8), :]

    def stat(k):
        return remote(stat_send, stat_recv.at[k], s_send.at[k], s_recv.at[k], at.column(*COLUMN[k]))

    for k in range(len(COLUMN)):
        stat(k).start()
    total = stat_send[...]
    for k in range(len(COLUMN)):
        stat(k).wait_recv()
    for k in range(len(COLUMN)):
        total = total + stat_recv[k]
    square[pl.ds(0, 8), :] = total
    lanes[...] = square[...].T

    def gradient(step, lost):
        rows = pl.ds(pl.multiple_of(step * 64, 64), 64)
        output = acc[rows, :]
        wanted = target[rows, :].astype(F32)
        norm_out = jnp.sqrt(lanes[rows, 0:1] + cosine_eps)
        norm_tar = jnp.sqrt(lanes[rows, 1:2] + cosine_eps)
        both = norm_out * norm_tar
        cosine = lanes[rows, 2:3] / both
        og = -(wanted * (1.0 / both) - output * (cosine / (norm_out * norm_out))) * (1.0 / 4096)
        og_out[rows, :] = og.astype(BF16)
        return lost + (1.0 - cosine)

    lost = lax.fori_loop(0, 2 * ROWS // 64, gradient, jnp.zeros((64, 1), F32))
    loss_out[...] = jnp.broadcast_to(jnp.sum(lost, axis=0, keepdims=True), (8, 128))

    def part(dj):
        return remote(part_send.at[dj], part_recv.at[dj], p_send.at[dj], p_recv.at[dj], peer)

    def result(dj):
        return remote(sum_send.at[dj], sum_recv.at[dj], r_send.at[dj], r_recv.at[dj], at.column(dj, 0))

    def produce(dj):
        weights = wbuf[(at.pipe + dj) % NP]
        part_send[dj] = nt(og_out[theirs, :], weights).astype(BF16)
        part(dj).start()
        part_mine[dj] = nt(og_out[mine, :], weights).astype(BF16)

    def send_on(dj):
        part(dj).wait_recv()
        sum_send[dj] = (part_mine[dj].astype(F32) + part_recv[dj].astype(F32)).astype(BF16)
        result(dj).start()

    steps = list(range(1, NP)) + [0]
    for k, dj in enumerate(steps):
        produce(dj)
        if k >= 1:
            send_on(steps[k - 1])
    part(0).wait_recv()
    for dj in range(1, NP):
        result(dj).wait_recv()

    @pl.loop(0, ROWS // 64)
    def _(step):
        rows = pl.ds(pl.multiple_of(step * 64, 64), 64)
        total = part_mine[0, rows, :].astype(F32) + part_recv[0, rows, :].astype(F32)
        for dj in range(1, NP):
            total = total + sum_recv[dj, rows, :].astype(F32)
        grad_out[rows, :] = total.astype(BF16)

    save.wait()
    peer_rows.wait_send()
    for dj in range(NP):
        forward(dj).wait_send()
        part(dj).wait_send()
    for dj in range(1, NP):
        share(dj).wait_send()
        result(dj).wait_send()
    for k in range(len(COLUMN)):
        stat(k).wait_send()


def middle(attended, wo, shallow, target):
    vmem = pl.BlockSpec(memory_space=pltpu.VMEM)
    anyspace = pl.BlockSpec(memory_space=pl.ANY)
    dma = pltpu.SemaphoreType.DMA
    blocks = pltpu.VMEM((NP, ROWS, BLK), BF16)
    return pl.pallas_call(
        middle_kernel,
        out_shape=(
            jax.ShapeDtypeStruct((ROWS, BLK), BF16),
            jax.ShapeDtypeStruct((NP, 2 * ROWS, BLK), BF16),
            jax.ShapeDtypeStruct((2 * ROWS, BLK), BF16),
            jax.ShapeDtypeStruct((8, 128), F32),
        ),
        in_specs=[vmem, anyspace, anyspace, vmem],
        out_specs=(vmem, anyspace, vmem, vmem),
        scratch_shapes=[
            pltpu.VMEM((NP, 2 * ROWS, BLK), BF16),
            pltpu.VMEM((NP, BLK, BLK), BF16),
            pltpu.VMEM((2 * ROWS, BLK), BF16),
            pltpu.VMEM((2 * ROWS, BLK), F32),
            pltpu.VMEM((2 * ROWS, 128), F32),
            pltpu.VMEM((128, 2 * ROWS), F32),
            pltpu.VMEM((8, 2 * ROWS), F32),
            pltpu.VMEM((15, 8, 2 * ROWS), F32),
            blocks, blocks, blocks, blocks, blocks,
            dma((NP,)), dma((NP,)), dma((NP,)), dma((NP,)), dma((15,)), dma((15,)),
            dma((NP,)), dma((NP,)), dma((NP,)), dma((NP,)), dma((1,)), dma((1,)), dma((3,)),
        ],
        compiler_params=pltpu.CompilerParams(
            collective_id=1, has_side_effects=True, vmem_limit_bytes=VLIM
        ),
        name="middle",
    )(attended, wo, shallow, target)


PLANES = [(dx, flip) for flip in (0, 1) for dx in range(NX) if (dx, flip) != (0, 0)]
N_REDUCE = 17


def tn(left, right):
    return lax.dot_general(
        left, right, (((0,), (0,)), ((), ())), preferred_element_type=F32
    )


class Reduce:
    def __init__(self, place, terms, corner, near, cross, cross_b, send_sems, recv_sems):
        self.place, self.terms = place, terms
        self.corner, self.near, self.cross, self.cross_b = corner, near, cross, cross_b
        self.send_sems, self.recv_sems = send_sems, recv_sems
        self.started = []

    def copy(self, k, dx, flip, row, rows, landing, device):
        source = self.terms.at[self.place.slot_of(dx, flip), pl.ds(row, rows)]
        return remote(source, landing, self.send_sems.at[k], self.recv_sems.at[k], device)

    def go(self, *what):
        copy = self.copy(*what)
        copy.start()
        self.started.append(copy)

    def wait(self, k, landing):
        remote(
            landing, landing, self.send_sems.at[k], self.recv_sems.at[k], self.place.plane(0, 1)
        ).wait_recv()

    def add(self, dx, flip, row, rows, *landings):
        slot = self.place.slot_of(dx, flip)

        @pl.loop(0, rows // 32)
        def _(step):
            low = pl.multiple_of(step * 32, 32)
            here = pl.ds(pl.multiple_of(row + low, 32), 32)
            total = self.terms[slot, here, :].astype(F32)
            for landing in landings:
                total = total + landing[pl.ds(low, 32), :].astype(F32)
            self.terms[slot, here, :] = total.astype(BF16)

    def x_begin(self, n):
        flip, row = (n, 0) if n < 2 else (0, HALF)
        self.go(4 * n, 2, flip, row, QUART, self.corner.at[n, 0], self.place.plane(1, 0))
        self.go(4 * n + 1, 2, flip, row + QUART, QUART, self.corner.at[n, 1], self.place.plane(-1, 0))

    def x_pass(self, n):
        flip, row = (n, 0) if n < 2 else (0, HALF)
        self.wait(4 * n, self.corner.at[n, 0])
        self.add(1, flip, row, QUART, self.corner.at[n, 0])
        self.go(4 * n + 2, 1, flip, row, HALF, self.near.at[n, 0], self.place.plane(1, 0))
        self.wait(4 * n + 1, self.corner.at[n, 1])
        self.add(-1, flip, row + QUART, QUART, self.corner.at[n, 1])
        self.go(4 * n + 3, -1, flip, row, HALF, self.near.at[n, 1], self.place.plane(-1, 0))

    def x_end(self, n):
        flip, row = (n, 0) if n < 2 else (0, HALF)
        self.wait(4 * n + 2, self.near.at[n, 0])
        self.wait(4 * n + 3, self.near.at[n, 1])
        self.add(0, flip, row, HALF, self.near.at[n, 0], self.near.at[n, 1])

    def z_second(self, dx):
        self.go(13 + dx, dx, 1, HALF, HALF, self.cross_b.at[dx], self.place.plane(0, 1))

    def z_second_add(self, dx):
        self.wait(13 + dx, self.cross_b.at[dx])
        self.add(dx, 0, HALF, HALF, self.cross_b.at[dx])

    def begin(self):
        self.z_second(2)
        self.x_begin(1)
        self.x_begin(0)
        for dx in (1, 3, 0):
            self.z_second(dx)

    def middle(self):
        self.x_pass(1)
        self.z_second_add(2)
        self.x_begin(2)
        self.x_pass(0)
        self.z_second_add(1)
        self.z_second_add(3)
        self.x_pass(2)

    def late(self):
        self.x_end(1)
        self.go(12, 0, 1, 0, HALF, self.cross, self.place.plane(0, 1))
        self.x_end(0)
        self.z_second_add(0)

    def finish(self):
        self.x_end(2)
        self.wait(12, self.cross)
        self.add(0, 0, 0, HALF, self.cross)

    def drain(self):
        for copy in self.started:
            copy.wait_send()


def squares_of(read, rows, width):
    def step(k, total):
        v = read(pl.ds(pl.multiple_of(k * 32, 32), 32)).astype(F32)
        v = jnp.sum((v * v).reshape(4, 8, width), axis=0)
        for first in range(0, width, 128):
            total = total + v[:, first:first + 128]
        return total

    return lax.fori_loop(0, rows // 32, step, jnp.zeros((8, 128), F32))


def back_kernel(
    normed, att_all, og, q_grad, kv_part, cosine, sine, loss,
    gq_out, go_out, stat_out,
    nbuf, abuf, both, kv_recv, o_terms, o_corner, o_near, o_cross, o_cross_b,
    q_terms, q_corner, q_near, q_cross, q_cross_b, stat_one, stat_two, from_column, from_plane,
    o_send, o_recv, q_send, q_recv, k_send, k_recv, g_send, g_recv, s_send, s_recv,
    c_send, c_recv, p_send, p_recv, local_sems,
):
    at = Place()
    greet([at.plane(*d) for d in PLANES] + [at.column(*d) for d in COLUMN], at)
    peer = at.column(0, 1)
    mine = pl.ds(pl.multiple_of(at.c * ROWS, ROWS), ROWS)
    theirs = pl.ds(pl.multiple_of(at.o * ROWS, ROWS), ROWS)

    def kv_copy(dj):
        return remote(
            kv_part.at[(at.pipe + dj) % NP], kv_recv.at[dj], k_send.at[dj], k_recv.at[dj],
            at.column(dj, 0),
        )

    for dj in range(1, NP):
        kv_copy(dj).start()
    load_att = pltpu.make_async_copy(att_all, abuf, local_sems.at[0])
    load_att.start()
    load_normed = pltpu.make_async_copy(normed, nbuf, local_sems.at[1])
    load_normed.start()

    load_att.wait()

    @pl.loop(0, NP)
    def _(k):
        o_terms[k] = tn(abuf[k], og[...]).astype(BF16)

    out_reduce = Reduce(at, o_terms, o_corner, o_near, o_cross, o_cross_b, o_send, o_recv)
    query_reduce = Reduce(at, q_terms, q_corner, q_near, q_cross, q_cross_b, q_send, q_recv)
    out_reduce.begin()

    total = kv_part[at.pipe].astype(F32)
    for dj in range(1, NP):
        kv_copy(dj).wait_recv()
        total = total + kv_recv[dj].astype(F32)
    is_key = (at.pipe % 2 == 0).astype(F32)
    total = turned(total, cosine[...], -sine[...]) * is_key + total * (1.0 - is_key)
    both[mine, pl.ds(0, BLK)] = q_grad[...]
    both[mine, pl.ds(BLK, HD)] = total.astype(BF16)
    exchange = remote(both.at[mine], both.at[mine], g_send.at[0], g_recv.at[0], peer)
    exchange.start()
    load_normed.wait()
    remote(both.at[theirs], both.at[theirs], g_send.at[0], g_recv.at[0], peer).wait_recv()

    @pl.loop(0, NP)
    def _(k):
        q_terms[k] = tn(nbuf[k], both[...]).astype(BF16)

    out_reduce.middle()
    query_reduce.begin()
    out_reduce.late()
    out_reduce.finish()

    own = at.slot
    swap = remote(o_terms.at[own], go_out, s_send.at[0], s_recv.at[0], at.swap())
    keep = pltpu.make_async_copy(o_terms.at[own], go_out, local_sems.at[2])

    @pl.when(at.swaps)
    def _():
        swap.start()

    @pl.when(jnp.logical_not(at.swaps))
    def _():
        keep.start()

    tile = squares_of(lambda rows: o_terms[own, rows, :], BLK, BLK)
    query_reduce.middle()
    query_reduce.late()
    query_reduce.finish()
    gq_out[...] = q_terms[own]
    stat_one[pl.ds(0, 8), :] = tile + squares_of(lambda rows: q_terms[own, rows, :], BLK, WQ)
    stat_one[pl.ds(8, 8), :] = loss[...]

    def column_copy(k):
        return remote(stat_one, from_column.at[k], c_send.at[k], c_recv.at[k], at.column(*COLUMN[k]))

    def plane_copy(k):
        return remote(stat_two, from_plane.at[k], p_send.at[k], p_recv.at[k], at.plane(*PLANES[k]))

    for k in range(len(COLUMN)):
        column_copy(k).start()
    total = stat_one[...]
    for k in range(len(COLUMN)):
        column_copy(k).wait_recv()
        total = total + from_column[k]
    stat_two[...] = total
    for k in range(len(PLANES)):
        plane_copy(k).start()
    for k in range(len(PLANES)):
        plane_copy(k).wait_recv()
        total = total + from_plane[k]
    stat_out[...] = total

    @pl.when(at.swaps)
    def _():
        swap.wait_recv()
        swap.wait_send()

    @pl.when(jnp.logical_not(at.swaps))
    def _():
        keep.wait()

    out_reduce.drain()
    query_reduce.drain()
    exchange.wait_send()
    for dj in range(1, NP):
        kv_copy(dj).wait_send()
    for k in range(len(COLUMN)):
        column_copy(k).wait_send()
    for k in range(len(PLANES)):
        plane_copy(k).wait_send()


def back(normed, att_all, og, q_grad, kv_part, cosine, sine, loss):
    vmem = pl.BlockSpec(memory_space=pltpu.VMEM)
    anyspace = pl.BlockSpec(memory_space=pl.ANY)
    dma = pltpu.SemaphoreType.DMA

    def buffers(width):
        return [
            pltpu.VMEM((NP, BLK, width), BF16),
            pltpu.VMEM((3, 2, QUART, width), BF16),
            pltpu.VMEM((3, 2, HALF, width), BF16),
            pltpu.VMEM((HALF, width), BF16),
            pltpu.VMEM((4, HALF, width), BF16),
        ]

    return pl.pallas_call(
        back_kernel,
        out_shape=(
            jax.ShapeDtypeStruct((BLK, WQ), BF16),
            jax.ShapeDtypeStruct((BLK, BLK), BF16),
            jax.ShapeDtypeStruct((16, 128), F32),
        ),
        in_specs=[anyspace, anyspace, vmem, vmem, vmem, vmem, vmem, vmem],
        out_specs=(vmem, vmem, vmem),
        scratch_shapes=[
            pltpu.VMEM((NP, 2 * ROWS, BLK), BF16),
            pltpu.VMEM((NP, 2 * ROWS, BLK), BF16),
            pltpu.VMEM((2 * ROWS, WQ), BF16),
            pltpu.VMEM((NP, ROWS, HD), BF16),
            *buffers(BLK), *buffers(WQ),
            pltpu.VMEM((16, 128), F32),
            pltpu.VMEM((16, 128), F32),
            pltpu.VMEM((15, 16, 128), F32),
            pltpu.VMEM((7, 16, 128), F32),
            dma((N_REDUCE,)), dma((N_REDUCE,)), dma((N_REDUCE,)), dma((N_REDUCE,)),
            dma((NP,)), dma((NP,)), dma((1,)), dma((1,)), dma((1,)), dma((1,)),
            dma((15,)), dma((15,)), dma((7,)), dma((7,)), dma((3,)),
        ],
        compiler_params=pltpu.CompilerParams(
            collective_id=2, has_side_effects=True, vmem_limit_bytes=VLIM
        ),
        name="back",
    )(normed, att_all, og, q_grad, kv_part, cosine, sine, loss)


def rotary_tables(positions):
    half_width = HD // 2
    exponent = jnp.arange(half_width).astype(F32) * (2.0 / HD)
    inverse = jnp.power(jnp.float32(theta_base), -exponent)
    angle_table = positions.astype(F32)[:, None] * inverse[None, :]
    cosine, sine = jnp.cos(angle_table), jnp.sin(angle_table)
    return jnp.concatenate([cosine, cosine], axis=1), jnp.concatenate([-sine, sine], axis=1)


def attend(queries, keys_head, values_head, allowed):
    score_scale = 1.0 / math.sqrt(queries.shape[-1])
    scores = (
        jnp.einsum("rhd,khd->hrk", queries, keys_head, preferred_element_type=F32) * score_scale
    )
    scores = jnp.where(allowed[None], scores, mask_fill)
    highest = jnp.max(scores, axis=-1, keepdims=True)
    weights = jnp.exp(scores - highest)
    softmax_rows = weights / jnp.sum(weights, axis=-1, keepdims=True)
    softmax_low = softmax_rows.astype(BF16)
    attended = jnp.einsum(
        "hrk,khd->rhd", softmax_low, values_head, preferred_element_type=F32
    ).astype(BF16)
    return (softmax_rows, softmax_low, attended)


def attend_grad(softmax_rows, softmax_low, queries, keys_head, values_head, att_grad):
    score_scale = 1.0 / math.sqrt(queries.shape[-1])
    inner_prod = jnp.einsum("rhd,khd->hrk", att_grad, values_head, preferred_element_type=F32)
    centred = inner_prod - jnp.sum(softmax_rows * inner_prod, axis=-1, keepdims=True)
    score_grad = (softmax_rows * centred * score_scale).astype(BF16)
    query_part = jnp.einsum("hrk,khd->rhd", score_grad, keys_head, preferred_element_type=F32)
    key_part = jnp.einsum("hrk,rhd->hkd", score_grad, queries, preferred_element_type=F32)
    value_part = jnp.einsum("hrk,rhd->hkd", softmax_low, att_grad, preferred_element_type=F32)
    return (query_part, key_part, value_part)


def per_device(shallow, teacher, positions, segments, in_gain, w_query, w_keyval, w_output):
    heads = BLK // HD
    all_rows = ROWS * lax.axis_size("dp")
    param_count = D * (2 * QH * HD + 2 * KV * HD)
    cosine, sine = rotary_tables(positions)
    queries, keyvals, normed, wo, target = front(
        shallow, in_gain[None], w_query, w_keyval, w_output, teacher, cosine, sine
    )
    queries = queries.reshape(ROWS, heads, HD)
    keyvals = keyvals.reshape(KV, 2, ROWS, HD)
    keys_head = keyvals[:, 0].transpose(1, 0, 2)
    values_head = keyvals[:, 1].transpose(1, 0, 2)
    row_order = jnp.arange(ROWS)
    allowed = (segments[:, None] == segments[None, :]) & (row_order[None, :] <= row_order[:, None])
    softmax_rows, softmax_low, attended = attend(queries, keys_head, values_head, allowed)
    att_grad, att_all, out_grad, loss = middle(
        attended.reshape(ROWS, BLK), wo, shallow, target.reshape(2 * ROWS, BLK)
    )
    query_part, key_part, value_part = attend_grad(
        softmax_rows, softmax_low, queries, keys_head, values_head, att_grad.reshape(ROWS, heads, HD)
    )
    half = HD // 2
    rolled = jnp.concatenate([query_part[..., half:], query_part[..., :half]], axis=-1)
    query_grad = (query_part * cosine[:, None] - rolled * sine[:, None]).astype(BF16)
    kv_part = jnp.stack([key_part, value_part], axis=1).astype(BF16).reshape(2 * KV, ROWS, HD)
    grad_qkv, grad_output, stats = back(
        normed, att_all, out_grad, query_grad.reshape(ROWS, BLK), kv_part, cosine, sine, loss
    )
    square_total = jnp.sum(stats[:8])
    inverse = 1.0 / jnp.sqrt(square_total / param_count + mean_eps)
    loss_total = stats[8, 0] / lax.axis_size("pipe") / 2
    grad_qkv = grad_qkv.astype(F32)
    return (
        loss_total / all_rows,
        grad_qkv[:, :BLK] * inverse,
        grad_qkv[:, BLK:] * inverse,
        grad_output.astype(F32) * inverse,
    )


def solution(mesh):
    placed = (
        P("dp", None),
        P(("dp", "pipe"), None),
        P("dp"),
        P("dp"),
        P(),
        P("dp", "pipe"),
        P("dp", "pipe"),
        P("pipe", "dp"),
    )
    return jax.shard_map(
        per_device,
        mesh=mesh,
        in_specs=placed,
        out_specs=(P(), P("dp", "pipe"), P("dp", "pipe"), P("pipe", "dp")),
        check_vma=False,
    )
```

```python
import functools
import math

import jax
import jax.numpy as jnp
from jax import lax
from jax.experimental import pallas as pl
from jax.experimental.pallas import tpu as pltpu
from jax.sharding import PartitionSpec as P

D = 8192
HD = 128
QH = 32
KV = 4
NP = 8
NX = 4
BLK = 512
ROWS = 256
WQ = 640

theta_base = 10000.0
norm_eps = 1e-05
cosine_eps = 1e-06
mean_eps = 1e-12
mask_fill = -1e30

MESH = pl.DeviceIdType.MESH
F32 = jnp.float32
BF16 = jnp.bfloat16
VLIM = 60 * 1024 * 1024


def remote(src, dst, send_sem, recv_sem, device):
    return pltpu.make_async_remote_copy(
        src_ref=src, dst_ref=dst, send_sem=send_sem, recv_sem=recv_sem,
        device_id=device, device_id_type=MESH,
    )


class Place:
    def __init__(self):
        dp = lax.axis_index("dp")
        self.dp = dp
        self.pipe = lax.axis_index("pipe")
        self.x = dp // 4
        self.z = (dp // 2) % 2
        self.c = dp % 2
        self.o = 1 - self.c
        self.y = self.pipe // 2
        self.high = self.pipe % 2
        self.slot = dp // 2
        self.swaps = self.slot != self.pipe

    def slot_of(self, axis, dx, flip):
        along, z = (self.x, self.z) if axis == "dp" else (self.y, self.high)
        return (along + dx + NX) % NX * 2 + (1 - z if flip else z)

    def near(self, axis, dx, flip):
        slot = self.slot_of(axis, dx, flip)
        return (slot * 2 + self.c, self.pipe) if axis == "dp" else (self.dp, slot)

    def cross(self, dx, flip, other):
        return (self.slot_of("dp", dx, flip) * 2 + (self.o if other else self.c), self.pipe)

    def column(self, dj, other):
        return (self.slot * 2 + (self.o if other else self.c), (self.pipe + dj) % NP)

    def swap(self):
        return (self.pipe * 2 + self.c, self.slot)


COLUMN = [(dj, other) for other in (0, 1) for dj in range(NP) if (dj, other) != (0, 0)]
PLANES = [(dx, flip) for flip in (0, 1) for dx in range(NX) if (dx, flip) != (0, 0)]
GROUP = [
    (dx, flip, other) for other in (0, 1) for flip in (0, 1) for dx in range(NX)
    if (dx, flip, other) != (0, 0, 0)
]


def greet(at):
    barrier = pltpu.get_barrier_semaphore()
    devices = [at.cross(*d) for d in GROUP] + [at.column(*d) for d in COLUMN]
    for device in devices:
        pl.semaphore_signal(barrier, inc=1, device_id=device, device_id_type=MESH)

    @pl.when(at.swaps)
    def _():
        pl.semaphore_signal(barrier, inc=1, device_id=at.swap(), device_id_type=MESH)

    pl.semaphore_wait(barrier, len(devices) + at.swaps.astype(jnp.int32))


FIRST = {
    "a_z": (0, 0, 0, 2, "z"),
    "a_xp": (0, 0, 0, 2, "p"),
    "a_xm": (0, 0, 0, 2, "m"),
    "a_fp": (-1, 0, 0, 1, "p"),
    "a_fm": (1, 0, 1, 1, "m"),
    "az_xp": (0, 1, 0, 2, "p"),
    "az_xm": (0, 1, 0, 2, "m"),
    "az_fp": (-1, 1, 0, 1, "p"),
    "az_fm": (1, 1, 1, 1, "m"),
}
SECOND = {
    "b_xp": (0, 0, 2, 2, "p"),
    "b_xm": (0, 0, 2, 2, "m"),
    "b_fp": (-1, 0, 2, 1, "p"),
    "b_fm": (1, 0, 3, 1, "m"),
    "b_z0": (0, 0, 2, 2, "z"),
    "b_zm": (-1, 0, 2, 2, "z"),
    "b_zp": (1, 0, 2, 2, "z"),
    "b_z2a": (2, 0, 2, 1, "z"),
    "b_z2b": (2, 0, 3, 1, "z"),
}
N_GATHER = len(FIRST) + len(SECOND)
N_FIRST = len(FIRST)


class Gather:
    def __init__(self, at, axis, view, rows, send_sems, recv_sems, halves):
        self.at, self.axis, self.view = at, axis, view
        self.send_sems, self.recv_sems = send_sems, recv_sems
        self.halves = halves
        self.table = {**FIRST, **SECOND} if halves else FIRST
        self.part = rows // 4 if halves else rows // 2
        self.order = {name: k for k, name in enumerate(self.table)}

    def copy(self, name, dx, flip):
        _, _, first, parts, way = self.table[name]
        k = self.order[name]
        region = self.view(
            self.at.slot_of(self.axis, dx, flip), first * self.part, parts * self.part
        )
        device = {
            "p": self.at.near(self.axis, 1, 0),
            "m": self.at.near(self.axis, -1, 0),
            "z": self.at.near(self.axis, 0, 1),
        }[way]
        return remote(region, region, self.send_sems.at[k], self.recv_sems.at[k], device)

    def out(self, name):
        return self.copy(name, self.table[name][0], self.table[name][1])

    def start(self, *names):
        for name in names:
            self.out(name).start()

    def wait(self, *names):
        for name in names:
            dx, flip, _, _, way = self.table[name]
            dx = dx + {"p": -1, "m": 1, "z": 0}[way]
            self.copy(name, dx, 1 - flip if way == "z" else flip).wait_recv()

    def begin(self):
        self.start("a_z", "a_xp", "a_xm")
        if self.halves:
            self.start("b_xp", "b_xm", "b_z0")

    def middle(self):
        self.wait("a_z")
        self.start("az_xp", "az_xm")
        self.wait("a_xp")
        self.start("a_fp")
        self.wait("a_xm")
        self.start("a_fm")
        if self.halves:
            self.wait("b_xp")
            self.start("b_fp", "b_zm")
            self.wait("b_xm")
            self.start("b_fm", "b_zp")

    def late(self):
        self.wait("az_xp")
        self.start("az_fp")
        self.wait("az_xm")
        self.start("az_fm")
        if self.halves:
            self.wait("b_fp")
            self.start("b_z2a")
            self.wait("b_fm")
            self.start("b_z2b")

    def finish(self):
        self.wait("a_fp", "a_fm", "az_fp", "az_fm")
        if self.halves:
            self.wait("b_z0", "b_zm", "b_zp", "b_z2a", "b_z2b")

    def drain(self):
        for name in self.table:
            self.out(name).wait_send()


N_REDUCE = 17
N_REDUCE_FIRST = 9


class Reduce:
    def __init__(self, at, axis, terms, rows, corner, near, cross, cross_b, send_sems, recv_sems):
        self.at, self.axis, self.terms = at, axis, terms
        self.corner, self.near, self.cross, self.cross_b = corner, near, cross, cross_b
        self.send_sems, self.recv_sems = send_sems, recv_sems
        self.half = rows if cross_b is None else rows // 2
        self.quarter = self.half // 2
        self.started = []

    def go(self, k, dx, flip, row, rows, landing, device):
        source = self.terms.at[self.at.slot_of(self.axis, dx, flip), pl.ds(row, rows)]
        copy = remote(
            source, landing, self.send_sems.at[k], self.recv_sems.at[k],
            self.at.near(self.axis, *device),
        )
        copy.start()
        self.started.append(copy)

    def wait(self, k, landing):
        remote(
            landing, landing, self.send_sems.at[k], self.recv_sems.at[k],
            self.at.near(self.axis, 0, 1),
        ).wait_recv()

    def add(self, dx, flip, row, rows, *landings):
        slot = self.at.slot_of(self.axis, dx, flip)

        @pl.loop(0, rows // 32)
        def _(step):
            low = pl.multiple_of(step * 32, 32)
            here = pl.ds(pl.multiple_of(row + low, 32), 32)
            total = self.terms[slot, here, :].astype(F32)
            for landing in landings:
                total = total + landing[pl.ds(low, 32), :].astype(F32)
            self.terms[slot, here, :] = total.astype(BF16)

    def where(self, n):
        return (n, 0) if n < 2 else (0, self.half)

    def x_begin(self, n):
        flip, row = self.where(n)
        quarter = self.quarter
        self.go(4 * n, 2, flip, row, quarter, self.corner.at[n, 0], (1, 0))
        self.go(4 * n + 1, 2, flip, row + quarter, quarter, self.corner.at[n, 1], (-1, 0))

    def x_pass(self, n):
        flip, row = self.where(n)
        quarter = self.quarter
        self.wait(4 * n, self.corner.at[n, 0])
        self.add(1, flip, row, quarter, self.corner.at[n, 0])
        self.go(4 * n + 2, 1, flip, row, self.half, self.near.at[n, 0], (1, 0))
        self.wait(4 * n + 1, self.corner.at[n, 1])
        self.add(-1, flip, row + quarter, quarter, self.corner.at[n, 1])
        self.go(4 * n + 3, -1, flip, row, self.half, self.near.at[n, 1], (-1, 0))

    def x_end(self, n):
        flip, row = self.where(n)
        self.wait(4 * n + 2, self.near.at[n, 0])
        self.wait(4 * n + 3, self.near.at[n, 1])
        self.add(0, flip, row, self.half, self.near.at[n, 0], self.near.at[n, 1])

    @property
    def z_sem(self):
        return 8 if self.cross_b is None else 12

    def z_first(self):
        self.go(self.z_sem, 0, 1, 0, self.half, self.cross, (0, 1))

    def z_first_add(self):
        self.wait(self.z_sem, self.cross)
        self.add(0, 0, 0, self.half, self.cross)

    def z_second(self, dx):
        self.go(13 + dx, dx, 1, self.half, self.half, self.cross_b.at[dx], (0, 1))

    def z_second_add(self, dx):
        self.wait(13 + dx, self.cross_b.at[dx])
        self.add(dx, 0, self.half, self.half, self.cross_b.at[dx])

    def begin(self):
        self.z_second(2)
        self.x_begin(1)
        self.x_begin(0)
        for dx in (1, 3, 0):
            self.z_second(dx)

    def middle(self):
        self.x_pass(1)
        self.z_second_add(2)
        self.x_begin(2)
        self.x_pass(0)
        self.z_second_add(1)
        self.z_second_add(3)
        self.x_pass(2)

    def late(self):
        self.x_end(1)
        self.z_first()
        self.x_end(0)
        self.z_second_add(0)

    def finish(self):
        self.x_end(2)
        self.z_first_add()

    def drain(self):
        for copy in self.started:
            copy.wait_send()


def nt(left, right):
    return lax.dot_general(
        left, right, (((1,), (1,)), ((), ())), preferred_element_type=F32
    )


def tn(left, right):
    return lax.dot_general(
        left, right, (((0,), (0,)), ((), ())), preferred_element_type=F32
    )


def turned(v, cosine, sine):
    half = HD // 2
    rolled = jnp.concatenate([v[:, half:], v[:, :half]], axis=1)
    return v * cosine + rolled * sine


def squares_of(read, rows, width):
    def step(k, total):
        v = read(pl.ds(pl.multiple_of(k * 32, 32), 32)).astype(F32)
        v = jnp.sum((v * v).reshape(4, 8, width), axis=0)
        for first in range(0, width, 128):
            total = total + v[:, first:first + 128]
        return total

    return lax.fori_loop(0, rows // 32, step, jnp.zeros((8, 128), F32))


def aligned(start, size):
    return pl.ds(pl.multiple_of(start, size), size)


def step_kernel(
    shallow, gain, wq, wkv, wo, teacher, cosine, sine, seg_column, seg_row,
    gq_out, go_out, stat_out,
    wbuf, obuf, nbuf, pbuf, tbuf, target, acc, sum_mine, sum_theirs, qbuf, kvbuf, probs,
    abuf, sbuf, ogbuf, lanes, square, stat_send, stat_recv,
    part_send, part_recv, g_terms, g_corner, g_near, g_cross,
    kv_part, kv_recv, o_terms, o_corner, o_near, o_cross, o_cross_b,
    qgbuf, stat_one, stat_two, from_column, from_plane,
    w_send, w_recv, o_send, o_recv, n_send, n_recv, x_send, x_recv, m_send, m_recv,
    t_send, t_recv, k_send, k_recv, swap_send, swap_recv,
    a_send, a_recv, f_send, f_recv, s_send, s_recv, p_send, p_recv, r_send, r_recv,
    d_send, d_recv, e_send, e_recv, q_send, q_recv, h_send, h_recv,
    c_send, c_recv, l_send, l_recv, local_sems,
):
    at = Place()
    mine = aligned(at.c * ROWS, ROWS)
    theirs = aligned(at.o * ROWS, ROWS)
    heads = BLK // HD
    greet(at)
    peer = at.column(0, 1)
    is_key = (at.pipe % 2 == 0).astype(F32)

    def slots(buf):
        return lambda slot, row, rows: buf.at[slot, pl.ds(row, rows)]

    def slots_mine(buf):
        return lambda slot, row, rows: buf.at[slot, aligned(at.c * ROWS + row, rows)]

    wg = Gather(at, "dp", slots(wbuf), BLK, w_send, w_recv, True)
    og = Gather(at, "dp", slots(obuf), BLK, o_send, o_recv, True)
    ng = Gather(
        at, "pipe", lambda slot, row, rows: tbuf.at[pl.ds(row, rows), aligned(slot * 32, 32)],
        16, m_send, m_recv, False,
    )
    ag = Gather(at, "pipe", slots_mine(abuf), ROWS, a_send, a_recv, False)
    qg = Gather(at, "dp", slots_mine(qgbuf), ROWS, q_send, q_recv, True)

    wbuf[at.slot, :, pl.ds(0, BLK)] = wq[...]
    wbuf[at.slot, :, pl.ds(BLK, HD)] = wkv[...]
    wg.begin()

    swap = remote(wo, obuf.at[at.pipe], swap_send.at[0], swap_recv.at[0], at.swap())
    keep = pltpu.make_async_copy(wo, obuf.at[at.pipe], local_sems.at[0])

    @pl.when(at.swaps)
    def _():
        swap.start()

    @pl.when(jnp.logical_not(at.swaps))
    def _():
        keep.start()

    def target_copy(k):
        dj, other = COLUMN[k]
        block = (at.pipe + dj) % NP * 2 + (at.o if other else at.c)
        return remote(
            teacher.at[:, aligned(block * BLK, BLK)],
            target.at[at.c, (at.pipe + 1) % NP],
            t_send.at[k], t_recv.at[k], at.column(dj, other),
        )

    def target_arrival(k):
        dj, other = COLUMN[k]
        region = target.at[at.o if other else at.c, (at.pipe - dj + NP + 1) % NP]
        return remote(region, region, t_send.at[k], t_recv.at[k], peer)

    for k in range(len(COLUMN)):
        target_copy(k).start()
    own_block = aligned((at.pipe * 2 + at.c) * BLK, BLK)
    peer_block = aligned((at.pipe * 2 + at.o) * BLK, BLK)
    own_target = pltpu.make_async_copy(
        teacher.at[:, own_block], target.at[at.c, (at.pipe + 1) % NP], local_sems.at[1]
    )
    own_target.start()
    own_rows = pltpu.make_async_copy(shallow.at[:, own_block], sbuf.at[mine], local_sems.at[2])
    own_rows.start()
    peer_rows = remote(shallow.at[:, peer_block], sbuf.at[mine], h_send.at[8], h_recv.at[8], peer)
    peer_rows.start()

    @pl.loop(0, ROWS // 32)
    def _(step):
        rows = aligned(step * 32, 32)

        def squares(k, total):
            part = shallow[rows, aligned(k * 1024, 1024)].astype(F32)
            return total + jnp.sum(part * part, axis=1, keepdims=True)

        total = lax.fori_loop(0, 8, squares, jnp.zeros((32, 1), F32))
        scale = lax.rsqrt(total / D + norm_eps)

        @pl.loop(0, NP)
        def _(k):
            here = aligned((k * 2 + at.c) * BLK, BLK)
            there = aligned((k * 2 + at.o) * BLK, BLK)
            nrows = aligned(at.c * ROWS + step * 32, 32)
            nbuf[k, nrows, :] = (shallow[rows, here].astype(F32) * scale * gain[:, here]).astype(BF16)
            pbuf[k, rows, :] = (shallow[rows, there].astype(F32) * scale * gain[:, there]).astype(BF16)

    normed_copy = remote(pbuf, nbuf.at[:, mine], n_send.at[0], n_recv.at[0], peer)
    normed_copy.start()

    group_rows = tbuf.at[at.dp, aligned(at.pipe * 32, 32)]

    def block_copy(k):
        dx, flip, other = GROUP[k]
        slot = at.slot_of("dp", dx, flip)
        if other:
            source = pbuf.at[slot, aligned(at.pipe * 32, 32)]
        else:
            source = nbuf.at[slot, aligned(at.c * ROWS + at.pipe * 32, 32)]
        return remote(source, group_rows, x_send.at[k], x_recv.at[k], at.cross(dx, flip, other))

    def block_arrival(k):
        dx, flip, other = GROUP[k]
        source = at.slot_of("dp", -dx, flip) * 2 + (at.o if other else at.c)
        region = tbuf.at[source, aligned(at.pipe * 32, 32)]
        return remote(region, region, x_send.at[k], x_recv.at[k], peer)

    for k in range(len(GROUP)):
        block_copy(k).start()
    own_block_copy = pltpu.make_async_copy(
        nbuf.at[at.slot, aligned(at.c * ROWS + at.pipe * 32, 32)], group_rows, local_sems.at[3]
    )
    own_block_copy.start()

    wg.middle()
    landed = nbuf.at[:, theirs]
    remote(landed, landed, n_send.at[0], n_recv.at[0], peer).wait_recv()
    own_block_copy.wait()
    for k in range(len(GROUP)):
        block_arrival(k).wait_recv()
    ng.begin()
    wg.late()

    @pl.when(at.swaps)
    def _():
        remote(wo, obuf.at[at.slot], swap_send.at[0], swap_recv.at[0], at.swap()).wait_recv()
        swap.wait_send()

    @pl.when(jnp.logical_not(at.swaps))
    def _():
        keep.wait()

    og.begin()
    wg.finish()

    acc[...] = jnp.zeros_like(acc)

    @pl.loop(0, NP)
    def _(k):
        acc[...] += jnp.dot(nbuf[k], wbuf[k], preferred_element_type=F32)

    sum_mine[...] = acc[theirs, :]
    sums = remote(sum_mine, sum_theirs, n_send.at[1], n_recv.at[1], peer)
    sums.start()
    ng.middle()
    sums.wait_recv()

    cos_table, sin_table = cosine[...], sine[...]
    for head in range(heads):
        cols = pl.ds(head * HD, HD)
        v = acc[mine, cols] + sum_theirs[:, cols]
        qbuf[head] = turned(v, cos_table, sin_table).astype(BF16)
    cols = pl.ds(BLK, HD)
    v = acc[mine, cols] + sum_theirs[:, cols]
    kvbuf[at.pipe] = (turned(v, cos_table, sin_table) * is_key + v * (1.0 - is_key)).astype(BF16)

    def kv_copy(dj):
        region = kvbuf.at[at.pipe]
        return remote(region, region, k_send.at[dj], k_recv.at[dj], at.column(dj, 0))

    def kv_arrival(dj):
        region = kvbuf.at[(at.pipe - dj + NP) % NP]
        return remote(region, region, k_send.at[dj], k_recv.at[dj], peer)

    for dj in range(1, NP):
        kv_copy(dj).start()
    og.middle()
    for dj in range(1, NP):
        kv_arrival(dj).wait_recv()

    score_scale = 1.0 / math.sqrt(HD)
    row_ids = lax.broadcasted_iota(jnp.int32, (ROWS, ROWS), 0)
    col_ids = lax.broadcasted_iota(jnp.int32, (ROWS, ROWS), 1)
    allowed = (seg_column[...] == seg_row[...]) & (col_ids <= row_ids)
    for head in range(heads):
        scores = nt(qbuf[head], kvbuf[2 * head]) * score_scale
        scores = jnp.where(allowed, scores, mask_fill)
        weights = jnp.exp(scores - jnp.max(scores, axis=1, keepdims=True))
        soft = weights * (1.0 / jnp.sum(weights, axis=1, keepdims=True))
        probs[head] = soft
        attended = jnp.dot(soft.astype(BF16), kvbuf[2 * head + 1], preferred_element_type=F32)
        abuf[at.pipe, mine, pl.ds(head * HD, HD)] = attended.astype(BF16)

    def forward(dx, flip):
        k = dx % NX * 2 + flip
        region = abuf.at[at.slot_of("pipe", dx, flip), mine]
        return remote(region, region, f_send.at[k], f_recv.at[k], peer)

    def multiply(dx, flip):
        k = dx % NX * 2 + flip
        source = at.slot_of("pipe", dx, flip)
        region = abuf.at[source, theirs]
        remote(region, region, f_send.at[k], f_recv.at[k], peer).wait_recv()
        acc[:, pl.ds(0, BLK)] += jnp.dot(abuf[source], obuf[source], preferred_element_type=F32)

    ag.begin()
    forward(0, 0).start()
    og.late()
    ng.late()
    ag.middle()
    forward(0, 1).start()
    forward(1, 0).start()
    forward(-1, 0).start()
    ag.late()
    forward(1, 1).start()
    forward(-1, 1).start()
    og.finish()
    acc[...] = jnp.zeros_like(acc)
    for d in ((0, 0), (0, 1), (1, 0), (-1, 0), (1, 1), (-1, 1)):
        multiply(*d)
    ag.wait("a_fp", "a_fm")
    forward(2, 0).start()
    ag.wait("az_fp", "az_fm")
    forward(2, 1).start()
    multiply(2, 0)
    multiply(2, 1)

    own_rows.wait()
    landed = sbuf.at[theirs]
    remote(landed, landed, h_send.at[8], h_recv.at[8], peer).wait_recv()
    own_target.wait()
    for k in range(len(COLUMN)):
        target_arrival(k).wait_recv()

    def wanted_rows(step):
        return target[step // 8, step % 8].astype(F32)

    lane = lax.broadcasted_iota(jnp.int32, (32, 128), 1)

    @pl.loop(0, 2 * NP)
    def _(step):
        rows = aligned(step * 32, 32)
        output = acc[rows, pl.ds(0, BLK)] + sbuf[rows, :].astype(F32)
        acc[rows, pl.ds(0, BLK)] = output
        wanted = wanted_rows(step)
        oo = jnp.sum(output * output, axis=1, keepdims=True)
        tt = jnp.sum(wanted * wanted, axis=1, keepdims=True)
        ot = jnp.sum(output * wanted, axis=1, keepdims=True)
        lanes[rows, :] = jnp.where(
            lane == 0, oo, jnp.where(lane == 1, tt, jnp.where(lane == 2, ot, 0.0))
        )

    square[...] = lanes[...].T
    stat_send[...] = square[pl.ds(0, 8), :]

    def stat(k):
        return remote(
            stat_send, stat_recv.at[k], s_send.at[k], s_recv.at[k], at.column(*COLUMN[k])
        )

    for k in range(len(COLUMN)):
        stat(k).start()
    ng.finish()
    total = stat_send[...]
    for k in range(len(COLUMN)):
        stat(k).wait_recv()
        total = total + stat_recv[k]
    square[pl.ds(0, 8), :] = total
    lanes[...] = square[...].T

    def gradient(step, lost):
        rows = aligned(step * 32, 32)
        output = acc[rows, pl.ds(0, BLK)]
        wanted = wanted_rows(step)
        norm_out = jnp.sqrt(lanes[rows, 0:1] + cosine_eps)
        norm_tar = jnp.sqrt(lanes[rows, 1:2] + cosine_eps)
        both = norm_out * norm_tar
        cosine_sim = lanes[rows, 2:3] / both
        grad = wanted * (1.0 / both) - output * (cosine_sim / (norm_out * norm_out))
        ogbuf[rows, :] = (grad * (-1.0 / 4096)).astype(BF16)
        return lost + (1.0 - cosine_sim)

    lost = lax.fori_loop(0, 2 * NP, gradient, jnp.zeros((32, 1), F32))
    lost = jnp.broadcast_to(jnp.sum(lost, axis=0, keepdims=True), (8, 128))

    grads = Reduce(at, "pipe", g_terms, ROWS, g_corner, g_near, g_cross, None, r_send, r_recv)
    outs = Reduce(at, "dp", o_terms, BLK, o_corner, o_near, o_cross, o_cross_b, e_send, e_recv)
    order = [(2, 1), (2, 0), (1, 1), (-1, 1), (1, 0), (-1, 0), (0, 1), (0, 0)]

    def part(k):
        return remote(part_send.at[k], part_recv.at[k], p_send.at[k], p_recv.at[k], peer)

    def produce(k):
        slot = at.slot_of("pipe", *order[k])
        weights = obuf[slot]
        part_send[k] = nt(ogbuf[theirs, :], weights).astype(BF16)
        part(k).start()
        g_terms[slot] = nt(ogbuf[mine, :], weights).astype(BF16)

    def settle(k):
        part(k).wait_recv()
        grads.add(*order[k], 0, ROWS, part_recv.at[k])

    produce(0)
    produce(1)
    settle(0)
    grads.x_begin(1)
    produce(2)
    settle(1)
    grads.x_begin(0)
    produce(3)
    settle(2)
    produce(4)
    settle(3)
    grads.x_pass(1)
    produce(5)
    settle(4)
    produce(6)
    settle(5)
    grads.x_pass(0)
    produce(7)
    settle(6)
    settle(7)

    @pl.loop(0, NP)
    def _(k):
        o_terms[k] = tn(abuf[k], ogbuf[...]).astype(BF16)

    outs.begin()
    grads.x_end(1)
    grads.z_first()
    grads.x_end(0)
    grads.z_first_add()

    def kv_grad_copy(dj):
        return remote(
            kv_part.at[(at.pipe + dj) % NP], kv_recv.at[dj], d_send.at[dj], d_recv.at[dj],
            at.column(dj, 0),
        )

    for head in range(heads):
        cols = pl.ds(head * HD, HD)
        soft = probs[head]
        att_grad = g_terms[at.pipe, :, cols]
        inner = nt(att_grad, kvbuf[2 * head + 1])
        centred = inner - jnp.sum(soft * inner, axis=1, keepdims=True)
        score_grad = (soft * centred * score_scale).astype(BF16)
        kv_part[2 * head] = tn(score_grad, qbuf[head]).astype(BF16)
        kv_part[2 * head + 1] = tn(soft.astype(BF16), att_grad).astype(BF16)
        grad = jnp.dot(score_grad, kvbuf[2 * head], preferred_element_type=F32)
        qgbuf[at.slot, mine, cols] = turned(grad, cos_table, -sin_table).astype(BF16)

    for dj in range(1, NP):
        kv_grad_copy(dj).start()
    outs.middle()
    total = kv_part[at.pipe].astype(F32)
    for dj in range(1, NP):
        kv_grad_copy(dj).wait_recv()
        total = total + kv_recv[dj].astype(F32)
    total = turned(total, cos_table, -sin_table) * is_key + total * (1.0 - is_key)
    qgbuf[at.slot, mine, pl.ds(BLK, HD)] = total.astype(BF16)

    def hand(dx, flip):
        k = dx % NX * 2 + flip
        region = qgbuf.at[at.slot_of("dp", dx, flip), mine]
        return remote(region, region, h_send.at[k], h_recv.at[k], peer)

    def contract(dx, flip):
        k = dx % NX * 2 + flip
        slot = at.slot_of("dp", dx, flip)
        region = qgbuf.at[slot, theirs]
        remote(region, region, h_send.at[k], h_recv.at[k], peer).wait_recv()
        for core in range(2):
            acc[...] += tn(tbuf[slot * 2 + core], qgbuf[slot, pl.ds(core * ROWS, ROWS), :])

    qg.begin()
    hand(0, 0).start()
    outs.late()
    outs.finish()

    own = at.slot
    give = remote(o_terms.at[own], go_out, swap_send.at[1], swap_recv.at[1], at.swap())
    hold = pltpu.make_async_copy(o_terms.at[own], go_out, local_sems.at[4])

    @pl.when(at.swaps)
    def _():
        give.start()

    @pl.when(jnp.logical_not(at.swaps))
    def _():
        hold.start()

    qg.middle()
    hand(1, 0).start()
    hand(-1, 0).start()
    qg.late()
    acc[...] = jnp.zeros_like(acc)
    contract(0, 0)
    tile = squares_of(lambda rows: o_terms[own, rows, :], BLK, BLK)
    qg.wait("a_fp", "a_fm")
    hand(2, 0).start()
    qg.wait("b_z0")
    hand(0, 1).start()
    contract(1, 0)
    contract(-1, 0)
    qg.wait("b_zm", "b_zp")
    hand(1, 1).start()
    hand(-1, 1).start()
    contract(2, 0)
    contract(0, 1)
    qg.wait("az_fp", "az_fm", "b_z2a", "b_z2b")
    hand(2, 1).start()
    contract(1, 1)
    contract(-1, 1)
    contract(2, 1)
    gq_out[...] = acc[...]
    stat_one[pl.ds(0, 8), :] = tile + squares_of(lambda rows: acc[rows, :], BLK, WQ)
    stat_one[pl.ds(8, 8), :] = lost

    def column_copy(k):
        return remote(
            stat_one, from_column.at[k], c_send.at[k], c_recv.at[k], at.column(*COLUMN[k])
        )

    def plane_copy(k):
        return remote(
            stat_two, from_plane.at[k], l_send.at[k], l_recv.at[k], at.near("dp", *PLANES[k])
        )

    for k in range(len(COLUMN)):
        column_copy(k).start()
    total = stat_one[...]
    for k in range(len(COLUMN)):
        column_copy(k).wait_recv()
        total = total + from_column[k]
    stat_two[...] = total
    for k in range(len(PLANES)):
        plane_copy(k).start()
    for k in range(len(PLANES)):
        plane_copy(k).wait_recv()
        total = total + from_plane[k]
    stat_out[...] = total

    @pl.when(at.swaps)
    def _():
        give.wait_recv()
        give.wait_send()

    @pl.when(jnp.logical_not(at.swaps))
    def _():
        hold.wait()

    for group in (wg, og, ng, ag, qg, grads, outs):
        group.drain()
    normed_copy.wait_send()
    peer_rows.wait_send()
    sums.wait_send()
    for k in range(len(GROUP)):
        block_copy(k).wait_send()
    for k in range(len(COLUMN)):
        target_copy(k).wait_send()
        stat(k).wait_send()
        column_copy(k).wait_send()
    for k in range(len(PLANES)):
        plane_copy(k).wait_send()
    for dj in range(1, NP):
        kv_copy(dj).wait_send()
        kv_grad_copy(dj).wait_send()
    for dx in range(NX):
        for flip in range(2):
            forward(dx, flip).wait_send()
            hand(dx, flip).wait_send()
            part(dx * 2 + flip).wait_send()


def run_step(shallow, gain, wq, wkv, wo, teacher, cosine, sine, seg_column, seg_row):
    vmem = pl.BlockSpec(memory_space=pltpu.VMEM)
    anyspace = pl.BlockSpec(memory_space=pl.ANY)

    def low(*shape):
        return pltpu.VMEM(shape, BF16)

    def wide(*shape):
        return pltpu.VMEM(shape, F32)

    def sems(*counts):
        return [pltpu.SemaphoreType.DMA((count,)) for count in counts for _ in range(2)]

    def reduce_buffers(numbers, half, width):
        return [
            low(numbers, 2, half // 2, width), low(numbers, 2, half, width), low(half, width)
        ]

    return pl.pallas_call(
        step_kernel,
        out_shape=(
            jax.ShapeDtypeStruct((BLK, WQ), F32),
            jax.ShapeDtypeStruct((BLK, BLK), BF16),
            jax.ShapeDtypeStruct((16, 128), F32),
        ),
        in_specs=[vmem, vmem, vmem, vmem, anyspace, anyspace, vmem, vmem, vmem, vmem],
        out_specs=(vmem, vmem, vmem),
        scratch_shapes=[
            low(NP, BLK, WQ), low(NP, BLK, BLK), low(NP, 2 * ROWS, BLK), low(NP, ROWS, BLK),
            low(16, ROWS, BLK), low(2, NP, ROWS // NP, BLK),
            wide(2 * ROWS, WQ), wide(ROWS, WQ), wide(ROWS, WQ),
            low(BLK // HD, ROWS, HD), low(NP, ROWS, HD), wide(BLK // HD, ROWS, ROWS),
            low(NP, 2 * ROWS, BLK), low(2 * ROWS, BLK), low(2 * ROWS, BLK),
            wide(2 * ROWS, 128), wide(128, 2 * ROWS), wide(8, 2 * ROWS), wide(15, 8, 2 * ROWS),
            low(NP, ROWS, BLK), low(NP, ROWS, BLK), low(NP, ROWS, BLK),
            *reduce_buffers(2, ROWS, BLK),
            low(NP, ROWS, HD), low(NP, ROWS, HD),
            low(NP, BLK, BLK), *reduce_buffers(3, BLK // 2, BLK), low(NX, BLK // 2, BLK),
            low(NP, 2 * ROWS, WQ),
            wide(16, 128), wide(16, 128), wide(15, 16, 128), wide(7, 16, 128),
            *sems(
                N_GATHER, N_GATHER, 2, 15, N_FIRST, 15, NP, 2, N_FIRST, NP, 15, NP,
                N_REDUCE_FIRST, NP, N_REDUCE, N_GATHER, NP + 1, 15, 7,
            ),
            pltpu.SemaphoreType.DMA((5,)),
        ],
        compiler_params=pltpu.CompilerParams(
            collective_id=0, has_side_effects=True, vmem_limit_bytes=VLIM
        ),
        name="adapter_step",
    )(shallow, gain, wq, wkv, wo, teacher, cosine, sine, seg_column, seg_row)


def rotary_tables(positions):
    half_width = HD // 2
    exponent = jnp.arange(half_width).astype(F32) * (2.0 / HD)
    inverse = jnp.power(jnp.float32(theta_base), -exponent)
    angle_table = positions.astype(F32)[:, None] * inverse[None, :]
    cosine, sine = jnp.cos(angle_table), jnp.sin(angle_table)
    return jnp.concatenate([cosine, cosine], axis=1), jnp.concatenate([-sine, sine], axis=1)


def per_device(shallow, teacher, positions, segments, in_gain, w_query, w_keyval, w_output):
    all_rows = ROWS * lax.axis_size("dp")
    param_count = D * (2 * QH * HD + 2 * KV * HD)
    cosine, sine = rotary_tables(positions)
    grad_qkv, grad_output, stats = run_step(
        shallow, in_gain[None], w_query, w_keyval, w_output, teacher, cosine, sine,
        segments[:, None], segments[None, :],
    )
    square_total = jnp.sum(stats[:8])
    inverse = 1.0 / jnp.sqrt(square_total / param_count + mean_eps)
    loss_total = stats[8, 0] / lax.axis_size("pipe") / 2
    return (
        loss_total / all_rows,
        grad_qkv[:, :BLK] * inverse,
        grad_qkv[:, BLK:] * inverse,
        grad_output.astype(F32) * inverse,
    )


def solution(mesh):
    placed = (
        P("dp", None),
        P(("dp", "pipe"), None),
        P("dp"),
        P("dp"),
        P(),
        P("dp", "pipe"),
        P("dp", "pipe"),
        P("pipe", "dp"),
    )
    return jax.shard_map(
        per_device,
        mesh=mesh,
        in_specs=placed,
        out_specs=(P(), P("dp", "pipe"), P("dp", "pipe"), P("pipe", "dp")),
        check_vma=False,
    )
```

```python
import functools
import math

import jax
import jax.numpy as jnp
from jax import lax
from jax.experimental import pallas as pl
from jax.experimental.pallas import tpu as pltpu
from jax.sharding import PartitionSpec as P

D = 8192
HD = 128
QH = 32
KV = 4
NP = 8
NX = 4
BLK = 512
ROWS = 256
WQ = 640
PARAMS = D * (2 * QH * HD + 2 * KV * HD)

theta_base = 10000.0
norm_eps = 1e-05
cosine_eps = 1e-06
mean_eps = 1e-12
mask_fill = -1e30

MESH = pl.DeviceIdType.MESH
F32 = jnp.float32
BF16 = jnp.bfloat16
VLIM = 60 * 1024 * 1024


def remote(src, dst, send_sem, recv_sem, device):
    return pltpu.make_async_remote_copy(
        src_ref=src, dst_ref=dst, send_sem=send_sem, recv_sem=recv_sem,
        device_id=device, device_id_type=MESH,
    )


class Place:
    def __init__(self):
        dp = lax.axis_index("dp")
        self.dp = dp
        self.pipe = lax.axis_index("pipe")
        self.x = dp // 4
        self.z = (dp // 2) % 2
        self.c = dp % 2
        self.o = 1 - self.c
        self.y = self.pipe // 2
        self.high = self.pipe % 2
        self.slot = dp // 2
        self.swaps = self.slot != self.pipe

    def slot_of(self, axis, dx, flip):
        along, z = (self.x, self.z) if axis == "dp" else (self.y, self.high)
        return (along + dx + NX) % NX * 2 + (1 - z if flip else z)

    def near(self, axis, dx, flip):
        slot = self.slot_of(axis, dx, flip)
        return (slot * 2 + self.c, self.pipe) if axis == "dp" else (self.dp, slot)

    def cross(self, dx, flip, other):
        return (self.slot_of("dp", dx, flip) * 2 + (self.o if other else self.c), self.pipe)

    def column(self, dj, other):
        return (self.slot * 2 + (self.o if other else self.c), (self.pipe + dj) % NP)

    def swap(self):
        return (self.pipe * 2 + self.c, self.slot)


COLUMN = [(dj, other) for other in (0, 1) for dj in range(NP) if (dj, other) != (0, 0)]
PLANES = [(dx, flip) for flip in (0, 1) for dx in range(NX) if (dx, flip) != (0, 0)]
GROUP = [
    (dx, flip, other) for other in (0, 1) for flip in (0, 1) for dx in range(NX)
    if (dx, flip, other) != (0, 0, 0)
]


def greet(at):
    barrier = pltpu.get_barrier_semaphore()
    devices = [at.cross(*d) for d in GROUP] + [at.column(*d) for d in COLUMN]
    for device in devices:
        pl.semaphore_signal(barrier, inc=1, device_id=device, device_id_type=MESH)

    @pl.when(at.swaps)
    def _():
        pl.semaphore_signal(barrier, inc=1, device_id=at.swap(), device_id_type=MESH)

    pl.semaphore_wait(barrier, len(devices) + at.swaps.astype(jnp.int32))


FIRST = {
    "a_z": (0, 0, 0, 2, "z"),
    "a_xp": (0, 0, 0, 2, "p"),
    "a_xm": (0, 0, 0, 2, "m"),
    "a_fp": (-1, 0, 0, 1, "p"),
    "a_fm": (1, 0, 1, 1, "m"),
    "az_xp": (0, 1, 0, 2, "p"),
    "az_xm": (0, 1, 0, 2, "m"),
    "az_fp": (-1, 1, 0, 1, "p"),
    "az_fm": (1, 1, 1, 1, "m"),
}
SECOND = {
    "b_xp": (0, 0, 2, 2, "p"),
    "b_xm": (0, 0, 2, 2, "m"),
    "b_fp": (-1, 0, 2, 1, "p"),
    "b_fm": (1, 0, 3, 1, "m"),
    "b_z0": (0, 0, 2, 2, "z"),
    "b_zm": (-1, 0, 2, 2, "z"),
    "b_zp": (1, 0, 2, 2, "z"),
    "b_z2a": (2, 0, 2, 1, "z"),
    "b_z2b": (2, 0, 3, 1, "z"),
}
N_GATHER = len(FIRST) + len(SECOND)
N_FIRST = len(FIRST)


class Gather:
    def __init__(self, at, axis, view, rows, send_sems, recv_sems, halves):
        self.at, self.axis, self.view = at, axis, view
        self.send_sems, self.recv_sems = send_sems, recv_sems
        self.halves = halves
        self.table = {**FIRST, **SECOND} if halves else FIRST
        self.part = rows // 4 if halves else rows // 2
        self.order = {name: k for k, name in enumerate(self.table)}

    def copy(self, name, dx, flip):
        _, _, first, parts, way = self.table[name]
        k = self.order[name]
        region = self.view(
            self.at.slot_of(self.axis, dx, flip), first * self.part, parts * self.part
        )
        device = {
            "p": self.at.near(self.axis, 1, 0),
            "m": self.at.near(self.axis, -1, 0),
            "z": self.at.near(self.axis, 0, 1),
        }[way]
        return remote(region, region, self.send_sems.at[k], self.recv_sems.at[k], device)

    def out(self, name):
        return self.copy(name, self.table[name][0], self.table[name][1])

    def start(self, *names):
        for name in names:
            self.out(name).start()

    def wait(self, *names):
        for name in names:
            dx, flip, _, _, way = self.table[name]
            dx = dx + {"p": -1, "m": 1, "z": 0}[way]
            self.copy(name, dx, 1 - flip if way == "z" else flip).wait_recv()

    def begin(self):
        self.start("a_z", "a_xp", "a_xm")
        if self.halves:
            self.start("b_xp", "b_xm")

    def middle(self):
        self.wait("a_z")
        if self.halves:
            self.start("b_z0")
        self.start("az_xp", "az_xm")
        self.wait("a_xp")
        self.start("a_fp")
        self.wait("a_xm")
        self.start("a_fm")
        if self.halves:
            self.wait("b_xp")
            self.start("b_fp", "b_zm")
            self.wait("b_xm")
            self.start("b_fm", "b_zp")

    def late(self):
        self.wait("az_xp")
        self.start("az_fp")
        self.wait("az_xm")
        self.start("az_fm")
        if self.halves:
            self.wait("b_fp")
            self.start("b_z2a")
            self.wait("b_fm")
            self.start("b_z2b")

    def finish(self):
        self.wait("a_fp", "a_fm", "az_fp", "az_fm")
        if self.halves:
            self.wait("b_z0", "b_zm", "b_zp", "b_z2a", "b_z2b")

    def drain(self):
        for name in self.table:
            self.out(name).wait_send()


N_REDUCE = 17
N_REDUCE_FIRST = 9


class Reduce:
    def __init__(self, at, axis, terms, rows, corner, near, cross, cross_b, send_sems, recv_sems):
        self.at, self.axis, self.terms = at, axis, terms
        self.corner, self.near, self.cross, self.cross_b = corner, near, cross, cross_b
        self.send_sems, self.recv_sems = send_sems, recv_sems
        self.half = rows if cross_b is None else rows // 2
        self.quarter = self.half // 2
        self.started = []

    def go(self, k, dx, flip, row, rows, landing, device):
        source = self.terms.at[self.at.slot_of(self.axis, dx, flip), pl.ds(row, rows)]
        copy = remote(
            source, landing, self.send_sems.at[k], self.recv_sems.at[k],
            self.at.near(self.axis, *device),
        )
        copy.start()
        self.started.append(copy)

    def wait(self, k, landing):
        remote(
            landing, landing, self.send_sems.at[k], self.recv_sems.at[k],
            self.at.near(self.axis, 0, 1),
        ).wait_recv()

    def add(self, dx, flip, row, rows, *landings):
        slot = self.at.slot_of(self.axis, dx, flip)

        @pl.loop(0, rows // 32)
        def _(step):
            low = pl.multiple_of(step * 32, 32)
            here = pl.ds(pl.multiple_of(row + low, 32), 32)
            total = self.terms[slot, here, :].astype(F32)
            for landing in landings:
                total = total + landing[pl.ds(low, 32), :].astype(F32)
            self.terms[slot, here, :] = total.astype(BF16)

    def where(self, n):
        return (n, 0) if n < 2 else (0, self.half)

    def x_begin(self, n):
        flip, row = self.where(n)
        quarter = self.quarter
        self.go(4 * n, 2, flip, row, quarter, self.corner.at[n, 0], (1, 0))
        self.go(4 * n + 1, 2, flip, row + quarter, quarter, self.corner.at[n, 1], (-1, 0))

    def x_pass(self, n):
        flip, row = self.where(n)
        quarter = self.quarter
        self.wait(4 * n, self.corner.at[n, 0])
        self.add(1, flip, row, quarter, self.corner.at[n, 0])
        self.go(4 * n + 2, 1, flip, row, self.half, self.near.at[n, 0], (1, 0))
        self.wait(4 * n + 1, self.corner.at[n, 1])
        self.add(-1, flip, row + quarter, quarter, self.corner.at[n, 1])
        self.go(4 * n + 3, -1, flip, row, self.half, self.near.at[n, 1], (-1, 0))

    def x_end(self, n):
        flip, row = self.where(n)
        self.wait(4 * n + 2, self.near.at[n, 0])
        self.wait(4 * n + 3, self.near.at[n, 1])
        self.add(0, flip, row, self.half, self.near.at[n, 0], self.near.at[n, 1])

    @property
    def z_sem(self):
        return 8 if self.cross_b is None else 12

    def z_first(self):
        self.go(self.z_sem, 0, 1, 0, self.half, self.cross, (0, 1))

    def z_first_add(self):
        self.wait(self.z_sem, self.cross)
        self.add(0, 0, 0, self.half, self.cross)

    def z_second(self, dx):
        self.go(13 + dx, dx, 1, self.half, self.half, self.cross_b.at[dx], (0, 1))

    def z_second_add(self, dx):
        self.wait(13 + dx, self.cross_b.at[dx])
        self.add(dx, 0, self.half, self.half, self.cross_b.at[dx])

    def begin(self):
        self.z_second(2)
        self.x_begin(1)
        self.x_begin(0)
        for dx in (1, 3, 0):
            self.z_second(dx)

    def middle(self):
        self.x_pass(1)
        self.z_second_add(2)
        self.x_begin(2)
        self.x_pass(0)
        self.z_second_add(1)
        self.z_second_add(3)
        self.x_pass(2)

    def late(self):
        self.x_end(1)
        self.z_first()
        self.x_end(0)
        self.z_second_add(0)

    def finish(self):
        self.x_end(2)
        self.z_first_add()

    def drain(self):
        for copy in self.started:
            copy.wait_send()


def nt(left, right):
    return lax.dot_general(
        left, right, (((1,), (1,)), ((), ())), preferred_element_type=F32
    )


def tn(left, right):
    return lax.dot_general(
        left, right, (((0,), (0,)), ((), ())), preferred_element_type=F32
    )


def turned(v, cosine, sine):
    half = HD // 2
    rolled = jnp.concatenate([v[:, half:], v[:, :half]], axis=1)
    return v * cosine + rolled * sine


def squares_of(read, rows, width):
    def step(k, total):
        v = read(pl.ds(pl.multiple_of(k * 32, 32), 32)).astype(F32)
        v = jnp.sum((v * v).reshape(4, 8, width), axis=0)
        for first in range(0, width, 128):
            total = total + v[:, first:first + 128]
        return total

    return lax.fori_loop(0, rows // 32, step, jnp.zeros((8, 128), F32))


def aligned(start, size):
    return pl.ds(pl.multiple_of(start, size), size)


def step_kernel(
    shallow, gain, wq, wkv, wo, teacher, cosine, sine, seg_row,
    gq_out, gkv_out, go_out, loss_out,
    wbuf, obuf, nbuf, pbuf, tbuf, target, acc, sum_mine, sum_theirs, qbuf, kvbuf, probs,
    abuf, sbuf, ogbuf, lanes, square, stat_send, stat_recv,
    part_send, part_recv, g_terms, g_corner, g_near, g_cross,
    kv_part, kv_recv, o_terms, o_corner, o_near, o_cross, o_cross_b,
    qgbuf, go_recv, stat_one, stat_two, from_column, from_plane,
    w_send, w_recv, v_send, v_recv, o_send, o_recv, n_send, n_recv, x_send, x_recv, m_send, m_recv,
    t_send, t_recv, k_send, k_recv, swap_send, swap_recv,
    a_send, a_recv, f_send, f_recv, s_send, s_recv, p_send, p_recv, r_send, r_recv,
    d_send, d_recv, e_send, e_recv, q_send, q_recv, h_send, h_recv,
    c_send, c_recv, l_send, l_recv, local_sems,
):
    at = Place()
    mine = aligned(at.c * ROWS, ROWS)
    theirs = aligned(at.o * ROWS, ROWS)
    heads = BLK // HD
    greet(at)
    peer = at.column(0, 1)
    is_key = (at.pipe % 2 == 0).astype(F32)

    def slots(buf):
        return lambda slot, row, rows: buf.at[slot, pl.ds(row, rows)]

    def slots_mine(buf):
        return lambda slot, row, rows: buf.at[slot, aligned(at.c * ROWS + row, rows)]

    def columns(buf, first, width):
        return lambda slot, row, rows: buf.at[slot, pl.ds(row, rows), pl.ds(first, width)]

    wg = Gather(at, "dp", columns(wbuf, 0, 384), BLK, w_send, w_recv, True)
    vg = Gather(at, "dp", columns(wbuf, 384, 256), BLK, v_send, v_recv, True)
    og = Gather(at, "dp", slots(obuf), BLK, o_send, o_recv, True)
    ng = Gather(
        at, "pipe", lambda slot, row, rows: tbuf.at[pl.ds(row, rows), aligned(slot * 32, 32)],
        16, m_send, m_recv, False,
    )
    ag = Gather(at, "pipe", slots_mine(abuf), ROWS, a_send, a_recv, False)
    qg = Gather(at, "dp", slots_mine(qgbuf), ROWS, q_send, q_recv, True)

    wbuf[at.slot, :, pl.ds(0, BLK)] = wq[...]
    wbuf[at.slot, :, pl.ds(BLK, HD)] = wkv[...]
    wg.begin()
    vg.begin()

    swap = remote(wo, obuf.at[at.pipe], swap_send.at[0], swap_recv.at[0], at.swap())
    keep = pltpu.make_async_copy(wo, obuf.at[at.pipe], local_sems.at[0])

    def target_copy(k):
        dj, other = COLUMN[k]
        block = (at.pipe + dj) % NP * 2 + (at.o if other else at.c)
        return remote(
            teacher.at[:, aligned(block * BLK, BLK)],
            target.at[at.c, (at.pipe + 1) % NP],
            t_send.at[k], t_recv.at[k], at.column(dj, other),
        )

    def target_arrival(k):
        dj, other = COLUMN[k]
        region = target.at[at.o if other else at.c, (at.pipe - dj + NP + 1) % NP]
        return remote(region, region, t_send.at[k], t_recv.at[k], peer)

    own_block = aligned((at.pipe * 2 + at.c) * BLK, BLK)
    peer_block = aligned((at.pipe * 2 + at.o) * BLK, BLK)
    own_target = pltpu.make_async_copy(
        teacher.at[:, own_block], target.at[at.c, (at.pipe + 1) % NP], local_sems.at[1]
    )
    own_target.start()
    own_rows = pltpu.make_async_copy(shallow.at[:, own_block], sbuf.at[mine], local_sems.at[2])
    own_rows.start()
    peer_rows = remote(shallow.at[:, peer_block], sbuf.at[mine], h_send.at[8], h_recv.at[8], peer)
    peer_rows.start()

    @pl.loop(0, ROWS // 32)
    def _(step):
        rows = aligned(step * 32, 32)

        def squares(k, total):
            part = shallow[rows, aligned(k * 1024, 1024)].astype(F32)
            return total + jnp.sum(part * part, axis=1, keepdims=True)

        total = lax.fori_loop(0, 8, squares, jnp.zeros((32, 1), F32))
        scale = lax.rsqrt(total / D + norm_eps)

        @pl.loop(0, NP)
        def _(k):
            here = aligned((k * 2 + at.c) * BLK, BLK)
            there = aligned((k * 2 + at.o) * BLK, BLK)
            nrows = aligned(at.c * ROWS + step * 32, 32)
            nbuf[k, nrows, :] = (shallow[rows, here].astype(F32) * scale * gain[:, here]).astype(BF16)
            pbuf[k, rows, :] = (shallow[rows, there].astype(F32) * scale * gain[:, there]).astype(BF16)

    normed_copy = remote(pbuf, nbuf.at[:, mine], n_send.at[0], n_recv.at[0], peer)
    normed_copy.start()

    group_rows = tbuf.at[at.dp, aligned(at.pipe * 32, 32)]

    def block_copy(k):
        dx, flip, other = GROUP[k]
        slot = at.slot_of("dp", dx, flip)
        if other:
            source = pbuf.at[slot, aligned(at.pipe * 32, 32)]
        else:
            source = nbuf.at[slot, aligned(at.c * ROWS + at.pipe * 32, 32)]
        return remote(source, group_rows, x_send.at[k], x_recv.at[k], at.cross(dx, flip, other))

    def block_arrival(k):
        dx, flip, other = GROUP[k]
        source = at.slot_of("dp", -dx, flip) * 2 + (at.o if other else at.c)
        region = tbuf.at[source, aligned(at.pipe * 32, 32)]
        return remote(region, region, x_send.at[k], x_recv.at[k], peer)

    wg.middle()
    vg.middle()

    @pl.when(at.swaps)
    def _():
        swap.start()

    @pl.when(jnp.logical_not(at.swaps))
    def _():
        keep.start()

    landed = nbuf.at[:, theirs]
    remote(landed, landed, n_send.at[0], n_recv.at[0], peer).wait_recv()
    wg.late()
    vg.late()

    @pl.when(at.swaps)
    def _():
        remote(wo, obuf.at[at.slot], swap_send.at[0], swap_recv.at[0], at.swap()).wait_recv()
        swap.wait_send()

    @pl.when(jnp.logical_not(at.swaps))
    def _():
        keep.wait()

    og.begin()

    def project(dx, flip):
        slot = at.slot_of("dp", dx, flip)
        acc[...] += jnp.dot(nbuf[slot], wbuf[slot], preferred_element_type=F32)

    acc[...] = jnp.zeros_like(acc)
    project(0, 0)
    project(1, 0)
    project(-1, 0)
    wg.wait("b_z0")
    vg.wait("b_z0")
    project(0, 1)
    wg.wait("a_fp", "a_fm")
    vg.wait("a_fp", "a_fm")
    project(2, 0)
    wg.wait("b_zm", "b_zp")
    vg.wait("b_zm", "b_zp")
    project(1, 1)
    project(-1, 1)
    wg.wait("az_fp", "az_fm", "b_z2a", "b_z2b")
    vg.wait("az_fp", "az_fm", "b_z2a", "b_z2b")
    project(2, 1)

    sum_mine[...] = acc[theirs, :]
    sums = remote(sum_mine, sum_theirs, n_send.at[1], n_recv.at[1], peer)
    sums.start()
    sums.wait_recv()

    cos_table, sin_table = cosine[...], sine[...]
    for head in range(heads):
        cols = pl.ds(head * HD, HD)
        v = acc[mine, cols] + sum_theirs[:, cols]
        qbuf[head] = turned(v, cos_table, sin_table).astype(BF16)
    cols = pl.ds(BLK, HD)
    v = acc[mine, cols] + sum_theirs[:, cols]
    kvbuf[at.pipe] = (turned(v, cos_table, sin_table) * is_key + v * (1.0 - is_key)).astype(BF16)

    def kv_copy(dj):
        region = kvbuf.at[at.pipe]
        return remote(region, region, k_send.at[dj], k_recv.at[dj], at.column(dj, 0))

    def kv_arrival(dj):
        region = kvbuf.at[(at.pipe - dj + NP) % NP]
        return remote(region, region, k_send.at[dj], k_recv.at[dj], peer)

    for dj in range(1, NP):
        kv_copy(dj).start()
    for k in range(len(COLUMN)):
        target_copy(k).start()
    og.middle()
    for dj in range(1, NP):
        kv_arrival(dj).wait_recv()

    score_scale = 1.0 / math.sqrt(HD)
    row_ids = lax.broadcasted_iota(jnp.int32, (ROWS, ROWS), 0)
    col_ids = lax.broadcasted_iota(jnp.int32, (ROWS, ROWS), 1)
    ids = jnp.broadcast_to(seg_row[...].astype(F32), (ROWS, ROWS))
    allowed = (ids.T == ids) & (col_ids <= row_ids)
    for head in range(heads):
        scores = nt(qbuf[head], kvbuf[2 * head]) * score_scale
        scores = jnp.where(allowed, scores, mask_fill)
        weights = jnp.exp(scores - jnp.max(scores, axis=1, keepdims=True))
        soft = weights * (1.0 / jnp.sum(weights, axis=1, keepdims=True))
        probs[head] = soft
        attended = jnp.dot(soft.astype(BF16), kvbuf[2 * head + 1], preferred_element_type=F32)
        abuf[at.pipe, mine, pl.ds(head * HD, HD)] = attended.astype(BF16)

    def forward(dx, flip):
        k = dx % NX * 2 + flip
        region = abuf.at[at.slot_of("pipe", dx, flip), mine]
        return remote(region, region, f_send.at[k], f_recv.at[k], peer)

    def multiply(dx, flip):
        k = dx % NX * 2 + flip
        source = at.slot_of("pipe", dx, flip)
        region = abuf.at[source, theirs]
        remote(region, region, f_send.at[k], f_recv.at[k], peer).wait_recv()
        acc[:, pl.ds(0, BLK)] += jnp.dot(abuf[source], obuf[source], preferred_element_type=F32)

    ag.begin()
    forward(0, 0).start()
    og.late()
    ag.middle()
    forward(0, 1).start()
    forward(1, 0).start()
    forward(-1, 0).start()
    ag.late()
    forward(1, 1).start()
    forward(-1, 1).start()
    og.finish()
    for k in range(len(GROUP)):
        block_copy(k).start()
    own_block_copy = pltpu.make_async_copy(
        nbuf.at[at.slot, aligned(at.c * ROWS + at.pipe * 32, 32)], group_rows, local_sems.at[3]
    )
    own_block_copy.start()
    acc[...] = jnp.zeros_like(acc)
    for d in ((0, 0), (0, 1), (1, 0), (-1, 0), (1, 1), (-1, 1)):
        multiply(*d)
    ag.wait("a_fp", "a_fm")
    forward(2, 0).start()
    ag.wait("az_fp", "az_fm")
    forward(2, 1).start()
    multiply(2, 0)
    own_block_copy.wait()
    for k in range(len(GROUP)):
        block_arrival(k).wait_recv()
    ng.begin()
    multiply(2, 1)

    own_rows.wait()
    landed = sbuf.at[theirs]
    remote(landed, landed, h_send.at[8], h_recv.at[8], peer).wait_recv()
    own_target.wait()
    for k in range(len(COLUMN)):
        target_arrival(k).wait_recv()

    def wanted_rows(step):
        return target[step // 8, step % 8].astype(F32)

    lane = lax.broadcasted_iota(jnp.int32, (32, 128), 1)

    @pl.loop(0, 2 * NP)
    def _(step):
        rows = aligned(step * 32, 32)
        output = acc[rows, pl.ds(0, BLK)] + sbuf[rows, :].astype(F32)
        acc[rows, pl.ds(0, BLK)] = output
        wanted = wanted_rows(step)
        oo = jnp.sum(output * output, axis=1, keepdims=True)
        tt = jnp.sum(wanted * wanted, axis=1, keepdims=True)
        ot = jnp.sum(output * wanted, axis=1, keepdims=True)
        lanes[rows, :] = jnp.where(
            lane == 0, oo, jnp.where(lane == 1, tt, jnp.where(lane == 2, ot, 0.0))
        )

    square[...] = lanes[...].T
    stat_send[...] = square[pl.ds(0, 8), :]

    def stat(k):
        return remote(
            stat_send, stat_recv.at[k], s_send.at[k], s_recv.at[k], at.column(*COLUMN[k])
        )

    for k in range(len(COLUMN)):
        stat(k).start()
    total = stat_send[...]
    for k in range(len(COLUMN)):
        stat(k).wait_recv()
        total = total + stat_recv[k]
    square[pl.ds(0, 8), :] = total
    lanes[...] = square[...].T

    def gradient(step, lost):
        rows = aligned(step * 32, 32)
        output = acc[rows, pl.ds(0, BLK)]
        wanted = wanted_rows(step)
        norm_out = jnp.sqrt(lanes[rows, 0:1] + cosine_eps)
        norm_tar = jnp.sqrt(lanes[rows, 1:2] + cosine_eps)
        both = norm_out * norm_tar
        cosine_sim = lanes[rows, 2:3] / both
        grad = wanted * (1.0 / both) - output * (cosine_sim / (norm_out * norm_out))
        ogbuf[rows, :] = (grad * (-1.0 / 4096)).astype(BF16)
        return lost + (1.0 - cosine_sim)

    lost = lax.fori_loop(0, 2 * NP, gradient, jnp.zeros((32, 1), F32))
    lost = jnp.broadcast_to(jnp.sum(lost, axis=0, keepdims=True), (8, 128))

    grads = Reduce(at, "pipe", g_terms, ROWS, g_corner, g_near, g_cross, None, r_send, r_recv)
    outs = Reduce(at, "dp", o_terms, BLK, o_corner, o_near, o_cross, o_cross_b, e_send, e_recv)
    order = [(2, 1), (2, 0), (1, 1), (-1, 1), (1, 0), (-1, 0), (0, 1), (0, 0)]

    def part(k):
        return remote(part_send.at[k], part_recv.at[k], p_send.at[k], p_recv.at[k], peer)

    def produce(k):
        slot = at.slot_of("pipe", *order[k])
        weights = obuf[slot]
        part_send[k] = nt(ogbuf[theirs, :], weights).astype(BF16)
        part(k).start()
        g_terms[slot] = nt(ogbuf[mine, :], weights).astype(BF16)

    def settle(k):
        part(k).wait_recv()
        grads.add(*order[k], 0, ROWS, part_recv.at[k])

    produce(0)
    produce(1)
    settle(0)
    grads.x_begin(1)
    produce(2)
    settle(1)
    grads.x_begin(0)
    produce(3)
    settle(2)
    produce(4)
    settle(3)
    grads.x_pass(1)
    produce(5)
    settle(4)
    produce(6)
    settle(5)
    grads.x_pass(0)
    produce(7)
    settle(6)
    settle(7)

    def out_term(dx, flip):
        slot = at.slot_of("dp", dx, flip)
        o_terms[slot] = tn(abuf[slot], ogbuf[...]).astype(BF16)

    out_term(2, 1)
    grads.x_end(1)
    grads.z_first()
    out_term(2, 0)
    outs.x_begin(1)
    outs.x_begin(0)
    out_term(1, 1)
    grads.x_end(0)
    out_term(3, 1)
    out_term(0, 1)
    grads.z_first_add()
    for dx in (2, 1, 3, 0):
        outs.z_second(dx)
    ng.middle()

    def kv_grad_copy(dj):
        return remote(
            kv_part.at[(at.pipe + dj) % NP], kv_recv.at[dj], d_send.at[dj], d_recv.at[dj],
            at.column(dj, 0),
        )

    for head in range(heads):
        cols = pl.ds(head * HD, HD)
        soft = probs[head]
        att_grad = g_terms[at.pipe, :, cols]
        inner = nt(att_grad, kvbuf[2 * head + 1])
        centred = inner - jnp.sum(soft * inner, axis=1, keepdims=True)
        score_grad = (soft * centred * score_scale).astype(BF16)
        kv_part[2 * head] = tn(score_grad, qbuf[head]).astype(BF16)
        kv_part[2 * head + 1] = tn(soft.astype(BF16), att_grad).astype(BF16)
        grad = jnp.dot(score_grad, kvbuf[2 * head], preferred_element_type=F32)
        qgbuf[at.slot, mine, cols] = turned(grad, cos_table, -sin_table).astype(BF16)

    for dj in range(1, NP):
        kv_grad_copy(dj).start()
    out_term(1, 0)
    out_term(-1, 0)
    out_term(0, 0)
    outs.x_pass(1)
    outs.z_second_add(2)
    outs.x_begin(2)
    total = kv_part[at.pipe].astype(F32)
    for dj in range(1, NP):
        kv_grad_copy(dj).wait_recv()
        total = total + kv_recv[dj].astype(F32)
    total = turned(total, cos_table, -sin_table) * is_key + total * (1.0 - is_key)
    qgbuf[at.slot, mine, pl.ds(BLK, HD)] = total.astype(BF16)

    def hand(dx, flip):
        k = dx % NX * 2 + flip
        region = qgbuf.at[at.slot_of("dp", dx, flip), mine]
        return remote(region, region, h_send.at[k], h_recv.at[k], peer)

    def contract(dx, flip):
        k = dx % NX * 2 + flip
        slot = at.slot_of("dp", dx, flip)
        region = qgbuf.at[slot, theirs]
        remote(region, region, h_send.at[k], h_recv.at[k], peer).wait_recv()
        acc[...] += jnp.dot(
            wbuf[slot, :, pl.ds(0, BLK)], qgbuf[slot], preferred_element_type=F32
        )

    qg.begin()
    hand(0, 0).start()
    outs.x_pass(0)
    outs.z_second_add(1)
    outs.z_second_add(3)
    outs.x_pass(2)
    ng.late()
    qg.middle()
    hand(1, 0).start()
    hand(-1, 0).start()
    outs.late()
    qg.late()
    outs.finish()

    own = at.slot
    give = remote(o_terms.at[own], go_recv, swap_send.at[1], swap_recv.at[1], at.swap())
    hold = pltpu.make_async_copy(o_terms.at[own], go_recv, local_sems.at[4])

    @pl.when(at.swaps)
    def _():
        give.start()

    @pl.when(jnp.logical_not(at.swaps))
    def _():
        hold.start()

    ng.finish()
    wg.drain()
    vg.drain()

    @pl.loop(0, NP)
    def _(k):
        for core in range(2):
            wbuf[k, :, pl.ds(core * ROWS, ROWS)] = tbuf[k * 2 + core].T

    acc[...] = jnp.zeros_like(acc)
    contract(0, 0)
    qg.wait("b_z0")
    hand(0, 1).start()
    contract(1, 0)
    contract(-1, 0)
    qg.wait("a_fp", "a_fm")
    hand(2, 0).start()
    qg.wait("b_zm", "b_zp")
    hand(1, 1).start()
    hand(-1, 1).start()
    contract(0, 1)
    contract(2, 0)
    tile = squares_of(lambda rows: o_terms[own, rows, :], BLK, BLK)
    qg.wait("az_fp", "az_fm", "b_z2a", "b_z2b")
    hand(2, 1).start()
    contract(1, 1)
    contract(-1, 1)
    contract(2, 1)
    stat_one[pl.ds(0, 8), :] = tile + squares_of(lambda rows: acc[rows, :], BLK, WQ)
    stat_one[pl.ds(8, 8), :] = lost

    def column_copy(k):
        return remote(
            stat_one, from_column.at[k], c_send.at[k], c_recv.at[k], at.column(*COLUMN[k])
        )

    def plane_copy(k):
        return remote(
            stat_two, from_plane.at[k], l_send.at[k], l_recv.at[k], at.near("dp", *PLANES[k])
        )

    for k in range(len(COLUMN)):
        column_copy(k).start()
    total = stat_one[...]
    for k in range(len(COLUMN)):
        column_copy(k).wait_recv()
        total = total + from_column[k]
    stat_two[...] = total
    for k in range(len(PLANES)):
        plane_copy(k).start()
    for k in range(len(PLANES)):
        plane_copy(k).wait_recv()
        total = total + from_plane[k]
    square_sum = jnp.sum(
        jnp.sum(total[:8], axis=0, keepdims=True), axis=1, keepdims=True
    )
    inverse = 1.0 / jnp.sqrt(square_sum * (1.0 / PARAMS) + mean_eps)
    loss_out[...] = total[8:] * (1.0 / (2 * NP * 4096))
    gq_out[...] = acc[:, pl.ds(0, BLK)] * inverse
    gkv_out[...] = acc[:, pl.ds(BLK, HD)] * inverse

    @pl.when(at.swaps)
    def _():
        give.wait_recv()
        give.wait_send()

    @pl.when(jnp.logical_not(at.swaps))
    def _():
        hold.wait()

    go_out[...] = go_recv[...].astype(F32) * inverse
    for group in (og, ng, ag, qg, grads, outs):
        group.drain()
    normed_copy.wait_send()
    peer_rows.wait_send()
    sums.wait_send()
    for k in range(len(GROUP)):
        block_copy(k).wait_send()
    for k in range(len(COLUMN)):
        target_copy(k).wait_send()
        stat(k).wait_send()
        column_copy(k).wait_send()
    for k in range(len(PLANES)):
        plane_copy(k).wait_send()
    for dj in range(1, NP):
        kv_copy(dj).wait_send()
        kv_grad_copy(dj).wait_send()
    for dx in range(NX):
        for flip in range(2):
            forward(dx, flip).wait_send()
            hand(dx, flip).wait_send()
            part(dx * 2 + flip).wait_send()


def run_step(shallow, gain, wq, wkv, wo, teacher, cosine, sine, seg_row):
    vmem = pl.BlockSpec(memory_space=pltpu.VMEM)
    anyspace = pl.BlockSpec(memory_space=pl.ANY)

    def low(*shape):
        return pltpu.VMEM(shape, BF16)

    def wide(*shape):
        return pltpu.VMEM(shape, F32)

    def sems(*counts):
        return [pltpu.SemaphoreType.DMA((count,)) for count in counts for _ in range(2)]

    def reduce_buffers(numbers, half, width):
        return [
            low(numbers, 2, half // 2, width), low(numbers, 2, half, width), low(half, width)
        ]

    return pl.pallas_call(
        step_kernel,
        out_shape=(
            jax.ShapeDtypeStruct((BLK, BLK), F32),
            jax.ShapeDtypeStruct((BLK, HD), F32),
            jax.ShapeDtypeStruct((BLK, BLK), F32),
            jax.ShapeDtypeStruct((8, 128), F32),
        ),
        in_specs=[vmem, vmem, vmem, vmem, anyspace, anyspace, vmem, vmem, vmem],
        out_specs=(vmem, vmem, vmem, vmem),
        scratch_shapes=[
            low(NP, BLK, WQ), low(NP, BLK, BLK), low(NP, 2 * ROWS, BLK), low(NP, ROWS, BLK),
            low(16, ROWS, BLK), low(2, NP, ROWS // NP, BLK),
            wide(2 * ROWS, WQ), wide(ROWS, WQ), wide(ROWS, WQ),
            low(BLK // HD, ROWS, HD), low(NP, ROWS, HD), wide(BLK // HD, ROWS, ROWS),
            low(NP, 2 * ROWS, BLK), low(2 * ROWS, BLK), low(2 * ROWS, BLK),
            wide(2 * ROWS, 128), wide(128, 2 * ROWS), wide(8, 2 * ROWS), wide(15, 8, 2 * ROWS),
            low(NP, ROWS, BLK), low(NP, ROWS, BLK), low(NP, ROWS, BLK),
            *reduce_buffers(2, ROWS, BLK),
            low(NP, ROWS, HD), low(NP, ROWS, HD),
            low(NP, BLK, BLK), *reduce_buffers(3, BLK // 2, BLK), low(NX, BLK // 2, BLK),
            low(NP, 2 * ROWS, WQ), low(BLK, BLK),
            wide(16, 128), wide(16, 128), wide(15, 16, 128), wide(7, 16, 128),
            *sems(
                N_GATHER, N_GATHER, N_GATHER, 2, 15, N_FIRST, 15, NP, 2, N_FIRST, NP, 15, NP,
                N_REDUCE_FIRST, NP, N_REDUCE, N_GATHER, NP + 1, 15, 7,
            ),
            pltpu.SemaphoreType.DMA((5,)),
        ],
        compiler_params=pltpu.CompilerParams(
            collective_id=0, has_side_effects=True, vmem_limit_bytes=VLIM
        ),
        name="adapter_step",
    )(shallow, gain, wq, wkv, wo, teacher, cosine, sine, seg_row)


def rotary_tables(positions):
    half_width = HD // 2
    exponent = jnp.arange(half_width).astype(F32) * (2.0 / HD)
    inverse = jnp.power(jnp.float32(theta_base), -exponent)
    angle_table = positions.astype(F32)[:, None] * inverse[None, :]
    cosine, sine = jnp.cos(angle_table), jnp.sin(angle_table)
    return jnp.concatenate([cosine, cosine], axis=1), jnp.concatenate([-sine, sine], axis=1)


def per_device(shallow, teacher, positions, segments, in_gain, w_query, w_keyval, w_output):
    cosine, sine = rotary_tables(positions)
    step_query, step_keyval, step_output, loss = run_step(
        shallow, in_gain[None], w_query, w_keyval, w_output, teacher, cosine, sine,
        segments[None, :],
    )
    return loss[0, 0], step_query, step_keyval, step_output


def solution(mesh):
    placed = (
        P("dp", None),
        P(("dp", "pipe"), None),
        P("dp"),
        P("dp"),
        P(),
        P("dp", "pipe"),
        P("dp", "pipe"),
        P("pipe", "dp"),
    )
    return jax.shard_map(
        per_device,
        mesh=mesh,
        in_specs=placed,
        out_specs=(P(), P("dp", "pipe"), P("dp", "pipe"), P("pipe", "dp")),
        check_vma=False,
    )
```

```python
import functools
import math

import jax
import jax.numpy as jnp
from jax import lax
from jax.experimental import pallas as pl
from jax.experimental.pallas import tpu as pltpu
from jax.sharding import PartitionSpec as P

D = 8192
HD = 128
QH = 32
KV = 4
NP = 8
NX = 4
BLK = 512
ROWS = 256
WQ = 640
PARAMS = D * (2 * QH * HD + 2 * KV * HD)

theta_base = 10000.0
norm_eps = 1e-05
cosine_eps = 1e-06
mean_eps = 1e-12
mask_fill = -1e30

MESH = pl.DeviceIdType.MESH
F32 = jnp.float32
BF16 = jnp.bfloat16
VLIM = 60 * 1024 * 1024


def remote(src, dst, send_sem, recv_sem, device):
    return pltpu.make_async_remote_copy(
        src_ref=src, dst_ref=dst, send_sem=send_sem, recv_sem=recv_sem,
        device_id=device, device_id_type=MESH,
    )


class Place:
    def __init__(self):
        dp = lax.axis_index("dp")
        self.dp = dp
        self.pipe = lax.axis_index("pipe")
        self.x = dp // 4
        self.z = (dp // 2) % 2
        self.c = dp % 2
        self.o = 1 - self.c
        self.y = self.pipe // 2
        self.high = self.pipe % 2
        self.slot = dp // 2
        self.swaps = self.slot != self.pipe

    def slot_of(self, axis, dx, flip):
        along, z = (self.x, self.z) if axis == "dp" else (self.y, self.high)
        return (along + dx + NX) % NX * 2 + (1 - z if flip else z)

    def near(self, axis, dx, flip):
        slot = self.slot_of(axis, dx, flip)
        return (slot * 2 + self.c, self.pipe) if axis == "dp" else (self.dp, slot)

    def cross(self, dx, flip, other):
        return (self.slot_of("dp", dx, flip) * 2 + (self.o if other else self.c), self.pipe)

    def column(self, dj, other):
        return (self.slot * 2 + (self.o if other else self.c), (self.pipe + dj) % NP)

    def swap(self):
        return (self.pipe * 2 + self.c, self.slot)


COLUMN = [(dj, other) for other in (0, 1) for dj in range(NP) if (dj, other) != (0, 0)]
PLANES = [(dx, flip) for flip in (0, 1) for dx in range(NX) if (dx, flip) != (0, 0)]
GROUP = [
    (dx, flip, other) for other in (0, 1) for flip in (0, 1) for dx in range(NX)
    if (dx, flip, other) != (0, 0, 0)
]


def greet(at):
    barrier = pltpu.get_barrier_semaphore()
    devices = [at.cross(*d) for d in GROUP] + [at.column(*d) for d in COLUMN]
    for device in devices:
        pl.semaphore_signal(barrier, inc=1, device_id=device, device_id_type=MESH)

    @pl.when(at.swaps)
    def _():
        pl.semaphore_signal(barrier, inc=1, device_id=at.swap(), device_id_type=MESH)

    pl.semaphore_wait(barrier, len(devices) + at.swaps.astype(jnp.int32))


FIRST = {
    "a_z": (0, 0, 0, 2, "z"),
    "a_xp": (0, 0, 0, 2, "p"),
    "a_xm": (0, 0, 0, 2, "m"),
    "a_fp": (-1, 0, 0, 1, "p"),
    "a_fm": (1, 0, 1, 1, "m"),
    "az_xp": (0, 1, 0, 2, "p"),
    "az_xm": (0, 1, 0, 2, "m"),
    "az_fp": (-1, 1, 0, 1, "p"),
    "az_fm": (1, 1, 1, 1, "m"),
}
SECOND = {
    "b_xp": (0, 0, 2, 2, "p"),
    "b_xm": (0, 0, 2, 2, "m"),
    "b_fp": (-1, 0, 2, 1, "p"),
    "b_fm": (1, 0, 3, 1, "m"),
    "b_z0": (0, 0, 2, 2, "z"),
    "b_zm": (-1, 0, 2, 2, "z"),
    "b_zp": (1, 0, 2, 2, "z"),
    "b_z2a": (2, 0, 2, 1, "z"),
    "b_z2b": (2, 0, 3, 1, "z"),
}
N_GATHER = len(FIRST) + len(SECOND)
N_FIRST = len(FIRST)


class Gather:
    def __init__(self, at, axis, view, rows, send_sems, recv_sems, halves):
        self.at, self.axis, self.view = at, axis, view
        self.send_sems, self.recv_sems = send_sems, recv_sems
        self.halves = halves
        self.table = {**FIRST, **SECOND} if halves else FIRST
        self.part = rows // 4 if halves else rows // 2
        self.order = {name: k for k, name in enumerate(self.table)}

    def copy(self, name, dx, flip):
        _, _, first, parts, way = self.table[name]
        k = self.order[name]
        region = self.view(
            self.at.slot_of(self.axis, dx, flip), first * self.part, parts * self.part
        )
        device = {
            "p": self.at.near(self.axis, 1, 0),
            "m": self.at.near(self.axis, -1, 0),
            "z": self.at.near(self.axis, 0, 1),
        }[way]
        return remote(region, region, self.send_sems.at[k], self.recv_sems.at[k], device)

    def out(self, name):
        return self.copy(name, self.table[name][0], self.table[name][1])

    def start(self, *names):
        for name in names:
            self.out(name).start()

    def wait(self, *names):
        for name in names:
            dx, flip, _, _, way = self.table[name]
            dx = dx + {"p": -1, "m": 1, "z": 0}[way]
            self.copy(name, dx, 1 - flip if way == "z" else flip).wait_recv()

    def begin(self):
        self.start("a_z", "a_xp", "a_xm")
        if self.halves:
            self.start("b_xp", "b_xm")

    def middle(self):
        self.wait("a_z")
        if self.halves:
            self.start("b_z0")
        self.start("az_xp", "az_xm")
        self.wait("a_xp")
        self.start("a_fp")
        self.wait("a_xm")
        self.start("a_fm")
        if self.halves:
            self.wait("b_xp")
            self.start("b_fp", "b_zm")
            self.wait("b_xm")
            self.start("b_fm", "b_zp")

    def late(self):
        self.wait("az_xp")
        self.start("az_fp")
        self.wait("az_xm")
        self.start("az_fm")
        if self.halves:
            self.wait("b_fp")
            self.start("b_z2a")
            self.wait("b_fm")
            self.start("b_z2b")

    def finish(self):
        self.wait("a_fp", "a_fm", "az_fp", "az_fm")
        if self.halves:
            self.wait("b_z0", "b_zm", "b_zp", "b_z2a", "b_z2b")

    def drain(self):
        for name in self.table:
            self.out(name).wait_send()


N_REDUCE = 17
N_REDUCE_FIRST = 9


class Reduce:
    def __init__(self, at, axis, terms, rows, corner, near, cross, cross_b, send_sems, recv_sems):
        self.at, self.axis, self.terms = at, axis, terms
        self.corner, self.near, self.cross, self.cross_b = corner, near, cross, cross_b
        self.send_sems, self.recv_sems = send_sems, recv_sems
        self.half = rows if cross_b is None else rows // 2
        self.quarter = self.half // 2
        self.started = []

    def go(self, k, dx, flip, row, rows, landing, device):
        source = self.terms.at[self.at.slot_of(self.axis, dx, flip), pl.ds(row, rows)]
        copy = remote(
            source, landing, self.send_sems.at[k], self.recv_sems.at[k],
            self.at.near(self.axis, *device),
        )
        copy.start()
        self.started.append(copy)

    def wait(self, k, landing):
        remote(
            landing, landing, self.send_sems.at[k], self.recv_sems.at[k],
            self.at.near(self.axis, 0, 1),
        ).wait_recv()

    def add(self, dx, flip, row, rows, *landings):
        slot = self.at.slot_of(self.axis, dx, flip)

        @pl.loop(0, rows // 32)
        def _(step):
            low = pl.multiple_of(step * 32, 32)
            here = pl.ds(pl.multiple_of(row + low, 32), 32)
            total = self.terms[slot, here, :].astype(F32)
            for landing in landings:
                total = total + landing[pl.ds(low, 32), :].astype(F32)
            self.terms[slot, here, :] = total.astype(BF16)

    def where(self, n):
        return (n, 0) if n < 2 else (0, self.half)

    def x_begin(self, n):
        flip, row = self.where(n)
        quarter = self.quarter
        self.go(4 * n, 2, flip, row, quarter, self.corner.at[n, 0], (1, 0))
        self.go(4 * n + 1, 2, flip, row + quarter, quarter, self.corner.at[n, 1], (-1, 0))

    def x_pass(self, n):
        flip, row = self.where(n)
        quarter = self.quarter
        self.wait(4 * n, self.corner.at[n, 0])
        self.add(1, flip, row, quarter, self.corner.at[n, 0])
        self.go(4 * n + 2, 1, flip, row, self.half, self.near.at[n, 0], (1, 0))
        self.wait(4 * n + 1, self.corner.at[n, 1])
        self.add(-1, flip, row + quarter, quarter, self.corner.at[n, 1])
        self.go(4 * n + 3, -1, flip, row, self.half, self.near.at[n, 1], (-1, 0))

    def x_end(self, n):
        flip, row = self.where(n)
        self.wait(4 * n + 2, self.near.at[n, 0])
        self.wait(4 * n + 3, self.near.at[n, 1])
        self.add(0, flip, row, self.half, self.near.at[n, 0], self.near.at[n, 1])

    @property
    def z_sem(self):
        return 8 if self.cross_b is None else 12

    def z_first(self):
        self.go(self.z_sem, 0, 1, 0, self.half, self.cross, (0, 1))

    def z_first_add(self):
        self.wait(self.z_sem, self.cross)
        self.add(0, 0, 0, self.half, self.cross)

    def z_second(self, dx):
        self.go(13 + dx, dx, 1, self.half, self.half, self.cross_b.at[dx], (0, 1))

    def z_second_add(self, dx):
        self.wait(13 + dx, self.cross_b.at[dx])
        self.add(dx, 0, self.half, self.half, self.cross_b.at[dx])

    def begin(self):
        self.z_second(2)
        self.x_begin(1)
        self.x_begin(0)
        for dx in (1, 3, 0):
            self.z_second(dx)

    def middle(self):
        self.x_pass(1)
        self.z_second_add(2)
        self.x_begin(2)
        self.x_pass(0)
        self.z_second_add(1)
        self.z_second_add(3)
        self.x_pass(2)

    def late(self):
        self.x_end(1)
        self.z_first()
        self.x_end(0)
        self.z_second_add(0)

    def finish(self):
        self.x_end(2)
        self.z_first_add()

    def drain(self):
        for copy in self.started:
            copy.wait_send()


def nt(left, right):
    return lax.dot_general(
        left, right, (((1,), (1,)), ((), ())), preferred_element_type=F32
    )


def tn(left, right):
    return lax.dot_general(
        left, right, (((0,), (0,)), ((), ())), preferred_element_type=F32
    )


def turned(v, cosine, sine):
    half = HD // 2
    rolled = jnp.concatenate([v[:, half:], v[:, :half]], axis=1)
    return v * cosine + rolled * sine


def squares_of(read, rows, width):
    def step(k, total):
        v = read(pl.ds(pl.multiple_of(k * 32, 32), 32)).astype(F32)
        v = jnp.sum((v * v).reshape(4, 8, width), axis=0)
        for first in range(0, width, 128):
            total = total + v[:, first:first + 128]
        return total

    return lax.fori_loop(0, rows // 32, step, jnp.zeros((8, 128), F32))


def aligned(start, size):
    return pl.ds(pl.multiple_of(start, size), size)


def step_kernel(
    shallow, gain, wq, wkv, wo, teacher, cosine, sine, seg_row,
    gq_out, gkv_out, go_out, loss_out,
    wbuf, obuf, nbuf, pbuf, tbuf, target, acc, sum_mine, sum_theirs, qbuf, kvbuf, probs,
    abuf, sbuf, ogbuf, lanes, square, stat_send, stat_recv,
    part_send, part_recv, g_terms, g_corner, g_near, g_cross,
    kv_part, kv_recv, o_terms, o_corner, o_near, o_cross, o_cross_b,
    qgbuf, go_recv, stat_one, stat_two, from_column, from_plane,
    w_send, w_recv, v_send, v_recv, o_send, o_recv, n_send, n_recv, x_send, x_recv, m_send, m_recv,
    t_send, t_recv, k_send, k_recv, swap_send, swap_recv,
    a_send, a_recv, f_send, f_recv, s_send, s_recv, p_send, p_recv, r_send, r_recv,
    d_send, d_recv, e_send, e_recv, q_send, q_recv, h_send, h_recv,
    c_send, c_recv, l_send, l_recv, local_sems,
):
    at = Place()
    mine = aligned(at.c * ROWS, ROWS)
    theirs = aligned(at.o * ROWS, ROWS)
    heads = BLK // HD
    greet(at)
    peer = at.column(0, 1)
    is_key = (at.pipe % 2 == 0).astype(F32)

    def slots(buf):
        return lambda slot, row, rows: buf.at[slot, pl.ds(row, rows)]

    def slots_mine(buf):
        return lambda slot, row, rows: buf.at[slot, aligned(at.c * ROWS + row, rows)]

    def columns(buf, first, width):
        return lambda slot, row, rows: buf.at[slot, pl.ds(row, rows), pl.ds(first, width)]

    wg = Gather(at, "dp", columns(wbuf, 0, 384), BLK, w_send, w_recv, True)
    vg = Gather(at, "dp", columns(wbuf, 384, 256), BLK, v_send, v_recv, True)
    og = Gather(at, "dp", slots(obuf), BLK, o_send, o_recv, True)
    ng = Gather(
        at, "pipe", lambda slot, row, rows: tbuf.at[pl.ds(row, rows), aligned(slot * 32, 32)],
        16, m_send, m_recv, False,
    )
    ag = Gather(at, "pipe", slots_mine(abuf), ROWS, a_send, a_recv, False)
    qg = Gather(at, "dp", slots_mine(qgbuf), ROWS, q_send, q_recv, True)

    wbuf[at.slot, :, pl.ds(0, BLK)] = wq[...]
    wbuf[at.slot, :, pl.ds(BLK, HD)] = wkv[...]
    wg.begin()
    vg.begin()

    swap = remote(wo, obuf.at[at.pipe], swap_send.at[0], swap_recv.at[0], at.swap())
    keep = pltpu.make_async_copy(wo, obuf.at[at.pipe], local_sems.at[0])

    def target_copy(k):
        dj, other = COLUMN[k]
        block = (at.pipe + dj) % NP * 2 + (at.o if other else at.c)
        return remote(
            teacher.at[:, aligned(block * BLK, BLK)],
            target.at[at.c, (at.pipe + 1) % NP],
            t_send.at[k], t_recv.at[k], at.column(dj, other),
        )

    def target_arrival(k):
        dj, other = COLUMN[k]
        region = target.at[at.o if other else at.c, (at.pipe - dj + NP + 1) % NP]
        return remote(region, region, t_send.at[k], t_recv.at[k], peer)

    own_block = aligned((at.pipe * 2 + at.c) * BLK, BLK)
    peer_block = aligned((at.pipe * 2 + at.o) * BLK, BLK)
    own_target = pltpu.make_async_copy(
        teacher.at[:, own_block], target.at[at.c, (at.pipe + 1) % NP], local_sems.at[1]
    )
    own_target.start()
    own_rows = pltpu.make_async_copy(shallow.at[:, own_block], sbuf.at[mine], local_sems.at[2])
    own_rows.start()
    peer_rows = remote(shallow.at[:, peer_block], sbuf.at[mine], h_send.at[8], h_recv.at[8], peer)
    peer_rows.start()

    @pl.loop(0, ROWS // 32)
    def _(step):
        rows = aligned(step * 32, 32)

        def squares(k, total):
            part = shallow[rows, aligned(k * 1024, 1024)].astype(F32)
            return total + jnp.sum(part * part, axis=1, keepdims=True)

        total = lax.fori_loop(0, 8, squares, jnp.zeros((32, 1), F32))
        scale = lax.rsqrt(total / D + norm_eps)

        @pl.loop(0, NP)
        def _(k):
            here = aligned((k * 2 + at.c) * BLK, BLK)
            there = aligned((k * 2 + at.o) * BLK, BLK)
            nrows = aligned(at.c * ROWS + step * 32, 32)
            nbuf[k, nrows, :] = (shallow[rows, here].astype(F32) * scale * gain[:, here]).astype(BF16)
            pbuf[k, rows, :] = (shallow[rows, there].astype(F32) * scale * gain[:, there]).astype(BF16)

    normed_copy = remote(pbuf, nbuf.at[:, mine], n_send.at[0], n_recv.at[0], peer)
    normed_copy.start()

    group_rows = tbuf.at[at.dp, aligned(at.pipe * 32, 32)]

    def block_copy(k):
        dx, flip, other = GROUP[k]
        slot = at.slot_of("dp", dx, flip)
        if other:
            source = pbuf.at[slot, aligned(at.pipe * 32, 32)]
        else:
            source = nbuf.at[slot, aligned(at.c * ROWS + at.pipe * 32, 32)]
        return remote(source, group_rows, x_send.at[k], x_recv.at[k], at.cross(dx, flip, other))

    def block_arrival(k):
        dx, flip, other = GROUP[k]
        source = at.slot_of("dp", -dx, flip) * 2 + (at.o if other else at.c)
        region = tbuf.at[source, aligned(at.pipe * 32, 32)]
        return remote(region, region, x_send.at[k], x_recv.at[k], peer)

    wg.middle()
    vg.middle()

    landed = nbuf.at[:, theirs]
    remote(landed, landed, n_send.at[0], n_recv.at[0], peer).wait_recv()
    wg.late()
    vg.late()

    @pl.when(at.swaps)
    def _():
        swap.start()

    @pl.when(jnp.logical_not(at.swaps))
    def _():
        keep.start()

    def project(dx, flip):
        slot = at.slot_of("dp", dx, flip)
        acc[...] += jnp.dot(nbuf[slot], wbuf[slot], preferred_element_type=F32)

    acc[...] = jnp.zeros_like(acc)
    project(0, 0)
    project(1, 0)
    project(-1, 0)
    wg.wait("b_z0")
    vg.wait("b_z0")
    project(0, 1)
    wg.wait("a_fp", "a_fm")
    vg.wait("a_fp", "a_fm")
    project(2, 0)
    wg.wait("b_zm", "b_zp")
    vg.wait("b_zm", "b_zp")
    project(1, 1)
    project(-1, 1)
    wg.wait("az_fp", "az_fm", "b_z2a", "b_z2b")
    vg.wait("az_fp", "az_fm", "b_z2a", "b_z2b")
    project(2, 1)

    sum_mine[...] = acc[theirs, :]
    sums = remote(sum_mine, sum_theirs, n_send.at[1], n_recv.at[1], peer)
    sums.start()
    sums.wait_recv()

    cos_table, sin_table = cosine[...], sine[...]
    for head in range(heads):
        cols = pl.ds(head * HD, HD)
        v = acc[mine, cols] + sum_theirs[:, cols]
        qbuf[head] = turned(v, cos_table, sin_table).astype(BF16)
    cols = pl.ds(BLK, HD)
    v = acc[mine, cols] + sum_theirs[:, cols]
    kvbuf[at.pipe] = (turned(v, cos_table, sin_table) * is_key + v * (1.0 - is_key)).astype(BF16)

    def kv_copy(dj):
        region = kvbuf.at[at.pipe]
        return remote(region, region, k_send.at[dj], k_recv.at[dj], at.column(dj, 0))

    def kv_arrival(dj):
        region = kvbuf.at[(at.pipe - dj + NP) % NP]
        return remote(region, region, k_send.at[dj], k_recv.at[dj], peer)

    for dj in range(1, NP):
        kv_copy(dj).start()
    for k in range(len(COLUMN)):
        target_copy(k).start()

    @pl.when(at.swaps)
    def _():
        remote(wo, obuf.at[at.slot], swap_send.at[0], swap_recv.at[0], at.swap()).wait_recv()
        swap.wait_send()

    @pl.when(jnp.logical_not(at.swaps))
    def _():
        keep.wait()

    og.begin()
    for dj in range(1, NP):
        kv_arrival(dj).wait_recv()

    score_scale = 1.0 / math.sqrt(HD)
    row_ids = lax.broadcasted_iota(jnp.int32, (ROWS, ROWS), 0)
    col_ids = lax.broadcasted_iota(jnp.int32, (ROWS, ROWS), 1)
    ids = jnp.broadcast_to(seg_row[...].astype(F32), (ROWS, ROWS))
    allowed = (ids.T == ids) & (col_ids <= row_ids)
    for head in range(heads):
        scores = nt(qbuf[head], kvbuf[2 * head]) * score_scale
        scores = jnp.where(allowed, scores, mask_fill)
        weights = jnp.exp(scores - jnp.max(scores, axis=1, keepdims=True))
        soft = weights * (1.0 / jnp.sum(weights, axis=1, keepdims=True))
        probs[head] = soft
        attended = jnp.dot(soft.astype(BF16), kvbuf[2 * head + 1], preferred_element_type=F32)
        abuf[at.pipe, mine, pl.ds(head * HD, HD)] = attended.astype(BF16)

    def forward(dx, flip):
        k = dx % NX * 2 + flip
        region = abuf.at[at.slot_of("pipe", dx, flip), mine]
        return remote(region, region, f_send.at[k], f_recv.at[k], peer)

    def multiply(dx, flip):
        k = dx % NX * 2 + flip
        source = at.slot_of("pipe", dx, flip)
        region = abuf.at[source, theirs]
        remote(region, region, f_send.at[k], f_recv.at[k], peer).wait_recv()
        acc[:, pl.ds(0, BLK)] += jnp.dot(abuf[source], obuf[source], preferred_element_type=F32)

    ag.begin()
    forward(0, 0).start()
    og.middle()
    ag.middle()
    forward(0, 1).start()
    forward(1, 0).start()
    forward(-1, 0).start()
    ag.late()
    og.late()
    for k in range(len(GROUP)):
        block_copy(k).start()
    own_block_copy = pltpu.make_async_copy(
        nbuf.at[at.slot, aligned(at.c * ROWS + at.pipe * 32, 32)], group_rows, local_sems.at[3]
    )
    own_block_copy.start()
    forward(1, 1).start()
    forward(-1, 1).start()
    og.finish()
    acc[...] = jnp.zeros_like(acc)
    for d in ((0, 0), (0, 1), (1, 0), (-1, 0), (1, 1), (-1, 1)):
        multiply(*d)
    ag.wait("a_fp", "a_fm")
    forward(2, 0).start()
    ag.wait("az_fp", "az_fm")
    forward(2, 1).start()
    multiply(2, 0)
    multiply(2, 1)

    own_rows.wait()
    landed = sbuf.at[theirs]
    remote(landed, landed, h_send.at[8], h_recv.at[8], peer).wait_recv()
    own_target.wait()
    for k in range(len(COLUMN)):
        target_arrival(k).wait_recv()

    def wanted_rows(step):
        return target[step // 8, step % 8].astype(F32)

    lane = lax.broadcasted_iota(jnp.int32, (32, 128), 1)

    @pl.loop(0, 2 * NP)
    def _(step):
        rows = aligned(step * 32, 32)
        output = acc[rows, pl.ds(0, BLK)] + sbuf[rows, :].astype(F32)
        acc[rows, pl.ds(0, BLK)] = output
        wanted = wanted_rows(step)
        oo = jnp.sum(output * output, axis=1, keepdims=True)
        tt = jnp.sum(wanted * wanted, axis=1, keepdims=True)
        ot = jnp.sum(output * wanted, axis=1, keepdims=True)
        lanes[rows, :] = jnp.where(
            lane == 0, oo, jnp.where(lane == 1, tt, jnp.where(lane == 2, ot, 0.0))
        )

    square[...] = lanes[...].T
    stat_send[...] = square[pl.ds(0, 8), :]

    def stat(k):
        return remote(
            stat_send, stat_recv.at[k], s_send.at[k], s_recv.at[k], at.column(*COLUMN[k])
        )

    for k in range(len(COLUMN)):
        stat(k).start()
    own_block_copy.wait()
    for k in range(len(GROUP)):
        block_arrival(k).wait_recv()
    ng.begin()
    total = stat_send[...]
    for k in range(len(COLUMN)):
        stat(k).wait_recv()
        total = total + stat_recv[k]
    square[pl.ds(0, 8), :] = total
    lanes[...] = square[...].T

    def gradient(step, lost):
        rows = aligned(step * 32, 32)
        output = acc[rows, pl.ds(0, BLK)]
        wanted = wanted_rows(step)
        norm_out = jnp.sqrt(lanes[rows, 0:1] + cosine_eps)
        norm_tar = jnp.sqrt(lanes[rows, 1:2] + cosine_eps)
        both = norm_out * norm_tar
        cosine_sim = lanes[rows, 2:3] / both
        grad = wanted * (1.0 / both) - output * (cosine_sim / (norm_out * norm_out))
        ogbuf[rows, :] = (grad * (-1.0 / 4096)).astype(BF16)
        return lost + (1.0 - cosine_sim)

    lost = lax.fori_loop(0, 2 * NP, gradient, jnp.zeros((32, 1), F32))
    lost = jnp.broadcast_to(jnp.sum(lost, axis=0, keepdims=True), (8, 128))

    grads = Reduce(at, "pipe", g_terms, ROWS, g_corner, g_near, g_cross, None, r_send, r_recv)
    outs = Reduce(at, "dp", o_terms, BLK, o_corner, o_near, o_cross, o_cross_b, e_send, e_recv)
    order = [(2, 1), (2, 0), (1, 1), (-1, 1), (1, 0), (-1, 0), (0, 1), (0, 0)]

    def part(k):
        return remote(part_send.at[k], part_recv.at[k], p_send.at[k], p_recv.at[k], peer)

    def produce(k):
        slot = at.slot_of("pipe", *order[k])
        weights = obuf[slot]
        part_send[k] = nt(ogbuf[theirs, :], weights).astype(BF16)
        part(k).start()
        g_terms[slot] = nt(ogbuf[mine, :], weights).astype(BF16)

    def settle(k):
        part(k).wait_recv()
        grads.add(*order[k], 0, ROWS, part_recv.at[k])

    def out_term(dx, flip):
        slot = at.slot_of("dp", dx, flip)
        o_terms[slot] = tn(abuf[slot], ogbuf[...]).astype(BF16)

    out_term(2, 1)
    outs.z_second(2)
    outs.x_begin(1)
    produce(0)
    produce(1)
    settle(0)
    grads.x_begin(1)
    out_term(2, 0)
    outs.x_begin(0)
    produce(2)
    settle(1)
    grads.x_begin(0)
    out_term(1, 1)
    outs.z_second(1)
    produce(3)
    settle(2)
    produce(4)
    settle(3)
    out_term(3, 1)
    outs.z_second(3)
    grads.x_pass(1)
    produce(5)
    settle(4)
    produce(6)
    settle(5)
    grads.x_pass(0)
    produce(7)
    settle(6)
    settle(7)
    outs.x_pass(1)
    grads.x_end(1)
    grads.z_first()
    out_term(1, 0)
    out_term(-1, 0)
    out_term(0, 1)
    grads.x_end(0)
    grads.z_first_add()
    outs.z_second(0)
    outs.x_pass(0)
    ng.middle()

    def kv_grad_copy(dj):
        return remote(
            kv_part.at[(at.pipe + dj) % NP], kv_recv.at[dj], d_send.at[dj], d_recv.at[dj],
            at.column(dj, 0),
        )

    for head in range(heads):
        cols = pl.ds(head * HD, HD)
        soft = probs[head]
        att_grad = g_terms[at.pipe, :, cols]
        inner = nt(att_grad, kvbuf[2 * head + 1])
        centred = inner - jnp.sum(soft * inner, axis=1, keepdims=True)
        score_grad = (soft * centred * score_scale).astype(BF16)
        kv_part[2 * head] = tn(score_grad, qbuf[head]).astype(BF16)
        kv_part[2 * head + 1] = tn(soft.astype(BF16), att_grad).astype(BF16)
        grad = jnp.dot(score_grad, kvbuf[2 * head], preferred_element_type=F32)
        qgbuf[at.slot, mine, cols] = turned(grad, cos_table, -sin_table).astype(BF16)

    for dj in range(1, NP):
        kv_grad_copy(dj).start()
    outs.z_second_add(2)
    outs.x_begin(2)
    out_term(0, 0)
    outs.z_second_add(1)
    outs.z_second_add(3)
    total = kv_part[at.pipe].astype(F32)
    for dj in range(1, NP):
        kv_grad_copy(dj).wait_recv()
        total = total + kv_recv[dj].astype(F32)
    total = turned(total, cos_table, -sin_table) * is_key + total * (1.0 - is_key)
    qgbuf[at.slot, mine, pl.ds(BLK, HD)] = total.astype(BF16)

    def hand(dx, flip):
        k = dx % NX * 2 + flip
        region = qgbuf.at[at.slot_of("dp", dx, flip), mine]
        return remote(region, region, h_send.at[k], h_recv.at[k], peer)

    def contract(dx, flip):
        k = dx % NX * 2 + flip
        slot = at.slot_of("dp", dx, flip)
        region = qgbuf.at[slot, theirs]
        remote(region, region, h_send.at[k], h_recv.at[k], peer).wait_recv()
        acc[...] += jnp.dot(
            wbuf[slot, :, pl.ds(0, BLK)], qgbuf[slot], preferred_element_type=F32
        )

    qg.begin()
    hand(0, 0).start()
    ng.late()
    outs.x_end(1)
    outs.z_first()
    outs.x_pass(2)
    ng.finish()
    wg.drain()
    vg.drain()

    @pl.loop(0, NP)
    def _(k):
        for core in range(2):
            wbuf[k, :, pl.ds(core * ROWS, ROWS)] = tbuf[k * 2 + core].T
    qg.middle()
    hand(1, 0).start()
    hand(-1, 0).start()
    outs.x_end(0)
    outs.z_second_add(0)
    qg.late()
    outs.finish()

    own = at.slot
    give = remote(o_terms.at[own], go_recv, swap_send.at[1], swap_recv.at[1], at.swap())
    hold = pltpu.make_async_copy(o_terms.at[own], go_recv, local_sems.at[4])

    @pl.when(at.swaps)
    def _():
        give.start()

    @pl.when(jnp.logical_not(at.swaps))
    def _():
        hold.start()

    acc[...] = jnp.zeros_like(acc)
    contract(0, 0)
    qg.wait("b_z0")
    hand(0, 1).start()
    contract(1, 0)
    contract(-1, 0)
    qg.wait("a_fp", "a_fm")
    hand(2, 0).start()
    qg.wait("b_zm", "b_zp")
    hand(1, 1).start()
    hand(-1, 1).start()
    contract(0, 1)
    contract(2, 0)
    tile = squares_of(lambda rows: o_terms[own, rows, :], BLK, BLK)
    qg.wait("az_fp", "az_fm", "b_z2a", "b_z2b")
    hand(2, 1).start()
    contract(1, 1)
    contract(-1, 1)
    contract(2, 1)
    stat_one[pl.ds(0, 8), :] = tile + squares_of(lambda rows: acc[rows, :], BLK, WQ)
    stat_one[pl.ds(8, 8), :] = lost

    def column_copy(k):
        return remote(
            stat_one, from_column.at[k], c_send.at[k], c_recv.at[k], at.column(*COLUMN[k])
        )

    def plane_copy(k):
        return remote(
            stat_two, from_plane.at[k], l_send.at[k], l_recv.at[k], at.near("dp", *PLANES[k])
        )

    for k in range(len(COLUMN)):
        column_copy(k).start()
    total = stat_one[...]
    for k in range(len(COLUMN)):
        column_copy(k).wait_recv()
        total = total + from_column[k]
    stat_two[...] = total
    for k in range(len(PLANES)):
        plane_copy(k).start()
    for k in range(len(PLANES)):
        plane_copy(k).wait_recv()
        total = total + from_plane[k]
    square_sum = jnp.sum(
        jnp.sum(total[:8], axis=0, keepdims=True), axis=1, keepdims=True
    )
    inverse = 1.0 / jnp.sqrt(square_sum * (1.0 / PARAMS) + mean_eps)
    loss_out[...] = total[8:] * (1.0 / (2 * NP * 4096))
    gq_out[...] = acc[:, pl.ds(0, BLK)] * inverse
    gkv_out[...] = acc[:, pl.ds(BLK, HD)] * inverse

    @pl.when(at.swaps)
    def _():
        give.wait_recv()
        give.wait_send()

    @pl.when(jnp.logical_not(at.swaps))
    def _():
        hold.wait()

    go_out[...] = go_recv[...].astype(F32) * inverse
    for group in (og, ng, ag, qg, grads, outs):
        group.drain()
    normed_copy.wait_send()
    peer_rows.wait_send()
    sums.wait_send()
    for k in range(len(GROUP)):
        block_copy(k).wait_send()
    for k in range(len(COLUMN)):
        target_copy(k).wait_send()
        stat(k).wait_send()
        column_copy(k).wait_send()
    for k in range(len(PLANES)):
        plane_copy(k).wait_send()
    for dj in range(1, NP):
        kv_copy(dj).wait_send()
        kv_grad_copy(dj).wait_send()
    for dx in range(NX):
        for flip in range(2):
            forward(dx, flip).wait_send()
            hand(dx, flip).wait_send()
            part(dx * 2 + flip).wait_send()


def run_step(shallow, gain, wq, wkv, wo, teacher, cosine, sine, seg_row):
    vmem = pl.BlockSpec(memory_space=pltpu.VMEM)
    anyspace = pl.BlockSpec(memory_space=pl.ANY)

    def low(*shape):
        return pltpu.VMEM(shape, BF16)

    def wide(*shape):
        return pltpu.VMEM(shape, F32)

    def sems(*counts):
        return [pltpu.SemaphoreType.DMA((count,)) for count in counts for _ in range(2)]

    def reduce_buffers(numbers, half, width):
        return [
            low(numbers, 2, half // 2, width), low(numbers, 2, half, width), low(half, width)
        ]

    return pl.pallas_call(
        step_kernel,
        out_shape=(
            jax.ShapeDtypeStruct((BLK, BLK), F32),
            jax.ShapeDtypeStruct((BLK, HD), F32),
            jax.ShapeDtypeStruct((BLK, BLK), F32),
            jax.ShapeDtypeStruct((8, 128), F32),
        ),
        in_specs=[vmem, vmem, vmem, vmem, anyspace, anyspace, vmem, vmem, vmem],
        out_specs=(vmem, vmem, vmem, vmem),
        scratch_shapes=[
            low(NP, BLK, WQ), low(NP, BLK, BLK), low(NP, 2 * ROWS, BLK), low(NP, ROWS, BLK),
            low(16, ROWS, BLK), low(2, NP, ROWS // NP, BLK),
            wide(2 * ROWS, WQ), wide(ROWS, WQ), wide(ROWS, WQ),
            low(BLK // HD, ROWS, HD), low(NP, ROWS, HD), wide(BLK // HD, ROWS, ROWS),
            low(NP, 2 * ROWS, BLK), low(2 * ROWS, BLK), low(2 * ROWS, BLK),
            wide(2 * ROWS, 128), wide(128, 2 * ROWS), wide(8, 2 * ROWS), wide(15, 8, 2 * ROWS),
            low(NP, ROWS, BLK), low(NP, ROWS, BLK), low(NP, ROWS, BLK),
            *reduce_buffers(2, ROWS, BLK),
            low(NP, ROWS, HD), low(NP, ROWS, HD),
            low(NP, BLK, BLK), *reduce_buffers(3, BLK // 2, BLK), low(NX, BLK // 2, BLK),
            low(NP, 2 * ROWS, WQ), low(BLK, BLK),
            wide(16, 128), wide(16, 128), wide(15, 16, 128), wide(7, 16, 128),
            *sems(
                N_GATHER, N_GATHER, N_GATHER, 2, 15, N_FIRST, 15, NP, 2, N_FIRST, NP, 15, NP,
                N_REDUCE_FIRST, NP, N_REDUCE, N_GATHER, NP + 1, 15, 7,
            ),
            pltpu.SemaphoreType.DMA((5,)),
        ],
        compiler_params=pltpu.CompilerParams(
            collective_id=0, has_side_effects=True, vmem_limit_bytes=VLIM
        ),
        name="adapter_step",
    )(shallow, gain, wq, wkv, wo, teacher, cosine, sine, seg_row)


def rotary_tables(positions):
    half_width = HD // 2
    exponent = jnp.arange(half_width).astype(F32) * (2.0 / HD)
    inverse = jnp.power(jnp.float32(theta_base), -exponent)
    angle_table = positions.astype(F32)[:, None] * inverse[None, :]
    cosine, sine = jnp.cos(angle_table), jnp.sin(angle_table)
    return jnp.concatenate([cosine, cosine], axis=1), jnp.concatenate([-sine, sine], axis=1)


def per_device(shallow, teacher, positions, segments, in_gain, w_query, w_keyval, w_output):
    cosine, sine = rotary_tables(positions)
    step_query, step_keyval, step_output, loss = run_step(
        shallow, in_gain[None], w_query, w_keyval, w_output, teacher, cosine, sine,
        segments[None, :],
    )
    return loss[0, 0], step_query, step_keyval, step_output


def solution(mesh):
    placed = (
        P("dp", None),
        P(("dp", "pipe"), None),
        P("dp"),
        P("dp"),
        P(),
        P("dp", "pipe"),
        P("dp", "pipe"),
        P("pipe", "dp"),
    )
    return jax.shard_map(
        per_device,
        mesh=mesh,
        in_specs=placed,
        out_specs=(P(), P("dp", "pipe"), P("dp", "pipe"), P("pipe", "dp")),
        check_vma=False,
    )
```

```python
import functools
import math

import jax
import jax.numpy as jnp
from jax import lax
from jax.experimental import pallas as pl
from jax.experimental.pallas import tpu as pltpu
from jax.sharding import PartitionSpec as P

D = 8192
HD = 128
QH = 32
KV = 4
NP = 8
NX = 4
BLK = 512
ROWS = 256
WQ = 640
PARAMS = D * (2 * QH * HD + 2 * KV * HD)

theta_base = 10000.0
norm_eps = 1e-05
cosine_eps = 1e-06
mean_eps = 1e-12
mask_fill = -1e30

MESH = pl.DeviceIdType.MESH
F32 = jnp.float32
BF16 = jnp.bfloat16
VLIM = 60 * 1024 * 1024


def remote(src, dst, send_sem, recv_sem, device):
    return pltpu.make_async_remote_copy(
        src_ref=src, dst_ref=dst, send_sem=send_sem, recv_sem=recv_sem,
        device_id=device, device_id_type=MESH,
    )


class Place:
    def __init__(self):
        dp = lax.axis_index("dp")
        self.dp = dp
        self.pipe = lax.axis_index("pipe")
        self.x = dp // 4
        self.z = (dp // 2) % 2
        self.c = dp % 2
        self.o = 1 - self.c
        self.y = self.pipe // 2
        self.high = self.pipe % 2
        self.slot = dp // 2
        self.swaps = self.slot != self.pipe

    def slot_of(self, axis, dx, flip):
        along, z = (self.x, self.z) if axis == "dp" else (self.y, self.high)
        return (along + dx + NX) % NX * 2 + (1 - z if flip else z)

    def near(self, axis, dx, flip):
        slot = self.slot_of(axis, dx, flip)
        return (slot * 2 + self.c, self.pipe) if axis == "dp" else (self.dp, slot)

    def cross(self, dx, flip, other):
        return (self.slot_of("dp", dx, flip) * 2 + (self.o if other else self.c), self.pipe)

    def column(self, dj, other):
        return (self.slot * 2 + (self.o if other else self.c), (self.pipe + dj) % NP)

    def swap(self):
        return (self.pipe * 2 + self.c, self.slot)


COLUMN = [(dj, other) for other in (0, 1) for dj in range(NP) if (dj, other) != (0, 0)]
PLANES = [(dx, flip) for flip in (0, 1) for dx in range(NX) if (dx, flip) != (0, 0)]
GROUP = [
    (dx, flip, other) for other in (0, 1) for flip in (0, 1) for dx in range(NX)
    if (dx, flip, other) != (0, 0, 0)
]


def greet(at):
    barrier = pltpu.get_barrier_semaphore()
    devices = [at.cross(*d) for d in GROUP] + [at.column(*d) for d in COLUMN]
    for device in devices:
        pl.semaphore_signal(barrier, inc=1, device_id=device, device_id_type=MESH)

    @pl.when(at.swaps)
    def _():
        pl.semaphore_signal(barrier, inc=1, device_id=at.swap(), device_id_type=MESH)

    pl.semaphore_wait(barrier, len(devices) + at.swaps.astype(jnp.int32))


FIRST = {
    "a_z": (0, 0, 0, 2, "z"),
    "a_xp": (0, 0, 0, 2, "p"),
    "a_xm": (0, 0, 0, 2, "m"),
    "a_fp": (-1, 0, 0, 1, "p"),
    "a_fm": (1, 0, 1, 1, "m"),
    "az_xp": (0, 1, 0, 2, "p"),
    "az_xm": (0, 1, 0, 2, "m"),
    "az_fp": (-1, 1, 0, 1, "p"),
    "az_fm": (1, 1, 1, 1, "m"),
}
SECOND = {
    "b_xp": (0, 0, 2, 2, "p"),
    "b_xm": (0, 0, 2, 2, "m"),
    "b_fp": (-1, 0, 2, 1, "p"),
    "b_fm": (1, 0, 3, 1, "m"),
    "b_z0": (0, 0, 2, 2, "z"),
    "b_zm": (-1, 0, 2, 2, "z"),
    "b_zp": (1, 0, 2, 2, "z"),
    "b_z2a": (2, 0, 2, 1, "z"),
    "b_z2b": (2, 0, 3, 1, "z"),
}
N_GATHER = len(FIRST) + len(SECOND)
N_FIRST = len(FIRST)


class Gather:
    def __init__(self, at, axis, view, rows, send_sems, recv_sems, halves):
        self.at, self.axis, self.view = at, axis, view
        self.send_sems, self.recv_sems = send_sems, recv_sems
        self.halves = halves
        self.table = {**FIRST, **SECOND} if halves else FIRST
        self.part = rows // 4 if halves else rows // 2
        self.order = {name: k for k, name in enumerate(self.table)}

    def copy(self, name, dx, flip):
        _, _, first, parts, way = self.table[name]
        k = self.order[name]
        region = self.view(
            self.at.slot_of(self.axis, dx, flip), first * self.part, parts * self.part
        )
        device = {
            "p": self.at.near(self.axis, 1, 0),
            "m": self.at.near(self.axis, -1, 0),
            "z": self.at.near(self.axis, 0, 1),
        }[way]
        return remote(region, region, self.send_sems.at[k], self.recv_sems.at[k], device)

    def out(self, name):
        return self.copy(name, self.table[name][0], self.table[name][1])

    def start(self, *names):
        for name in names:
            self.out(name).start()

    def wait(self, *names):
        for name in names:
            dx, flip, _, _, way = self.table[name]
            dx = dx + {"p": -1, "m": 1, "z": 0}[way]
            self.copy(name, dx, 1 - flip if way == "z" else flip).wait_recv()

    def begin(self):
        self.start("a_z", "a_xp", "a_xm")
        if self.halves:
            self.start("b_xp", "b_xm")

    def middle(self):
        self.wait("a_z")
        if self.halves:
            self.start("b_z0")
        self.start("az_xp", "az_xm")
        self.wait("a_xp")
        self.start("a_fp")
        self.wait("a_xm")
        self.start("a_fm")
        if self.halves:
            self.wait("b_xp")
            self.start("b_fp", "b_zm")
            self.wait("b_xm")
            self.start("b_fm", "b_zp")

    def late(self):
        self.wait("az_xp")
        self.start("az_fp")
        self.wait("az_xm")
        self.start("az_fm")
        if self.halves:
            self.wait("b_fp")
            self.start("b_z2a")
            self.wait("b_fm")
            self.start("b_z2b")

    def finish(self):
        self.wait("a_fp", "a_fm", "az_fp", "az_fm")
        if self.halves:
            self.wait("b_z0", "b_zm", "b_zp", "b_z2a", "b_z2b")

    def drain(self):
        for name in self.table:
            self.out(name).wait_send()


N_REDUCE = 17
N_REDUCE_FIRST = 9


class Reduce:
    def __init__(self, at, axis, terms, rows, corner, near, cross, cross_b, send_sems, recv_sems):
        self.at, self.axis, self.terms = at, axis, terms
        self.corner, self.near, self.cross, self.cross_b = corner, near, cross, cross_b
        self.send_sems, self.recv_sems = send_sems, recv_sems
        self.half = rows if cross_b is None else rows // 2
        self.quarter = self.half // 2
        self.started = []

    def go(self, k, dx, flip, row, rows, landing, device):
        source = self.terms.at[self.at.slot_of(self.axis, dx, flip), pl.ds(row, rows)]
        copy = remote(
            source, landing, self.send_sems.at[k], self.recv_sems.at[k],
            self.at.near(self.axis, *device),
        )
        copy.start()
        self.started.append(copy)

    def wait(self, k, landing):
        remote(
            landing, landing, self.send_sems.at[k], self.recv_sems.at[k],
            self.at.near(self.axis, 0, 1),
        ).wait_recv()

    def add(self, dx, flip, row, rows, *landings):
        slot = self.at.slot_of(self.axis, dx, flip)

        @pl.loop(0, rows // 32)
        def _(step):
            low = pl.multiple_of(step * 32, 32)
            here = pl.ds(pl.multiple_of(row + low, 32), 32)
            total = self.terms[slot, here, :].astype(F32)
            for landing in landings:
                total = total + landing[pl.ds(low, 32), :].astype(F32)
            self.terms[slot, here, :] = total.astype(BF16)

    def where(self, n):
        return (n, 0) if n < 2 else (0, self.half)

    def x_begin(self, n):
        flip, row = self.where(n)
        quarter = self.quarter
        self.go(4 * n, 2, flip, row, quarter, self.corner.at[n, 0], (1, 0))
        self.go(4 * n + 1, 2, flip, row + quarter, quarter, self.corner.at[n, 1], (-1, 0))

    def x_pass(self, n):
        flip, row = self.where(n)
        quarter = self.quarter
        self.wait(4 * n, self.corner.at[n, 0])
        self.add(1, flip, row, quarter, self.corner.at[n, 0])
        self.go(4 * n + 2, 1, flip, row, self.half, self.near.at[n, 0], (1, 0))
        self.wait(4 * n + 1, self.corner.at[n, 1])
        self.add(-1, flip, row + quarter, quarter, self.corner.at[n, 1])
        self.go(4 * n + 3, -1, flip, row, self.half, self.near.at[n, 1], (-1, 0))

    def x_end(self, n):
        flip, row = self.where(n)
        self.wait(4 * n + 2, self.near.at[n, 0])
        self.wait(4 * n + 3, self.near.at[n, 1])
        self.add(0, flip, row, self.half, self.near.at[n, 0], self.near.at[n, 1])

    @property
    def z_sem(self):
        return 8 if self.cross_b is None else 12

    def z_first(self):
        self.go(self.z_sem, 0, 1, 0, self.half, self.cross, (0, 1))

    def z_first_add(self):
        self.wait(self.z_sem, self.cross)
        self.add(0, 0, 0, self.half, self.cross)

    def z_second(self, dx):
        self.go(13 + dx, dx, 1, self.half, self.half, self.cross_b.at[dx], (0, 1))

    def z_second_add(self, dx):
        self.wait(13 + dx, self.cross_b.at[dx])
        self.add(dx, 0, self.half, self.half, self.cross_b.at[dx])

    def begin(self):
        self.z_second(2)
        self.x_begin(1)
        self.x_begin(0)
        for dx in (1, 3, 0):
            self.z_second(dx)

    def middle(self):
        self.x_pass(1)
        self.z_second_add(2)
        self.x_begin(2)
        self.x_pass(0)
        self.z_second_add(1)
        self.z_second_add(3)
        self.x_pass(2)

    def late(self):
        self.x_end(1)
        self.z_first()
        self.x_end(0)
        self.z_second_add(0)

    def finish(self):
        self.x_end(2)
        self.z_first_add()

    def drain(self):
        for copy in self.started:
            copy.wait_send()


def nt(left, right):
    return lax.dot_general(
        left, right, (((1,), (1,)), ((), ())), preferred_element_type=F32
    )


def tn(left, right):
    return lax.dot_general(
        left, right, (((0,), (0,)), ((), ())), preferred_element_type=F32
    )


def turned(v, cosine, sine):
    half = HD // 2
    rolled = jnp.concatenate([v[:, half:], v[:, :half]], axis=1)
    return v * cosine + rolled * sine


def squares_of(read, rows, width):
    def step(k, total):
        v = read(pl.ds(pl.multiple_of(k * 32, 32), 32)).astype(F32)
        v = jnp.sum((v * v).reshape(4, 8, width), axis=0)
        for first in range(0, width, 128):
            total = total + v[:, first:first + 128]
        return total

    return lax.fori_loop(0, rows // 32, step, jnp.zeros((8, 128), F32))


def aligned(start, size):
    return pl.ds(pl.multiple_of(start, size), size)


def step_kernel(
    shallow, gain, wq, wkv, wo, teacher, cosine, sine, seg_row,
    gq_out, gkv_out, go_out, scale_out,
    wbuf, obuf, nbuf, pbuf, tbuf, target, acc, sum_mine, sum_theirs, qbuf, kvbuf, probs,
    abuf, sbuf, ogbuf, lanes, square, stat_send, stat_recv,
    part_send, part_recv, g_terms, g_corner, g_near, g_cross,
    kv_part, kv_recv, o_terms, o_corner, o_near, o_cross, o_cross_b,
    qgbuf, go_recv, stat_one, stat_two, from_column, from_plane,
    w_send, w_recv, v_send, v_recv, o_send, o_recv, n_send, n_recv, x_send, x_recv, m_send, m_recv,
    t_send, t_recv, k_send, k_recv, swap_send, swap_recv,
    a_send, a_recv, f_send, f_recv, s_send, s_recv, p_send, p_recv, r_send, r_recv,
    d_send, d_recv, e_send, e_recv, q_send, q_recv, u_send, u_recv, h_send, h_recv,
    c_send, c_recv, l_send, l_recv, local_sems,
):
    at = Place()
    mine = aligned(at.c * ROWS, ROWS)
    theirs = aligned(at.o * ROWS, ROWS)
    heads = BLK // HD
    greet(at)
    peer = at.column(0, 1)
    is_key = (at.pipe % 2 == 0).astype(F32)

    def slots(buf):
        return lambda slot, row, rows: buf.at[slot, pl.ds(row, rows)]

    def slots_mine(buf):
        return lambda slot, row, rows: buf.at[slot, aligned(at.c * ROWS + row, rows)]

    def columns(buf, first, width):
        return lambda slot, row, rows: buf.at[slot, pl.ds(row, rows), pl.ds(first, width)]

    wg = Gather(at, "dp", columns(wbuf, 0, 384), BLK, w_send, w_recv, True)
    vg = Gather(at, "dp", columns(wbuf, 384, 256), BLK, v_send, v_recv, True)
    og = Gather(at, "dp", slots(obuf), BLK, o_send, o_recv, True)
    ng = Gather(
        at, "pipe", lambda slot, row, rows: tbuf.at[pl.ds(row, rows), aligned(slot * 32, 32)],
        16, m_send, m_recv, False,
    )
    ag = Gather(at, "pipe", slots_mine(abuf), ROWS, a_send, a_recv, False)

    def columns_mine(buf, first, width):
        return lambda slot, row, rows: buf.at[
            slot, aligned(at.c * ROWS + row, rows), pl.ds(first, width)
        ]

    qg = Gather(at, "dp", columns_mine(qgbuf, 0, BLK), ROWS, q_send, q_recv, True)
    kg = Gather(at, "dp", columns_mine(qgbuf, BLK, HD), ROWS, u_send, u_recv, True)

    wbuf[at.slot, :, pl.ds(0, BLK)] = wq[...]
    wbuf[at.slot, :, pl.ds(BLK, HD)] = wkv[...]
    wg.begin()
    vg.begin()

    swap = remote(wo, obuf.at[at.pipe], swap_send.at[0], swap_recv.at[0], at.swap())
    keep = pltpu.make_async_copy(wo, obuf.at[at.pipe], local_sems.at[0])

    def target_copy(k):
        dj, other = COLUMN[k]
        block = (at.pipe + dj) % NP * 2 + (at.o if other else at.c)
        return remote(
            teacher.at[:, aligned(block * BLK, BLK)],
            target.at[at.c, (at.pipe + 1) % NP],
            t_send.at[k], t_recv.at[k], at.column(dj, other),
        )

    def target_arrival(k):
        dj, other = COLUMN[k]
        region = target.at[at.o if other else at.c, (at.pipe - dj + NP + 1) % NP]
        return remote(region, region, t_send.at[k], t_recv.at[k], peer)

    own_block = aligned((at.pipe * 2 + at.c) * BLK, BLK)
    peer_block = aligned((at.pipe * 2 + at.o) * BLK, BLK)
    own_target = pltpu.make_async_copy(
        teacher.at[:, own_block], target.at[at.c, (at.pipe + 1) % NP], local_sems.at[1]
    )
    own_target.start()
    own_rows = pltpu.make_async_copy(shallow.at[:, own_block], sbuf.at[mine], local_sems.at[2])
    own_rows.start()
    peer_rows = remote(shallow.at[:, peer_block], sbuf.at[mine], h_send.at[8], h_recv.at[8], peer)
    peer_rows.start()

    @pl.loop(0, ROWS // 32)
    def _(step):
        rows = aligned(step * 32, 32)

        def squares(k, total):
            part = shallow[rows, aligned(k * 1024, 1024)].astype(F32)
            return total + jnp.sum(part * part, axis=1, keepdims=True)

        total = lax.fori_loop(0, 8, squares, jnp.zeros((32, 1), F32))
        scale = lax.rsqrt(total / D + norm_eps)

        @pl.loop(0, NP)
        def _(k):
            here = aligned((k * 2 + at.c) * BLK, BLK)
            there = aligned((k * 2 + at.o) * BLK, BLK)
            nrows = aligned(at.c * ROWS + step * 32, 32)
            nbuf[k, nrows, :] = (shallow[rows, here].astype(F32) * scale * gain[:, here]).astype(BF16)
            pbuf[k, rows, :] = (shallow[rows, there].astype(F32) * scale * gain[:, there]).astype(BF16)

    normed_copy = remote(pbuf, nbuf.at[:, mine], n_send.at[0], n_recv.at[0], peer)
    normed_copy.start()

    group_rows = tbuf.at[at.dp, aligned(at.pipe * 32, 32)]

    def block_copy(k):
        dx, flip, other = GROUP[k]
        slot = at.slot_of("dp", dx, flip)
        if other:
            source = pbuf.at[slot, aligned(at.pipe * 32, 32)]
        else:
            source = nbuf.at[slot, aligned(at.c * ROWS + at.pipe * 32, 32)]
        return remote(source, group_rows, x_send.at[k], x_recv.at[k], at.cross(dx, flip, other))

    def block_arrival(k):
        dx, flip, other = GROUP[k]
        source = at.slot_of("dp", -dx, flip) * 2 + (at.o if other else at.c)
        region = tbuf.at[source, aligned(at.pipe * 32, 32)]
        return remote(region, region, x_send.at[k], x_recv.at[k], peer)

    wg.middle()
    vg.middle()

    landed = nbuf.at[:, theirs]
    remote(landed, landed, n_send.at[0], n_recv.at[0], peer).wait_recv()
    wg.late()
    vg.late()

    @pl.when(at.swaps)
    def _():
        swap.start()

    @pl.when(jnp.logical_not(at.swaps))
    def _():
        keep.start()

    def project(dx, flip):
        slot = at.slot_of("dp", dx, flip)
        acc[...] += jnp.dot(nbuf[slot], wbuf[slot], preferred_element_type=F32)

    acc[...] = jnp.zeros_like(acc)
    project(0, 0)
    project(1, 0)
    project(-1, 0)
    wg.wait("b_z0")
    vg.wait("b_z0")
    project(0, 1)
    wg.wait("a_fp", "a_fm")
    vg.wait("a_fp", "a_fm")
    project(2, 0)
    wg.wait("b_zm", "b_zp")
    vg.wait("b_zm", "b_zp")
    project(1, 1)
    project(-1, 1)
    wg.wait("az_fp", "az_fm", "b_z2a", "b_z2b")
    vg.wait("az_fp", "az_fm", "b_z2a", "b_z2b")
    project(2, 1)

    sum_mine[...] = acc[theirs, :]
    sums = remote(sum_mine, sum_theirs, n_send.at[1], n_recv.at[1], peer)
    sums.start()
    sums.wait_recv()

    cos_table, sin_table = cosine[...], sine[...]
    for head in range(heads):
        cols = pl.ds(head * HD, HD)
        v = acc[mine, cols] + sum_theirs[:, cols]
        qbuf[head] = turned(v, cos_table, sin_table).astype(BF16)
    cols = pl.ds(BLK, HD)
    v = acc[mine, cols] + sum_theirs[:, cols]
    kvbuf[at.pipe] = (turned(v, cos_table, sin_table) * is_key + v * (1.0 - is_key)).astype(BF16)

    def kv_copy(dj):
        region = kvbuf.at[at.pipe]
        return remote(region, region, k_send.at[dj], k_recv.at[dj], at.column(dj, 0))

    def kv_arrival(dj):
        region = kvbuf.at[(at.pipe - dj + NP) % NP]
        return remote(region, region, k_send.at[dj], k_recv.at[dj], peer)

    for dj in range(1, NP):
        kv_copy(dj).start()
    for k in range(len(COLUMN)):
        target_copy(k).start()

    @pl.when(at.swaps)
    def _():
        remote(wo, obuf.at[at.slot], swap_send.at[0], swap_recv.at[0], at.swap()).wait_recv()
        swap.wait_send()

    @pl.when(jnp.logical_not(at.swaps))
    def _():
        keep.wait()

    og.begin()
    for dj in range(1, NP):
        kv_arrival(dj).wait_recv()

    score_scale = 1.0 / math.sqrt(HD)
    row_ids = lax.broadcasted_iota(jnp.int32, (ROWS, ROWS), 0)
    col_ids = lax.broadcasted_iota(jnp.int32, (ROWS, ROWS), 1)
    ids = jnp.broadcast_to(seg_row[...].astype(F32), (ROWS, ROWS))
    allowed = (ids.T == ids) & (col_ids <= row_ids)
    for head in range(heads):
        scores = nt(qbuf[head], kvbuf[2 * head]) * score_scale
        scores = jnp.where(allowed, scores, mask_fill)
        weights = jnp.exp(scores - jnp.max(scores, axis=1, keepdims=True))
        soft = weights * (1.0 / jnp.sum(weights, axis=1, keepdims=True))
        probs[head] = soft
        attended = jnp.dot(soft.astype(BF16), kvbuf[2 * head + 1], preferred_element_type=F32)
        abuf[at.pipe, mine, pl.ds(head * HD, HD)] = attended.astype(BF16)

    def forward(dx, flip):
        k = dx % NX * 2 + flip
        region = abuf.at[at.slot_of("pipe", dx, flip), mine]
        return remote(region, region, f_send.at[k], f_recv.at[k], peer)

    def multiply(dx, flip):
        k = dx % NX * 2 + flip
        source = at.slot_of("pipe", dx, flip)
        region = abuf.at[source, theirs]
        remote(region, region, f_send.at[k], f_recv.at[k], peer).wait_recv()
        acc[:, pl.ds(0, BLK)] += jnp.dot(abuf[source], obuf[source], preferred_element_type=F32)

    ag.begin()
    forward(0, 0).start()
    og.middle()
    ag.middle()
    forward(0, 1).start()
    forward(1, 0).start()
    forward(-1, 0).start()
    ag.late()
    og.late()
    for k in range(len(GROUP)):
        block_copy(k).start()
    own_block_copy = pltpu.make_async_copy(
        nbuf.at[at.slot, aligned(at.c * ROWS + at.pipe * 32, 32)], group_rows, local_sems.at[3]
    )
    own_block_copy.start()
    forward(1, 1).start()
    forward(-1, 1).start()
    og.finish()
    acc[...] = jnp.zeros_like(acc)
    for d in ((0, 0), (0, 1), (1, 0), (-1, 0), (1, 1), (-1, 1)):
        multiply(*d)
    ag.wait("a_fp", "a_fm")
    forward(2, 0).start()
    ag.wait("az_fp", "az_fm")
    forward(2, 1).start()
    multiply(2, 0)
    multiply(2, 1)

    own_rows.wait()
    landed = sbuf.at[theirs]
    remote(landed, landed, h_send.at[8], h_recv.at[8], peer).wait_recv()
    own_target.wait()
    for k in range(len(COLUMN)):
        target_arrival(k).wait_recv()

    def wanted_rows(step):
        return target[step // 8, step % 8].astype(F32)

    lane = lax.broadcasted_iota(jnp.int32, (32, 128), 1)

    @pl.loop(0, 2 * NP)
    def _(step):
        rows = aligned(step * 32, 32)
        output = acc[rows, pl.ds(0, BLK)] + sbuf[rows, :].astype(F32)
        acc[rows, pl.ds(0, BLK)] = output
        wanted = wanted_rows(step)
        oo = jnp.sum(output * output, axis=1, keepdims=True)
        tt = jnp.sum(wanted * wanted, axis=1, keepdims=True)
        ot = jnp.sum(output * wanted, axis=1, keepdims=True)
        lanes[rows, :] = jnp.where(
            lane == 0, oo, jnp.where(lane == 1, tt, jnp.where(lane == 2, ot, 0.0))
        )

    square[...] = lanes[...].T
    stat_send[...] = square[pl.ds(0, 8), :]

    def stat(k):
        return remote(
            stat_send, stat_recv.at[k], s_send.at[k], s_recv.at[k], at.column(*COLUMN[k])
        )

    for k in range(len(COLUMN)):
        stat(k).start()
    own_block_copy.wait()
    for k in range(len(GROUP)):
        block_arrival(k).wait_recv()
    ng.begin()
    total = stat_send[...]
    for k in range(len(COLUMN)):
        stat(k).wait_recv()
        total = total + stat_recv[k]
    square[pl.ds(0, 8), :] = total
    lanes[...] = square[...].T

    def gradient(step, lost):
        rows = aligned(step * 32, 32)
        output = acc[rows, pl.ds(0, BLK)]
        wanted = wanted_rows(step)
        norm_out = jnp.sqrt(lanes[rows, 0:1] + cosine_eps)
        norm_tar = jnp.sqrt(lanes[rows, 1:2] + cosine_eps)
        both = norm_out * norm_tar
        cosine_sim = lanes[rows, 2:3] / both
        grad = wanted * (1.0 / both) - output * (cosine_sim / (norm_out * norm_out))
        ogbuf[rows, :] = (grad * (-1.0 / 4096)).astype(BF16)
        return lost + (1.0 - cosine_sim)

    lost = lax.fori_loop(0, 2 * NP, gradient, jnp.zeros((32, 1), F32))
    lost = jnp.broadcast_to(jnp.sum(lost, axis=0, keepdims=True), (8, 128))

    grads = Reduce(at, "pipe", g_terms, ROWS, g_corner, g_near, g_cross, None, r_send, r_recv)
    outs = Reduce(at, "dp", o_terms, BLK, o_corner, o_near, o_cross, o_cross_b, e_send, e_recv)
    order = [(2, 1), (2, 0), (1, 1), (-1, 1), (1, 0), (-1, 0), (0, 1), (0, 0)]

    def part(k):
        return remote(part_send.at[k], part_recv.at[k], p_send.at[k], p_recv.at[k], peer)

    def produce(k):
        slot = at.slot_of("pipe", *order[k])
        weights = obuf[slot]
        part_send[k] = nt(ogbuf[theirs, :], weights).astype(BF16)
        part(k).start()
        g_terms[slot] = nt(ogbuf[mine, :], weights).astype(BF16)

    def settle(k):
        part(k).wait_recv()
        grads.add(*order[k], 0, ROWS, part_recv.at[k])

    def out_term(dx, flip):
        slot = at.slot_of("dp", dx, flip)
        o_terms[slot] = tn(abuf[slot], ogbuf[...]).astype(BF16)

    out_term(2, 1)
    outs.z_second(2)
    outs.x_begin(1)
    produce(0)
    produce(1)
    settle(0)
    grads.x_begin(1)
    out_term(2, 0)
    outs.x_begin(0)
    produce(2)
    settle(1)
    grads.x_begin(0)
    out_term(1, 1)
    outs.z_second(1)
    produce(3)
    settle(2)
    produce(4)
    settle(3)
    out_term(3, 1)
    outs.z_second(3)
    grads.x_pass(1)
    produce(5)
    settle(4)
    produce(6)
    settle(5)
    grads.x_pass(0)
    produce(7)
    settle(6)
    settle(7)
    outs.x_pass(1)
    grads.x_end(1)
    grads.z_first()
    out_term(1, 0)
    out_term(-1, 0)
    out_term(0, 1)
    grads.x_end(0)
    grads.z_first_add()
    outs.z_second(0)
    outs.x_pass(0)
    ng.middle()

    def kv_grad_copy(dj):
        return remote(
            kv_part.at[(at.pipe + dj) % NP], kv_recv.at[dj], d_send.at[dj], d_recv.at[dj],
            at.column(dj, 0),
        )

    for head in range(heads):
        cols = pl.ds(head * HD, HD)
        soft = probs[head]
        att_grad = g_terms[at.pipe, :, cols]
        inner = nt(att_grad, kvbuf[2 * head + 1])
        centred = inner - jnp.sum(soft * inner, axis=1, keepdims=True)
        score_grad = (soft * centred * score_scale).astype(BF16)
        kv_part[2 * head] = tn(score_grad, qbuf[head]).astype(BF16)
        kv_part[2 * head + 1] = tn(soft.astype(BF16), att_grad).astype(BF16)
        grad = jnp.dot(score_grad, kvbuf[2 * head], preferred_element_type=F32)
        qgbuf[at.slot, mine, cols] = turned(grad, cos_table, -sin_table).astype(BF16)

    for dj in range(1, NP):
        kv_grad_copy(dj).start()
    qg.begin()
    outs.z_second_add(2)
    outs.x_begin(2)
    out_term(0, 0)
    outs.z_second_add(1)
    outs.z_second_add(3)
    total = kv_part[at.pipe].astype(F32)
    for dj in range(1, NP):
        kv_grad_copy(dj).wait_recv()
        total = total + kv_recv[dj].astype(F32)
    total = turned(total, cos_table, -sin_table) * is_key + total * (1.0 - is_key)
    qgbuf[at.slot, mine, pl.ds(BLK, HD)] = total.astype(BF16)

    def hand(dx, flip):
        k = dx % NX * 2 + flip
        region = qgbuf.at[at.slot_of("dp", dx, flip), mine]
        return remote(region, region, h_send.at[k], h_recv.at[k], peer)

    def contract(dx, flip):
        k = dx % NX * 2 + flip
        slot = at.slot_of("dp", dx, flip)
        region = qgbuf.at[slot, theirs]
        remote(region, region, h_send.at[k], h_recv.at[k], peer).wait_recv()
        acc[...] += jnp.dot(
            wbuf[slot, :, pl.ds(0, BLK)], qgbuf[slot], preferred_element_type=F32
        )

    kg.begin()
    hand(0, 0).start()
    ng.late()
    outs.x_end(1)
    outs.z_first()
    outs.x_pass(2)
    ng.finish()
    wg.drain()
    vg.drain()

    @pl.loop(0, NP)
    def _(k):
        for core in range(2):
            wbuf[k, :, pl.ds(core * ROWS, ROWS)] = tbuf[k * 2 + core].T
    qg.middle()
    kg.middle()
    hand(1, 0).start()
    hand(-1, 0).start()
    outs.x_end(0)
    outs.z_second_add(0)
    qg.late()
    kg.late()
    outs.finish()

    own = at.slot
    give = remote(o_terms.at[own], go_recv, swap_send.at[1], swap_recv.at[1], at.swap())
    hold = pltpu.make_async_copy(o_terms.at[own], go_recv, local_sems.at[4])

    @pl.when(at.swaps)
    def _():
        give.start()

    @pl.when(jnp.logical_not(at.swaps))
    def _():
        hold.start()

    acc[...] = jnp.zeros_like(acc)
    contract(0, 0)
    qg.wait("b_z0")
    kg.wait("b_z0")
    hand(0, 1).start()
    contract(1, 0)
    contract(-1, 0)
    qg.wait("a_fp", "a_fm")
    kg.wait("a_fp", "a_fm")
    hand(2, 0).start()
    qg.wait("b_zm", "b_zp")
    kg.wait("b_zm", "b_zp")
    hand(1, 1).start()
    hand(-1, 1).start()
    contract(0, 1)
    contract(2, 0)
    tile = squares_of(lambda rows: o_terms[own, rows, :], BLK, BLK)
    qg.wait("az_fp", "az_fm", "b_z2a", "b_z2b")
    kg.wait("az_fp", "az_fm", "b_z2a", "b_z2b")
    hand(2, 1).start()
    contract(1, 1)
    contract(-1, 1)
    contract(2, 1)
    stat_one[pl.ds(0, 8), :] = tile + squares_of(lambda rows: acc[rows, :], BLK, WQ)
    stat_one[pl.ds(8, 8), :] = lost

    def column_copy(k):
        return remote(
            stat_one, from_column.at[k], c_send.at[k], c_recv.at[k], at.column(*COLUMN[k])
        )

    def plane_copy(k):
        return remote(
            stat_two, from_plane.at[k], l_send.at[k], l_recv.at[k], at.near("dp", *PLANES[k])
        )

    for k in range(len(COLUMN)):
        column_copy(k).start()
    gq_out[...] = acc[:, pl.ds(0, BLK)].astype(BF16)
    gkv_out[...] = acc[:, pl.ds(BLK, HD)].astype(BF16)
    total = stat_one[...]
    for k in range(len(COLUMN)):
        column_copy(k).wait_recv()
        total = total + from_column[k]
    stat_two[...] = total
    for k in range(len(PLANES)):
        plane_copy(k).start()
    for k in range(len(PLANES)):
        plane_copy(k).wait_recv()
        total = total + from_plane[k]
    square_sum = jnp.sum(
        jnp.sum(total[:8], axis=0, keepdims=True), axis=1, keepdims=True
    )
    inverse = 1.0 / jnp.sqrt(square_sum * (1.0 / PARAMS) + mean_eps)
    scale_out[pl.ds(0, 8), :] = jnp.broadcast_to(inverse, (8, 128))
    scale_out[pl.ds(8, 8), :] = total[8:] * (1.0 / (2 * NP * 4096))

    @pl.when(at.swaps)
    def _():
        give.wait_recv()
        give.wait_send()

    @pl.when(jnp.logical_not(at.swaps))
    def _():
        hold.wait()

    go_out[...] = go_recv[...]
    for group in (og, ng, ag, qg, kg, grads, outs):
        group.drain()
    normed_copy.wait_send()
    peer_rows.wait_send()
    sums.wait_send()
    for k in range(len(GROUP)):
        block_copy(k).wait_send()
    for k in range(len(COLUMN)):
        target_copy(k).wait_send()
        stat(k).wait_send()
        column_copy(k).wait_send()
    for k in range(len(PLANES)):
        plane_copy(k).wait_send()
    for dj in range(1, NP):
        kv_copy(dj).wait_send()
        kv_grad_copy(dj).wait_send()
    for dx in range(NX):
        for flip in range(2):
            forward(dx, flip).wait_send()
            hand(dx, flip).wait_send()
            part(dx * 2 + flip).wait_send()


def run_step(shallow, gain, wq, wkv, wo, teacher, cosine, sine, seg_row):
    vmem = pl.BlockSpec(memory_space=pltpu.VMEM)
    anyspace = pl.BlockSpec(memory_space=pl.ANY)

    def low(*shape):
        return pltpu.VMEM(shape, BF16)

    def wide(*shape):
        return pltpu.VMEM(shape, F32)

    def sems(*counts):
        return [pltpu.SemaphoreType.DMA((count,)) for count in counts for _ in range(2)]

    def reduce_buffers(numbers, half, width):
        return [
            low(numbers, 2, half // 2, width), low(numbers, 2, half, width), low(half, width)
        ]

    return pl.pallas_call(
        step_kernel,
        out_shape=(
            jax.ShapeDtypeStruct((BLK, BLK), BF16),
            jax.ShapeDtypeStruct((BLK, HD), BF16),
            jax.ShapeDtypeStruct((BLK, BLK), BF16),
            jax.ShapeDtypeStruct((16, 128), F32),
        ),
        in_specs=[vmem, vmem, vmem, vmem, anyspace, anyspace, vmem, vmem, vmem],
        out_specs=(vmem, vmem, vmem, vmem),
        scratch_shapes=[
            low(NP, BLK, WQ), low(NP, BLK, BLK), low(NP, 2 * ROWS, BLK), low(NP, ROWS, BLK),
            low(16, ROWS, BLK), low(2, NP, ROWS // NP, BLK),
            wide(2 * ROWS, WQ), wide(ROWS, WQ), wide(ROWS, WQ),
            low(BLK // HD, ROWS, HD), low(NP, ROWS, HD), wide(BLK // HD, ROWS, ROWS),
            low(NP, 2 * ROWS, BLK), low(2 * ROWS, BLK), low(2 * ROWS, BLK),
            wide(2 * ROWS, 128), wide(128, 2 * ROWS), wide(8, 2 * ROWS), wide(15, 8, 2 * ROWS),
            low(NP, ROWS, BLK), low(NP, ROWS, BLK), low(NP, ROWS, BLK),
            *reduce_buffers(2, ROWS, BLK),
            low(NP, ROWS, HD), low(NP, ROWS, HD),
            low(NP, BLK, BLK), *reduce_buffers(3, BLK // 2, BLK), low(NX, BLK // 2, BLK),
            low(NP, 2 * ROWS, WQ), low(BLK, BLK),
            wide(16, 128), wide(16, 128), wide(15, 16, 128), wide(7, 16, 128),
            *sems(
                N_GATHER, N_GATHER, N_GATHER, 2, 15, N_FIRST, 15, NP, 2, N_FIRST, NP, 15, NP,
                N_REDUCE_FIRST, NP, N_REDUCE, N_GATHER, N_GATHER, NP + 1, 15, 7,
            ),
            pltpu.SemaphoreType.DMA((5,)),
        ],
        compiler_params=pltpu.CompilerParams(
            collective_id=0, has_side_effects=True, vmem_limit_bytes=VLIM
        ),
        name="adapter_step",
    )(shallow, gain, wq, wkv, wo, teacher, cosine, sine, seg_row)


def rotary_tables(positions):
    half_width = HD // 2
    exponent = jnp.arange(half_width).astype(F32) * (2.0 / HD)
    inverse = jnp.power(jnp.float32(theta_base), -exponent)
    angle_table = positions.astype(F32)[:, None] * inverse[None, :]
    cosine, sine = jnp.cos(angle_table), jnp.sin(angle_table)
    return jnp.concatenate([cosine, cosine], axis=1), jnp.concatenate([-sine, sine], axis=1)


def per_device(shallow, teacher, positions, segments, in_gain, w_query, w_keyval, w_output):
    cosine, sine = rotary_tables(positions)
    query, keyval, output, scale = run_step(
        shallow, in_gain[None], w_query, w_keyval, w_output, teacher, cosine, sine,
        segments[None, :],
    )
    inverse = scale[:1, :1]
    return (
        scale[8, 0],
        query.astype(F32) * inverse,
        keyval.astype(F32) * inverse,
        output.astype(F32) * inverse,
    )


def solution(mesh):
    placed = (
        P("dp", None),
        P(("dp", "pipe"), None),
        P("dp"),
        P("dp"),
        P(),
        P("dp", "pipe"),
        P("dp", "pipe"),
        P("pipe", "dp"),
    )
    return jax.shard_map(
        per_device,
        mesh=mesh,
        in_specs=placed,
        out_specs=(P(), P("dp", "pipe"), P("dp", "pipe"), P("pipe", "dp")),
        check_vma=False,
    )
```

```python
import functools
import math

import jax
import jax.numpy as jnp
from jax import lax
from jax.experimental import pallas as pl
from jax.experimental.pallas import tpu as pltpu
from jax.sharding import PartitionSpec as P

D = 8192
HD = 128
QH = 32
KV = 4
NP = 8
NX = 4
BLK = 512
ROWS = 256
WQ = 640
PARAMS = D * (2 * QH * HD + 2 * KV * HD)

theta_base = 10000.0
norm_eps = 1e-05
cosine_eps = 1e-06
mean_eps = 1e-12
mask_fill = -1e30

MESH = pl.DeviceIdType.MESH
F32 = jnp.float32
BF16 = jnp.bfloat16
VLIM = 60 * 1024 * 1024


def remote(src, dst, send_sem, recv_sem, device):
    return pltpu.make_async_remote_copy(
        src_ref=src, dst_ref=dst, send_sem=send_sem, recv_sem=recv_sem,
        device_id=device, device_id_type=MESH,
    )


class Place:
    def __init__(self):
        dp = lax.axis_index("dp")
        self.dp = dp
        self.pipe = lax.axis_index("pipe")
        self.x = dp // 4
        self.z = (dp // 2) % 2
        self.c = dp % 2
        self.o = 1 - self.c
        self.y = self.pipe // 2
        self.high = self.pipe % 2
        self.slot = dp // 2
        self.swaps = self.slot != self.pipe

    def slot_of(self, axis, dx, flip):
        along, z = (self.x, self.z) if axis == "dp" else (self.y, self.high)
        return (along + dx + NX) % NX * 2 + (1 - z if flip else z)

    def near(self, axis, dx, flip):
        slot = self.slot_of(axis, dx, flip)
        return (slot * 2 + self.c, self.pipe) if axis == "dp" else (self.dp, slot)

    def cross(self, dx, flip, other):
        return (self.slot_of("dp", dx, flip) * 2 + (self.o if other else self.c), self.pipe)

    def column(self, dj, other):
        return (self.slot * 2 + (self.o if other else self.c), (self.pipe + dj) % NP)

    def swap(self):
        return (self.pipe * 2 + self.c, self.slot)


COLUMN = [(dj, other) for other in (0, 1) for dj in range(NP) if (dj, other) != (0, 0)]
PLANES = [(dx, flip) for flip in (0, 1) for dx in range(NX) if (dx, flip) != (0, 0)]
GROUP = [
    (dx, flip, other) for other in (0, 1) for flip in (0, 1) for dx in range(NX)
    if (dx, flip, other) != (0, 0, 0)
]


def greet(at):
    barrier = pltpu.get_barrier_semaphore()
    devices = [at.cross(*d) for d in GROUP] + [at.column(*d) for d in COLUMN]
    for device in devices:
        pl.semaphore_signal(barrier, inc=1, device_id=device, device_id_type=MESH)

    @pl.when(at.swaps)
    def _():
        pl.semaphore_signal(barrier, inc=1, device_id=at.swap(), device_id_type=MESH)

    pl.semaphore_wait(barrier, len(devices) + at.swaps.astype(jnp.int32))


FIRST = {
    "a_z": (0, 0, 0, 2, "z"),
    "a_xp": (0, 0, 0, 2, "p"),
    "a_xm": (0, 0, 0, 2, "m"),
    "a_fp": (-1, 0, 0, 1, "p"),
    "a_fm": (1, 0, 1, 1, "m"),
    "az_xp": (0, 1, 0, 2, "p"),
    "az_xm": (0, 1, 0, 2, "m"),
    "az_fp": (-1, 1, 0, 1, "p"),
    "az_fm": (1, 1, 1, 1, "m"),
}
SECOND = {
    "b_xp": (0, 0, 2, 2, "p"),
    "b_xm": (0, 0, 2, 2, "m"),
    "b_fp": (-1, 0, 2, 1, "p"),
    "b_fm": (1, 0, 3, 1, "m"),
    "b_z0": (0, 0, 2, 2, "z"),
    "b_zm": (-1, 0, 2, 2, "z"),
    "b_zp": (1, 0, 2, 2, "z"),
    "b_z2a": (2, 0, 2, 1, "z"),
    "b_z2b": (2, 0, 3, 1, "z"),
}
N_GATHER = len(FIRST) + len(SECOND)
N_FIRST = len(FIRST)


class Gather:
    def __init__(self, at, axis, view, rows, send_sems, recv_sems, halves):
        self.at, self.axis, self.view = at, axis, view
        self.send_sems, self.recv_sems = send_sems, recv_sems
        self.halves = halves
        self.table = {**FIRST, **SECOND} if halves else FIRST
        self.part = rows // 4 if halves else rows // 2
        self.order = {name: k for k, name in enumerate(self.table)}

    def copy(self, name, dx, flip):
        _, _, first, parts, way = self.table[name]
        k = self.order[name]
        region = self.view(
            self.at.slot_of(self.axis, dx, flip), first * self.part, parts * self.part
        )
        device = {
            "p": self.at.near(self.axis, 1, 0),
            "m": self.at.near(self.axis, -1, 0),
            "z": self.at.near(self.axis, 0, 1),
        }[way]
        return remote(region, region, self.send_sems.at[k], self.recv_sems.at[k], device)

    def out(self, name):
        return self.copy(name, self.table[name][0], self.table[name][1])

    def start(self, *names):
        for name in names:
            self.out(name).start()

    def wait(self, *names):
        for name in names:
            dx, flip, _, _, way = self.table[name]
            dx = dx + {"p": -1, "m": 1, "z": 0}[way]
            self.copy(name, dx, 1 - flip if way == "z" else flip).wait_recv()

    def begin(self):
        self.start("a_z", "a_xp", "a_xm")
        if self.halves:
            self.start("b_xp", "b_xm")

    def middle(self):
        self.wait("a_z")
        if self.halves:
            self.start("b_z0")
        self.start("az_xp", "az_xm")
        self.wait("a_xp")
        self.start("a_fp")
        self.wait("a_xm")
        self.start("a_fm")
        if self.halves:
            self.wait("b_xp")
            self.start("b_fp", "b_zm")
            self.wait("b_xm")
            self.start("b_fm", "b_zp")

    def late(self):
        self.wait("az_xp")
        self.start("az_fp")
        self.wait("az_xm")
        self.start("az_fm")
        if self.halves:
            self.wait("b_fp")
            self.start("b_z2a")
            self.wait("b_fm")
            self.start("b_z2b")

    def finish(self):
        self.wait("a_fp", "a_fm", "az_fp", "az_fm")
        if self.halves:
            self.wait("b_z0", "b_zm", "b_zp", "b_z2a", "b_z2b")

    def drain(self):
        for name in self.table:
            self.out(name).wait_send()


N_REDUCE = 17
N_REDUCE_FIRST = 9


class Reduce:
    def __init__(self, at, axis, terms, rows, corner, near, cross, cross_b, send_sems, recv_sems):
        self.at, self.axis, self.terms = at, axis, terms
        self.corner, self.near, self.cross, self.cross_b = corner, near, cross, cross_b
        self.send_sems, self.recv_sems = send_sems, recv_sems
        self.half = rows if cross_b is None else rows // 2
        self.quarter = self.half // 2
        self.started = []

    def go(self, k, dx, flip, row, rows, landing, device):
        source = self.terms.at[self.at.slot_of(self.axis, dx, flip), pl.ds(row, rows)]
        copy = remote(
            source, landing, self.send_sems.at[k], self.recv_sems.at[k],
            self.at.near(self.axis, *device),
        )
        copy.start()
        self.started.append(copy)

    def wait(self, k, landing):
        remote(
            landing, landing, self.send_sems.at[k], self.recv_sems.at[k],
            self.at.near(self.axis, 0, 1),
        ).wait_recv()

    def add(self, dx, flip, row, rows, *landings):
        slot = self.at.slot_of(self.axis, dx, flip)

        @pl.loop(0, rows // 32)
        def _(step):
            low = pl.multiple_of(step * 32, 32)
            here = pl.ds(pl.multiple_of(row + low, 32), 32)
            total = self.terms[slot, here, :].astype(F32)
            for landing in landings:
                total = total + landing[pl.ds(low, 32), :].astype(F32)
            self.terms[slot, here, :] = total.astype(BF16)

    def where(self, n):
        return (n, 0) if n < 2 else (0, self.half)

    def x_begin(self, n):
        flip, row = self.where(n)
        quarter = self.quarter
        self.go(4 * n, 2, flip, row, quarter, self.corner.at[n, 0], (1, 0))
        self.go(4 * n + 1, 2, flip, row + quarter, quarter, self.corner.at[n, 1], (-1, 0))

    def x_pass(self, n):
        flip, row = self.where(n)
        quarter = self.quarter
        self.wait(4 * n, self.corner.at[n, 0])
        self.add(1, flip, row, quarter, self.corner.at[n, 0])
        self.go(4 * n + 2, 1, flip, row, self.half, self.near.at[n, 0], (1, 0))
        self.wait(4 * n + 1, self.corner.at[n, 1])
        self.add(-1, flip, row + quarter, quarter, self.corner.at[n, 1])
        self.go(4 * n + 3, -1, flip, row, self.half, self.near.at[n, 1], (-1, 0))

    def x_end(self, n):
        flip, row = self.where(n)
        self.wait(4 * n + 2, self.near.at[n, 0])
        self.wait(4 * n + 3, self.near.at[n, 1])
        self.add(0, flip, row, self.half, self.near.at[n, 0], self.near.at[n, 1])

    @property
    def z_sem(self):
        return 8 if self.cross_b is None else 12

    def z_first(self):
        self.go(self.z_sem, 0, 1, 0, self.half, self.cross, (0, 1))

    def z_first_add(self):
        self.wait(self.z_sem, self.cross)
        self.add(0, 0, 0, self.half, self.cross)

    def z_second(self, dx):
        self.go(13 + dx, dx, 1, self.half, self.half, self.cross_b.at[dx], (0, 1))

    def z_second_add(self, dx):
        self.wait(13 + dx, self.cross_b.at[dx])
        self.add(dx, 0, self.half, self.half, self.cross_b.at[dx])

    def begin(self):
        self.z_second(2)
        self.x_begin(1)
        self.x_begin(0)
        for dx in (1, 3, 0):
            self.z_second(dx)

    def middle(self):
        self.x_pass(1)
        self.z_second_add(2)
        self.x_begin(2)
        self.x_pass(0)
        self.z_second_add(1)
        self.z_second_add(3)
        self.x_pass(2)

    def late(self):
        self.x_end(1)
        self.z_first()
        self.x_end(0)
        self.z_second_add(0)

    def finish(self):
        self.x_end(2)
        self.z_first_add()

    def drain(self):
        for copy in self.started:
            copy.wait_send()


def nt(left, right):
    return lax.dot_general(
        left, right, (((1,), (1,)), ((), ())), preferred_element_type=F32
    )


def tn(left, right):
    return lax.dot_general(
        left, right, (((0,), (0,)), ((), ())), preferred_element_type=F32
    )


def turned(v, cosine, sine):
    half = HD // 2
    rolled = jnp.concatenate([v[:, half:], v[:, :half]], axis=1)
    return v * cosine + rolled * sine


def squares_of(read, rows, width):
    def step(k, total):
        v = read(pl.ds(pl.multiple_of(k * 32, 32), 32)).astype(F32)
        v = jnp.sum((v * v).reshape(4, 8, width), axis=0)
        for first in range(0, width, 128):
            total = total + v[:, first:first + 128]
        return total

    return lax.fori_loop(0, rows // 32, step, jnp.zeros((8, 128), F32))


def aligned(start, size):
    return pl.ds(pl.multiple_of(start, size), size)


def step_kernel(
    shallow, gain, wq, wkv, wo, teacher, cosine, sine, seg_row,
    gq_out, gkv_out, go_out, scale_out,
    wbuf, obuf, nbuf, pbuf, tbuf, target, acc, sum_mine, sum_theirs, qbuf, kvbuf, probs,
    abuf, sbuf, ogbuf, lanes, square, stat_send, stat_recv,
    part_send, part_recv, g_terms, g_corner, g_near, g_cross,
    kv_part, kv_recv, o_terms, o_corner, o_near, o_cross, o_cross_b,
    qgbuf, go_recv, stat_one, stat_two, from_column, from_plane,
    w_send, w_recv, v_send, v_recv, o_send, o_recv, n_send, n_recv, x_send, x_recv, m_send, m_recv,
    t_send, t_recv, k_send, k_recv, swap_send, swap_recv,
    a_send, a_recv, f_send, f_recv, s_send, s_recv, p_send, p_recv, r_send, r_recv,
    d_send, d_recv, e_send, e_recv, q_send, q_recv, u_send, u_recv, h_send, h_recv,
    c_send, c_recv, l_send, l_recv, local_sems,
):
    at = Place()
    mine = aligned(at.c * ROWS, ROWS)
    theirs = aligned(at.o * ROWS, ROWS)
    heads = BLK // HD
    greet(at)
    peer = at.column(0, 1)
    is_key = (at.pipe % 2 == 0).astype(F32)

    def slots(buf):
        return lambda slot, row, rows: buf.at[slot, pl.ds(row, rows)]

    def slots_mine(buf):
        return lambda slot, row, rows: buf.at[slot, aligned(at.c * ROWS + row, rows)]

    def columns(buf, first, width):
        return lambda slot, row, rows: buf.at[slot, pl.ds(row, rows), pl.ds(first, width)]

    wg = Gather(at, "dp", columns(wbuf, 0, 384), BLK, w_send, w_recv, True)
    vg = Gather(at, "dp", columns(wbuf, 384, 256), BLK, v_send, v_recv, True)
    og = Gather(at, "dp", slots(obuf), BLK, o_send, o_recv, True)
    ng = Gather(
        at, "pipe", lambda slot, row, rows: tbuf.at[pl.ds(row, rows), aligned(slot * 32, 32)],
        16, m_send, m_recv, False,
    )
    ag = Gather(at, "pipe", slots_mine(abuf), ROWS, a_send, a_recv, False)

    def columns_mine(buf, first, width):
        return lambda slot, row, rows: buf.at[
            slot, aligned(at.c * ROWS + row, rows), pl.ds(first, width)
        ]

    qg = Gather(at, "dp", columns_mine(qgbuf, 0, BLK), ROWS, q_send, q_recv, True)
    kg = Gather(at, "dp", columns_mine(qgbuf, BLK, HD), ROWS, u_send, u_recv, True)

    wbuf[at.slot, :, pl.ds(0, BLK)] = wq[...]
    wbuf[at.slot, :, pl.ds(BLK, HD)] = wkv[...]
    wg.begin()
    vg.begin()

    swap = remote(wo, obuf.at[at.pipe], swap_send.at[0], swap_recv.at[0], at.swap())
    keep = pltpu.make_async_copy(wo, obuf.at[at.pipe], local_sems.at[0])

    def target_copy(k):
        dj, other = COLUMN[k]
        block = (at.pipe + dj) % NP * 2 + (at.o if other else at.c)
        return remote(
            teacher.at[:, aligned(block * BLK, BLK)],
            target.at[at.c, (at.pipe + 1) % NP],
            t_send.at[k], t_recv.at[k], at.column(dj, other),
        )

    def target_arrival(k):
        dj, other = COLUMN[k]
        region = target.at[at.o if other else at.c, (at.pipe - dj + NP + 1) % NP]
        return remote(region, region, t_send.at[k], t_recv.at[k], peer)

    own_block = aligned((at.pipe * 2 + at.c) * BLK, BLK)
    peer_block = aligned((at.pipe * 2 + at.o) * BLK, BLK)
    own_target = pltpu.make_async_copy(
        teacher.at[:, own_block], target.at[at.c, (at.pipe + 1) % NP], local_sems.at[1]
    )
    own_target.start()
    own_rows = pltpu.make_async_copy(shallow.at[:, own_block], sbuf.at[mine], local_sems.at[2])
    own_rows.start()
    peer_rows = remote(shallow.at[:, peer_block], sbuf.at[mine], h_send.at[8], h_recv.at[8], peer)
    peer_rows.start()

    @pl.loop(0, ROWS // 32)
    def _(step):
        rows = aligned(step * 32, 32)

        def squares(k, total):
            part = shallow[rows, aligned(k * 1024, 1024)].astype(F32)
            return total + jnp.sum(part * part, axis=1, keepdims=True)

        total = lax.fori_loop(0, 8, squares, jnp.zeros((32, 1), F32))
        scale = lax.rsqrt(total / D + norm_eps)

        @pl.loop(0, NP)
        def _(k):
            here = aligned((k * 2 + at.c) * BLK, BLK)
            there = aligned((k * 2 + at.o) * BLK, BLK)
            nrows = aligned(at.c * ROWS + step * 32, 32)
            nbuf[k, nrows, :] = (shallow[rows, here].astype(F32) * scale * gain[:, here]).astype(BF16)
            pbuf[k, rows, :] = (shallow[rows, there].astype(F32) * scale * gain[:, there]).astype(BF16)

    normed_copy = remote(pbuf, nbuf.at[:, mine], n_send.at[0], n_recv.at[0], peer)
    normed_copy.start()

    group_rows = tbuf.at[at.dp, aligned(at.pipe * 32, 32)]

    def block_copy(k):
        dx, flip, other = GROUP[k]
        slot = at.slot_of("dp", dx, flip)
        if other:
            source = pbuf.at[slot, aligned(at.pipe * 32, 32)]
        else:
            source = nbuf.at[slot, aligned(at.c * ROWS + at.pipe * 32, 32)]
        return remote(source, group_rows, x_send.at[k], x_recv.at[k], at.cross(dx, flip, other))

    def block_arrival(k):
        dx, flip, other = GROUP[k]
        source = at.slot_of("dp", -dx, flip) * 2 + (at.o if other else at.c)
        region = tbuf.at[source, aligned(at.pipe * 32, 32)]
        return remote(region, region, x_send.at[k], x_recv.at[k], peer)

    wg.middle()
    vg.middle()

    landed = nbuf.at[:, theirs]
    remote(landed, landed, n_send.at[0], n_recv.at[0], peer).wait_recv()
    wg.late()
    vg.late()

    @pl.when(at.swaps)
    def _():
        swap.start()

    @pl.when(jnp.logical_not(at.swaps))
    def _():
        keep.start()

    def project(dx, flip):
        slot = at.slot_of("dp", dx, flip)
        acc[...] += jnp.dot(nbuf[slot], wbuf[slot], preferred_element_type=F32)

    acc[...] = jnp.zeros_like(acc)
    project(0, 0)
    project(1, 0)
    project(-1, 0)
    wg.wait("b_z0")
    vg.wait("b_z0")
    project(0, 1)
    wg.wait("a_fp", "a_fm")
    vg.wait("a_fp", "a_fm")
    project(2, 0)
    wg.wait("b_zm", "b_zp")
    vg.wait("b_zm", "b_zp")
    project(1, 1)
    project(-1, 1)
    wg.wait("az_fp", "az_fm", "b_z2a", "b_z2b")
    vg.wait("az_fp", "az_fm", "b_z2a", "b_z2b")
    project(2, 1)

    sum_mine[...] = acc[theirs, :]
    sums = remote(sum_mine, sum_theirs, n_send.at[1], n_recv.at[1], peer)
    sums.start()
    sums.wait_recv()

    cos_table, sin_table = cosine[...], sine[...]
    for head in range(heads):
        cols = pl.ds(head * HD, HD)
        v = acc[mine, cols] + sum_theirs[:, cols]
        qbuf[head] = turned(v, cos_table, sin_table).astype(BF16)
    cols = pl.ds(BLK, HD)
    v = acc[mine, cols] + sum_theirs[:, cols]
    kvbuf[at.pipe] = (turned(v, cos_table, sin_table) * is_key + v * (1.0 - is_key)).astype(BF16)

    def kv_copy(dj):
        region = kvbuf.at[at.pipe]
        return remote(region, region, k_send.at[dj], k_recv.at[dj], at.column(dj, 0))

    def kv_arrival(dj):
        region = kvbuf.at[(at.pipe - dj + NP) % NP]
        return remote(region, region, k_send.at[dj], k_recv.at[dj], peer)

    for dj in range(1, NP):
        kv_copy(dj).start()
    for k in range(len(COLUMN)):
        target_copy(k).start()

    @pl.when(at.swaps)
    def _():
        remote(wo, obuf.at[at.slot], swap_send.at[0], swap_recv.at[0], at.swap()).wait_recv()
        swap.wait_send()

    @pl.when(jnp.logical_not(at.swaps))
    def _():
        keep.wait()

    og.begin()
    for dj in range(1, NP):
        kv_arrival(dj).wait_recv()

    score_scale = 1.0 / math.sqrt(HD)
    row_ids = lax.broadcasted_iota(jnp.int32, (ROWS, ROWS), 0)
    col_ids = lax.broadcasted_iota(jnp.int32, (ROWS, ROWS), 1)
    ids = jnp.broadcast_to(seg_row[...].astype(F32), (ROWS, ROWS))
    allowed = (ids.T == ids) & (col_ids <= row_ids)
    for head in range(heads):
        scores = nt(qbuf[head], kvbuf[2 * head]) * score_scale
        scores = jnp.where(allowed, scores, mask_fill)
        weights = jnp.exp(scores - jnp.max(scores, axis=1, keepdims=True))
        soft = weights * (1.0 / jnp.sum(weights, axis=1, keepdims=True))
        probs[head] = soft
        attended = jnp.dot(soft.astype(BF16), kvbuf[2 * head + 1], preferred_element_type=F32)
        abuf[at.pipe, mine, pl.ds(head * HD, HD)] = attended.astype(BF16)

    def forward(dx, flip):
        k = dx % NX * 2 + flip
        region = abuf.at[at.slot_of("pipe", dx, flip), mine]
        return remote(region, region, f_send.at[k], f_recv.at[k], peer)

    def multiply(dx, flip):
        k = dx % NX * 2 + flip
        source = at.slot_of("pipe", dx, flip)
        region = abuf.at[source, theirs]
        remote(region, region, f_send.at[k], f_recv.at[k], peer).wait_recv()
        acc[:, pl.ds(0, BLK)] += jnp.dot(abuf[source], obuf[source], preferred_element_type=F32)

    ag.begin()
    forward(0, 0).start()
    og.middle()
    ag.middle()
    forward(0, 1).start()
    forward(1, 0).start()
    forward(-1, 0).start()
    ag.late()
    og.late()
    for k in range(len(GROUP)):
        block_copy(k).start()
    own_block_copy = pltpu.make_async_copy(
        nbuf.at[at.slot, aligned(at.c * ROWS + at.pipe * 32, 32)], group_rows, local_sems.at[3]
    )
    own_block_copy.start()
    forward(1, 1).start()
    forward(-1, 1).start()
    og.finish()
    acc[...] = jnp.zeros_like(acc)
    for d in ((0, 0), (0, 1), (1, 0), (-1, 0), (1, 1), (-1, 1)):
        multiply(*d)
    ag.wait("a_fp", "a_fm")
    forward(2, 0).start()
    ag.wait("az_fp", "az_fm")
    forward(2, 1).start()
    multiply(2, 0)
    multiply(2, 1)

    own_rows.wait()
    landed = sbuf.at[theirs]
    remote(landed, landed, h_send.at[8], h_recv.at[8], peer).wait_recv()
    own_target.wait()
    for k in range(len(COLUMN)):
        target_arrival(k).wait_recv()

    def wanted_rows(step):
        return target[step // 8, step % 8].astype(F32)

    lane = lax.broadcasted_iota(jnp.int32, (32, 128), 1)

    @pl.loop(0, 2 * NP)
    def _(step):
        rows = aligned(step * 32, 32)
        output = acc[rows, pl.ds(0, BLK)] + sbuf[rows, :].astype(F32)
        acc[rows, pl.ds(0, BLK)] = output
        wanted = wanted_rows(step)
        oo = jnp.sum(output * output, axis=1, keepdims=True)
        tt = jnp.sum(wanted * wanted, axis=1, keepdims=True)
        ot = jnp.sum(output * wanted, axis=1, keepdims=True)
        lanes[rows, :] = jnp.where(
            lane == 0, oo, jnp.where(lane == 1, tt, jnp.where(lane == 2, ot, 0.0))
        )

    square[...] = lanes[...].T
    stat_send[...] = square[pl.ds(0, 8), :]

    def stat(k):
        return remote(
            stat_send, stat_recv.at[k], s_send.at[k], s_recv.at[k], at.column(*COLUMN[k])
        )

    for k in range(len(COLUMN)):
        stat(k).start()
    own_block_copy.wait()
    for k in range(len(GROUP)):
        block_arrival(k).wait_recv()
    ng.begin()
    total = stat_send[...]
    for k in range(len(COLUMN)):
        stat(k).wait_recv()
        total = total + stat_recv[k]
    square[pl.ds(0, 8), :] = total
    lanes[...] = square[...].T

    def gradient(step, lost):
        rows = aligned(step * 32, 32)
        output = acc[rows, pl.ds(0, BLK)]
        wanted = wanted_rows(step)
        norm_out = jnp.sqrt(lanes[rows, 0:1] + cosine_eps)
        norm_tar = jnp.sqrt(lanes[rows, 1:2] + cosine_eps)
        both = norm_out * norm_tar
        cosine_sim = lanes[rows, 2:3] / both
        grad = wanted * (1.0 / both) - output * (cosine_sim / (norm_out * norm_out))
        ogbuf[rows, :] = (grad * (-1.0 / 4096)).astype(BF16)
        return lost + (1.0 - cosine_sim)

    lost = lax.fori_loop(0, 2 * NP, gradient, jnp.zeros((32, 1), F32))
    lost = jnp.broadcast_to(jnp.sum(lost, axis=0, keepdims=True), (8, 128))

    grads = Reduce(at, "pipe", g_terms, ROWS, g_corner, g_near, g_cross, None, r_send, r_recv)
    outs = Reduce(at, "dp", o_terms, BLK, o_corner, o_near, o_cross, o_cross_b, e_send, e_recv)
    order = [(2, 1), (2, 0), (1, 1), (-1, 1), (1, 0), (-1, 0), (0, 1), (0, 0)]

    def part(k):
        return remote(part_send.at[k], part_recv.at[k], p_send.at[k], p_recv.at[k], peer)

    def produce(k):
        slot = at.slot_of("pipe", *order[k])
        weights = obuf[slot]
        part_send[k] = nt(ogbuf[theirs, :], weights).astype(BF16)
        part(k).start()
        g_terms[slot] = nt(ogbuf[mine, :], weights).astype(BF16)

    def settle(k):
        part(k).wait_recv()
        grads.add(*order[k], 0, ROWS, part_recv.at[k])

    def out_term(dx, flip):
        slot = at.slot_of("dp", dx, flip)
        o_terms[slot] = tn(abuf[slot], ogbuf[...]).astype(BF16)

    out_term(2, 1)
    outs.z_second(2)
    outs.x_begin(1)
    produce(0)
    produce(1)
    settle(0)
    grads.x_begin(1)
    out_term(2, 0)
    outs.x_begin(0)
    produce(2)
    settle(1)
    grads.x_begin(0)
    out_term(1, 1)
    outs.z_second(1)
    produce(3)
    settle(2)
    produce(4)
    settle(3)
    out_term(3, 1)
    outs.z_second(3)
    grads.x_pass(1)
    produce(5)
    settle(4)
    produce(6)
    settle(5)
    grads.x_pass(0)
    produce(7)
    settle(6)
    settle(7)
    outs.x_pass(1)
    grads.x_end(1)
    grads.z_first()
    out_term(1, 0)
    out_term(-1, 0)
    out_term(0, 1)
    grads.x_end(0)
    grads.z_first_add()
    outs.z_second(0)
    outs.x_pass(0)
    ng.middle()

    def kv_grad_copy(dj):
        return remote(
            kv_part.at[(at.pipe + dj) % NP], kv_recv.at[dj], d_send.at[dj], d_recv.at[dj],
            at.column(dj, 0),
        )

    for head in range(heads):
        cols = pl.ds(head * HD, HD)
        soft = probs[head]
        att_grad = g_terms[at.pipe, :, cols]
        inner = nt(att_grad, kvbuf[2 * head + 1])
        centred = inner - jnp.sum(soft * inner, axis=1, keepdims=True)
        score_grad = (soft * centred * score_scale).astype(BF16)
        kv_part[2 * head] = tn(score_grad, qbuf[head]).astype(BF16)
        kv_part[2 * head + 1] = tn(soft.astype(BF16), att_grad).astype(BF16)
        grad = jnp.dot(score_grad, kvbuf[2 * head], preferred_element_type=F32)
        qgbuf[at.slot, mine, cols] = turned(grad, cos_table, -sin_table).astype(BF16)

    for dj in range(1, NP):
        kv_grad_copy(dj).start()
    qg.begin()
    outs.z_second_add(2)
    outs.x_begin(2)
    out_term(0, 0)
    outs.z_second_add(1)
    outs.z_second_add(3)
    total = kv_part[at.pipe].astype(F32)
    for dj in range(1, NP):
        kv_grad_copy(dj).wait_recv()
        total = total + kv_recv[dj].astype(F32)
    total = turned(total, cos_table, -sin_table) * is_key + total * (1.0 - is_key)
    qgbuf[at.slot, mine, pl.ds(BLK, HD)] = total.astype(BF16)

    def hand(dx, flip):
        k = dx % NX * 2 + flip
        region = qgbuf.at[at.slot_of("dp", dx, flip), mine]
        return remote(region, region, h_send.at[k], h_recv.at[k], peer)

    def contract(dx, flip):
        k = dx % NX * 2 + flip
        slot = at.slot_of("dp", dx, flip)
        region = qgbuf.at[slot, theirs]
        remote(region, region, h_send.at[k], h_recv.at[k], peer).wait_recv()
        acc[...] += jnp.dot(
            wbuf[slot, :, pl.ds(0, BLK)], qgbuf[slot], preferred_element_type=F32
        )

    kg.begin()
    hand(0, 0).start()
    ng.late()
    outs.x_end(1)
    outs.z_first()
    outs.x_pass(2)
    ng.finish()
    wg.drain()
    vg.drain()

    @pl.loop(0, NP)
    def _(k):
        for core in range(2):
            wbuf[k, :, pl.ds(core * ROWS, ROWS)] = tbuf[k * 2 + core].T
    qg.middle()
    kg.middle()
    hand(1, 0).start()
    hand(-1, 0).start()
    outs.x_end(0)
    outs.z_second_add(0)
    qg.late()
    kg.late()
    outs.finish()

    own = at.slot
    give = remote(o_terms.at[own], go_recv, swap_send.at[1], swap_recv.at[1], at.swap())
    hold = pltpu.make_async_copy(o_terms.at[own], go_recv, local_sems.at[4])

    @pl.when(at.swaps)
    def _():
        give.start()

    @pl.when(jnp.logical_not(at.swaps))
    def _():
        hold.start()

    acc[...] = jnp.zeros_like(acc)
    contract(0, 0)
    qg.wait("b_z0")
    kg.wait("b_z0")
    hand(0, 1).start()
    contract(1, 0)
    contract(-1, 0)
    qg.wait("a_fp", "a_fm")
    kg.wait("a_fp", "a_fm")
    hand(2, 0).start()
    qg.wait("b_zm", "b_zp")
    kg.wait("b_zm", "b_zp")
    hand(1, 1).start()
    hand(-1, 1).start()
    contract(0, 1)
    contract(2, 0)
    tile = squares_of(lambda rows: o_terms[own, rows, :], BLK, BLK)
    qg.wait("az_fp", "az_fm", "b_z2a", "b_z2b")
    kg.wait("az_fp", "az_fm", "b_z2a", "b_z2b")
    hand(2, 1).start()
    contract(1, 1)
    contract(-1, 1)
    contract(2, 1)
    stat_one[pl.ds(0, 8), :] = tile + squares_of(lambda rows: acc[rows, :], BLK, WQ)
    stat_one[pl.ds(8, 8), :] = lost

    def column_copy(k):
        return remote(
            stat_one, from_column.at[k], c_send.at[k], c_recv.at[k], at.column(*COLUMN[k])
        )

    def plane_copy(k):
        return remote(
            stat_two, from_plane.at[k], l_send.at[k], l_recv.at[k], at.near("dp", *PLANES[k])
        )

    for k in range(len(COLUMN)):
        column_copy(k).start()
    gq_out[...] = acc[:, pl.ds(0, BLK)].astype(BF16)
    gkv_out[...] = acc[:, pl.ds(BLK, HD)].astype(BF16)
    total = stat_one[...]
    for k in range(len(COLUMN)):
        column_copy(k).wait_recv()
        total = total + from_column[k]
    stat_two[...] = total
    for k in range(len(PLANES)):
        plane_copy(k).start()
    for k in range(len(PLANES)):
        plane_copy(k).wait_recv()
        total = total + from_plane[k]
    square_sum = jnp.sum(
        jnp.sum(total[:8], axis=0, keepdims=True), axis=1, keepdims=True
    )
    inverse = 1.0 / jnp.sqrt(square_sum * (1.0 / PARAMS) + mean_eps)
    scale_out[pl.ds(0, 8), :] = jnp.broadcast_to(inverse, (8, 128))
    scale_out[pl.ds(8, 8), :] = total[8:] * (1.0 / (2 * NP * 4096))

    @pl.when(at.swaps)
    def _():
        give.wait_recv()
        give.wait_send()

    @pl.when(jnp.logical_not(at.swaps))
    def _():
        hold.wait()

    go_out[...] = go_recv[...]
    for group in (og, ng, ag, qg, kg, grads, outs):
        group.drain()
    normed_copy.wait_send()
    peer_rows.wait_send()
    sums.wait_send()
    for k in range(len(GROUP)):
        block_copy(k).wait_send()
    for k in range(len(COLUMN)):
        target_copy(k).wait_send()
        stat(k).wait_send()
        column_copy(k).wait_send()
    for k in range(len(PLANES)):
        plane_copy(k).wait_send()
    for dj in range(1, NP):
        kv_copy(dj).wait_send()
        kv_grad_copy(dj).wait_send()
    for dx in range(NX):
        for flip in range(2):
            forward(dx, flip).wait_send()
            hand(dx, flip).wait_send()
            part(dx * 2 + flip).wait_send()


def run_step(shallow, gain, wq, wkv, wo, teacher, cosine, sine, seg_row):
    vmem = pl.BlockSpec(memory_space=pltpu.VMEM)
    anyspace = pl.BlockSpec(memory_space=pl.ANY)

    def low(*shape):
        return pltpu.VMEM(shape, BF16)

    def wide(*shape):
        return pltpu.VMEM(shape, F32)

    def sems(*counts):
        return [pltpu.SemaphoreType.DMA((count,)) for count in counts for _ in range(2)]

    def reduce_buffers(numbers, half, width):
        return [
            low(numbers, 2, half // 2, width), low(numbers, 2, half, width), low(half, width)
        ]

    return pl.pallas_call(
        step_kernel,
        out_shape=(
            jax.ShapeDtypeStruct((BLK, BLK), BF16),
            jax.ShapeDtypeStruct((BLK, HD), BF16),
            jax.ShapeDtypeStruct((BLK, BLK), BF16),
            jax.ShapeDtypeStruct((16, 128), F32),
        ),
        in_specs=[vmem, vmem, vmem, vmem, anyspace, anyspace, vmem, vmem, vmem],
        out_specs=(vmem, vmem, vmem, vmem),
        scratch_shapes=[
            low(NP, BLK, WQ), low(NP, BLK, BLK), low(NP, 2 * ROWS, BLK), low(NP, ROWS, BLK),
            low(16, ROWS, BLK), low(2, NP, ROWS // NP, BLK),
            wide(2 * ROWS, WQ), wide(ROWS, WQ), wide(ROWS, WQ),
            low(BLK // HD, ROWS, HD), low(NP, ROWS, HD), wide(BLK // HD, ROWS, ROWS),
            low(NP, 2 * ROWS, BLK), low(2 * ROWS, BLK), low(2 * ROWS, BLK),
            wide(2 * ROWS, 128), wide(128, 2 * ROWS), wide(8, 2 * ROWS), wide(15, 8, 2 * ROWS),
            low(NP, ROWS, BLK), low(NP, ROWS, BLK), low(NP, ROWS, BLK),
            *reduce_buffers(2, ROWS, BLK),
            low(NP, ROWS, HD), low(NP, ROWS, HD),
            low(NP, BLK, BLK), *reduce_buffers(3, BLK // 2, BLK), low(NX, BLK // 2, BLK),
            low(NP, 2 * ROWS, WQ), low(BLK, BLK),
            wide(16, 128), wide(16, 128), wide(15, 16, 128), wide(7, 16, 128),
            *sems(
                N_GATHER, N_GATHER, N_GATHER, 2, 15, N_FIRST, 15, NP, 2, N_FIRST, NP, 15, NP,
                N_REDUCE_FIRST, NP, N_REDUCE, N_GATHER, N_GATHER, NP + 1, 15, 7,
            ),
            pltpu.SemaphoreType.DMA((5,)),
        ],
        compiler_params=pltpu.CompilerParams(
            collective_id=0, has_side_effects=True, vmem_limit_bytes=VLIM
        ),
        name="adapter_step",
    )(shallow, gain, wq, wkv, wo, teacher, cosine, sine, seg_row)


def rotary_tables(positions):
    half_width = HD // 2
    exponent = jnp.arange(half_width).astype(F32) * (2.0 / HD)
    inverse = jnp.power(jnp.float32(theta_base), -exponent)
    angle_table = positions.astype(F32)[:, None] * inverse[None, :]
    cosine, sine = jnp.cos(angle_table), jnp.sin(angle_table)
    return jnp.concatenate([cosine, cosine], axis=1), jnp.concatenate([-sine, sine], axis=1)


def per_device(shallow, teacher, positions, segments, in_gain, w_query, w_keyval, w_output):
    cosine, sine = rotary_tables(positions)
    query, keyval, output, scale = run_step(
        shallow, in_gain[None], w_query, w_keyval, w_output, teacher, cosine, sine,
        segments[None, :],
    )
    inverse = scale[0, 0]
    return (
        scale[8, 0],
        query.astype(F32) * inverse,
        keyval.astype(F32) * inverse,
        output.astype(F32) * inverse,
    )


def solution(mesh):
    placed = (
        P("dp", None),
        P(("dp", "pipe"), None),
        P("dp"),
        P("dp"),
        P(),
        P("dp", "pipe"),
        P("dp", "pipe"),
        P("pipe", "dp"),
    )
    return jax.shard_map(
        per_device,
        mesh=mesh,
        in_specs=placed,
        out_specs=(P(), P("dp", "pipe"), P("dp", "pipe"), P("pipe", "dp")),
        check_vma=False,
    )
```
